32 devices in a mesh: group: 4 (over y, core), wide: 8 (over z, x).
Axes of the slice: x: 2, y: 2, z: 4, core: 2. Of those that a mesh axis runs over, the one named last changes fastest.
Arguments:
- tokens: bfloat16 [32768, 1024], P(('group', 'wide')), may hold values from -6 to 6
- cotangent: bfloat16 [32768, 1024], P(('group', 'wide')), may hold values from -6 to 6
- noise_index: int32 [256], P(('group', 'wide')), may hold values from 0 to 255
- time_embed: bfloat16 [256, 1024], replicated, may hold values from -6 to 6
- ln1_gain: bfloat16 [1024], P('wide'), may hold values from 0.5 to 1.5
- ln1_shift: bfloat16 [1024], P('wide'), may hold values from -1.75 to 1.75
- w_qkv: bfloat16 [1024, 3072], P('wide'), may hold values from -0.1875 to 0.1875
- w_out: bfloat16 [1024, 1024], P('wide'), may hold values from -2 to 2
- ln2_gain: bfloat16 [1024], P('wide'), may hold values from 0.5 to 1.5
- ln2_shift: bfloat16 [1024], P('wide'), may hold values from -1.75 to 1.75
- w_time: bfloat16 [1024, 1024], P('wide'), may hold values from -0.1875 to 0.1875
- w_up: bfloat16 [1024, 4096], P('wide'), may hold values from -0.1875 to 0.1875
- up_bias: bfloat16 [4096], P('wide'), may hold values from -1.75 to 1.75
- w_down: bfloat16 [4096, 1024], P('wide'), may hold values from -0.09375 to 0.09375
- down_bias: bfloat16 [1024], P('wide'), may hold values from -1.75 to 1.75
Outputs:
- output: bfloat16 [32768, 1024], P(('group', 'wide'))
- grad_tokens: float32 [32768, 1024], P(('group', 'wide'))
- grad_ln1_gain: float32 [1024], P('wide')
- grad_ln1_shift: float32 [1024], P('wide')
- grad_w_qkv: float32 [1024, 3072], P('wide')
- grad_w_out: float32 [1024, 1024], P('wide')
- grad_ln2_gain: float32 [1024], P('wide')
- grad_ln2_shift: float32 [1024], P('wide')
- grad_w_time: float32 [1024, 1024], P('wide')
- grad_w_up: float32 [1024, 4096], P('wide')
- grad_up_bias: float32 [4096], P('wide')
- grad_w_down: float32 [4096, 1024], P('wide')
- grad_down_bias: float32 [1024], P('wide')
The draws below stay inside these ranges and needn't reach their ends.
Inputs may be any that keep to these rules, and one draw needn't show every extreme that they name: `noise_index`: the row of time_embed that each sequence uses.
All inputs are finite; a program needn't handle non-finite values.
Results may differ from the reference program's by a relative error of at most 0.015.
Values may be sent and summed in bfloat16 or wider, within the bound.
No kernel may reach another device: no remote copies, remote signals or barrier semaphores. Data moves between devices by JAX's collectives and lax.ppermute only.
A program may use at most 256 MiB of HBM per device.

```python
import math
import jax
import jax.numpy as jnp
from jax import lax

D = 1024
FF = 4096
HEAD_DIM = 64
SEQ_LEN = 128
NOISE_LEVELS = 256
BATCH = 256
TOKENS = 32768


def place_ends(values, stream_key, smallest, top_value):
    shape = values.shape
    spot = [jax.random.randint(jax.random.fold_in(stream_key, axis), (), 0, shape[axis]) for axis in range(len(shape))]
    values = values.at[tuple(spot)].set(smallest)
    longest = shape.index(max(shape))
    spot[longest] = (spot[longest] + 1) % shape[longest]
    return values.at[tuple(spot)].set(top_value)


def raised(entries, rng, source, target, shards_of, factor):
    owner, partner = [(jnp.arange(entries.shape[position]) // (entries.shape[position] // shards_of)).reshape([-1 if axis == position else 1 for axis in range(entries.ndim)]) for position in (source, target)]
    chosen = jax.random.permutation(rng, shards_of)[partner]
    strong = (owner == chosen) | (owner == (partner + shards_of // 2) % shards_of)
    return jnp.where(strong, factor * entries, entries)


def block_levels(key, shape, split, least, high):
    level = 1.0
    for axis_at, blocks in split:
        heights = jax.random.uniform(jax.random.fold_in(jax.random.fold_in(key, 6), axis_at), (blocks,), jnp.float32, least / len(split), high / len(split))
        level = level * jnp.repeat(jnp.exp(heights), shape[axis_at] // blocks).reshape((-1,) + (1,) * (len(shape) - 1 - axis_at))
    return level


def normal_values(own_key, shape, spread, bound, split=(), kind=jnp.bfloat16):
    values = spread * jax.random.normal(own_key, shape, jnp.float32)
    if split:
        values = values * block_levels(own_key, shape, split, -0.22, 0.18)
    return jnp.clip(values, -bound, bound).astype(kind)


def gaussian_with(key, dims, width, limit, pieces, heavy, kind=jnp.bfloat16):
    entries = width * jax.random.normal(key, dims, jnp.float32)
    if pieces:
        entries = entries * block_levels(key, dims, pieces, -0.22, 0.18)
    return jnp.clip(raised(entries, jax.random.fold_in(key, 3), *heavy), -limit, limit).astype(kind)


def setup_inputs(seed: int = 0) -> dict:
    key_of = jax.random.split(jax.random.key(seed), 16)
    return {
        "tokens": gaussian_with(key_of[0], (TOKENS, D), 1.0, 6.0, ((0, 32),), (0, 1, 32, 2.75)),
        "cotangent": gaussian_with(key_of[1], (TOKENS, D), 1.0, 6.0, ((0, 32),), (0, 1, 32, 2.75)),
        "noise_index": place_ends(jax.random.randint(key_of[2], (BATCH,), 0, NOISE_LEVELS), jax.random.fold_in(key_of[2], 1), 0, NOISE_LEVELS - 1).astype(jnp.int32),
        "time_embed": normal_values(key_of[3], (NOISE_LEVELS, D), 1.0, 6.0),
        "ln1_gain": jnp.clip(1.0 + 0.1 * jax.random.normal(key_of[4], (D,), jnp.float32), 0.5, 1.5).astype(jnp.bfloat16),
        "ln1_shift": normal_values(key_of[5], (D,), 0.3, 1.75, ((0, 8),)),
        "w_qkv": normal_values(key_of[6], (D, 3 * D), D ** -0.5, 0.1875, ((0, 8),)),
        "w_out": normal_values(key_of[7], (D, D), (D // SEQ_LEN) ** -0.5, 2.0, ((0, 8),)),
        "ln2_gain": jnp.clip(1.0 + 0.1 * jax.random.normal(key_of[8], (D,), jnp.float32), 0.5, 1.5).astype(jnp.bfloat16),
        "ln2_shift": normal_values(key_of[9], (D,), 0.3, 1.75, ((0, 8),)),
        "w_time": normal_values(key_of[10], (D, D), D ** -0.5, 0.1875, ((0, 8),)),
        "w_up": normal_values(key_of[11], (D, FF), D ** -0.5, 0.1875, ((0, 8),)),
        "up_bias": normal_values(key_of[12], (FF,), 0.3, 1.75, ((0, 8),)),
        "w_down": normal_values(key_of[13], (FF, D), FF ** -0.5, 0.09375, ((0, 8),)),
        "down_bias": normal_values(key_of[14], (D,), 0.3, 1.75, ((0, 8),)),
    }


@jax.custom_vjp
def low(v):
    return lax.optimization_barrier(v.astype(jnp.bfloat16)).astype(jnp.float32)

@jax.custom_vjp
def low_back(v):
    return v

def low_keep(v):
    return (low(v), None)

def low_pass(kept, grad):
    return (grad,)

def back_keep(v):
    return (v, None)

def back_low(kept, grad):
    return (low(grad),)
low.defvjp(low_keep, low_pass)
low_back.defvjp(back_keep, back_low)
EPSILON = 1e-05
HIGHEST = lax.Precision.HIGHEST

def layer_norm(values, gain_vec, shift_vec):
    average = lax.optimization_barrier(jnp.mean(values, axis=-1, keepdims=True))
    centered = values - average
    variance = lax.optimization_barrier(jnp.mean(centered * centered, axis=-1, keepdims=True))
    return centered * lax.rsqrt(variance + EPSILON) * gain_vec + shift_vec

def rotary_tables(length, head_size):
    half_dim = head_size // 2
    frequency = jnp.exp(jnp.arange(half_dim, dtype=jnp.float32) * (-2.0 * math.log(10000.0) / head_size))
    angles = jnp.arange(length, dtype=jnp.float32)[:, None] * frequency[None, :]
    angles = jnp.concatenate([angles, angles], axis=1)
    return (jnp.cos(angles), jnp.sin(angles))

def rotate_half(values):
    half_dim = values.shape[-1] // 2
    return jnp.concatenate([-values[..., half_dim:], values[..., :half_dim]], axis=-1)

def rotate(values, cosine, sine_table):
    return values * cosine + rotate_half(values) * sine_table

def block_forward(params, block):
    gain_one, shift_one, w_qkv, w_out, gain_two, shift_two, w_time, w_up, up_bias, w_down, down_bias, table = params
    inputs, indices = block
    seq_count = indices.shape[0]
    row_count, model_width = inputs.shape
    length = row_count // seq_count
    head_count = model_width // HEAD_DIM
    act_one = low(layer_norm(inputs, gain_one, shift_one))
    projected = low_back(jnp.dot(act_one, w_qkv, precision=HIGHEST))
    projected = projected.reshape(seq_count, length, 3, head_count, HEAD_DIM)
    cosine, sine_table = rotary_tables(length, HEAD_DIM)
    cosine = cosine[None, :, None, :]
    sine_table = sine_table[None, :, None, :]
    queries = low(rotate(projected[:, :, 0], cosine, sine_table))
    key_rows = low(rotate(projected[:, :, 1], cosine, sine_table))
    value_rows = low(projected[:, :, 2])
    scores = low_back(jnp.einsum('bqhd,bkhd->bhqk', queries, key_rows, precision=HIGHEST) * HEAD_DIM ** (-0.5))
    probs_low = low(jax.nn.softmax(scores, axis=-1))
    attended = jnp.einsum('bhqk,bkhd->bqhd', probs_low, value_rows, precision=HIGHEST)
    attended = low(low_back(attended.reshape(row_count, model_width)))
    middle = inputs + low_back(jnp.dot(attended, w_out, precision=HIGHEST))
    normed_two = layer_norm(middle, gain_two, shift_two)
    embedded = low(table[indices])
    channel_scale = 1.0 + low_back(jnp.dot(embedded, w_time, precision=HIGHEST))
    scaled = (normed_two.reshape(seq_count, length, model_width) * channel_scale[:, None, :]).reshape(row_count, model_width)
    act_two = low(scaled)
    pre_act = low_back(jnp.dot(act_two, w_up, precision=HIGHEST) + up_bias)
    hidden_low = low(jax.nn.gelu(pre_act, approximate=False))
    return middle + low_back(jnp.dot(hidden_low, w_down, precision=HIGHEST) + down_bias)

def reference(tokens, cotangent, noise_index, time_embed, ln1_gain, ln1_shift, w_qkv, w_out, ln2_gain, ln2_shift, w_time, w_up, up_bias, w_down, down_bias):
    params = tuple((array.astype(jnp.float32) for array in (ln1_gain, ln1_shift, w_qkv, w_out, ln2_gain, ln2_shift, w_time, w_up, up_bias, w_down, down_bias)))
    table = time_embed.astype(jnp.float32)
    group_seqs = math.gcd(BATCH, max(1, 4096 // SEQ_LEN))
    blocks = BATCH // group_seqs
    inputs = tokens.astype(jnp.float32).reshape(blocks, group_seqs * SEQ_LEN, D)
    indices = noise_index.reshape(blocks, group_seqs)

    def forward_all(inputs, params):
        stepper = jax.checkpoint(lambda block: block_forward(params + (table,), block))
        return lax.map(stepper, (inputs, indices))
    result, backward = jax.vjp(forward_all, inputs, params)
    grad_inputs, grad_params = backward(cotangent.astype(jnp.float32).reshape(blocks, group_seqs * SEQ_LEN, D))
    return (result.reshape(TOKENS, D).astype(jnp.bfloat16), grad_inputs.reshape(TOKENS, D), grad_params[0], grad_params[1], grad_params[2], grad_params[3], grad_params[4], grad_params[5], grad_params[6], grad_params[7], grad_params[8], grad_params[9], grad_params[10])
```

```python
import functools
import math

import jax
import jax.numpy as jnp
from jax import lax
from jax.experimental import pallas as pl
from jax.experimental.pallas import tpu as pltpu
from jax.sharding import PartitionSpec as P

HEAD_DIM = 64
EPSILON = 1e-05
BOTH = ("group", "wide")
F32 = jnp.float32
BF16 = jnp.bfloat16
BLOCKS = 32
VMEM_BYTES = 58 * 2**20


def add(a, b):
    return (a.astype(F32) + b.astype(F32)).astype(BF16)


def swapped(flag, a, b):
    return jnp.where(flag == 0, a, b), jnp.where(flag == 0, b, a)


def dot(a, b):
    return jnp.dot(a, b, preferred_element_type=F32)


def dot_nt(a, b):
    return lax.dot_general(a, b, (((1,), (1,)), ((), ())), preferred_element_type=F32)


class Plan:
    def __init__(self):
        def pairs(target):
            found = []
            for index in range(32):
                group, wide = divmod(index, 8)
                y, core, z, x = target(group // 2, group % 2, wide // 2, wide % 2)
                found.append((index, (y * 2 + core) * 8 + z * 2 + x))
            return found

        self.core_pairs = pairs(lambda y, c, z, x: (y, 1 - c, z, x))
        self.y_pairs = pairs(lambda y, c, z, x: (1 - y, c, z, x))
        self.x_pairs = pairs(lambda y, c, z, x: (y, c, z, 1 - x))
        self.first_pairs = pairs(lambda y, c, z, x: (y, c, z, 1 - x) if c == 0 else (1 - y, c, z, x))
        self.second_pairs = pairs(lambda y, c, z, x: (1 - y, c, z, x) if c == 0 else (y, c, z, 1 - x))
        self.z_pairs = [pairs(lambda y, c, z, x, step=step: (y, c, (z - step) % 4, x)) for step in range(4)]
        self.wide_pairs = [
            [(g * 8 + w, g * 8 + (w - step) % 8) for g in range(4) for w in range(8)] for step in range(8)
        ]

    def enter(self):
        self.group = lax.axis_index("group")
        self.wide = lax.axis_index("wide")
        y, core = self.group // 2, self.group % 2
        z, x = self.wide // 2, self.wide % 2
        self.core, self.y = core, y
        slot = jnp.arange(BLOCKS, dtype=jnp.int32)
        holder = core ^ (slot // 16)
        second, first, step = (slot // 8) % 2, (slot // 4) % 2, slot % 4
        across = jnp.where(holder == 0, first, second)
        along = jnp.where(holder == 0, second, first)
        places = (((z + step) % 4) * 2 + (x ^ across)) * 4 + (y ^ along) * 2 + holder
        block_z, block_x, block_y, block_core = slot // 8, (slot // 4) % 2, (slot // 2) % 2, slot % 2
        off_x, off_y = block_x ^ x, block_y ^ y
        first = jnp.where(block_core == 0, off_x, off_y)
        second = jnp.where(block_core == 0, off_y, off_x)
        slots = (((block_core ^ core) * 2 + second) * 2 + first) * 4 + (block_z - z) % 4
        return places.astype(jnp.int32), slots.astype(jnp.int32)

    def move(self, value, pairs):
        return lax.ppermute(value, BOTH, pairs)

    def gather(self, shard):
        rows = shard.shape[0] // 4
        own = lax.dynamic_slice_in_dim(shard, self.group * rows, rows, 0)
        own4 = jnp.stack([own] + [self.move(own, self.z_pairs[step]) for step in (1, 2, 3)])
        first = self.move(own4, self.first_pairs)
        second = self.move(own4, self.second_pairs)
        both = self.move(first, self.second_pairs)
        half = [own4, first, second, both]
        return half + [self.move(piece, self.core_pairs) for piece in half]

    def scatter(self, send, keep):
        got = self.move(send, self.first_pairs)
        got = self.move(add(keep[1], got[1]), self.second_pairs), got[0]
        kept = keep[0]
        total = kept[0].astype(F32) + got[1][0].astype(F32) + got[0][0].astype(F32)
        for step in (1, 2, 3):
            part = (kept[step].astype(F32) + got[1][step].astype(F32) + got[0][step].astype(F32)).astype(BF16)
            total = total + self.move(part, self.z_pairs[4 - step]).astype(F32)
        own = total.astype(BF16)
        along = self.move(own, self.y_pairs)
        across = self.move(own, self.core_pairs)
        both = self.move(along, self.core_pairs)
        low, high = swapped(self.core, own, across), swapped(self.core, along, both)
        even, odd = swapped(self.y, low[0], high[0]), swapped(self.y, low[1], high[1])
        return jnp.concatenate([even[0], odd[0], even[1], odd[1]]).astype(F32)

    def gather_small(self, small):
        return jnp.stack([small] + [self.move(small, self.wide_pairs[step]) for step in range(1, 8)])

    def in_order(self, parts):
        return lax.dynamic_slice_in_dim(jnp.concatenate([parts, parts]), (8 - self.wide) % 8, 8, 0)

    def spread_rows(self, parts):
        total = parts[0]
        for step in range(1, 8):
            total = total + self.move(parts[step], self.wide_pairs[8 - step])
        return total

    def gather_all(self, rows):
        for pairs in (self.core_pairs, self.x_pairs, self.y_pairs):
            rows = jnp.concatenate([rows, self.move(rows, pairs)])
        return jnp.concatenate([rows] + [self.move(rows, self.z_pairs[step]) for step in (1, 2, 3)])

    def sum_small(self, vectors):
        for pairs in (self.core_pairs, self.x_pairs, self.y_pairs):
            vectors = vectors + self.move(vectors, pairs)
        total = vectors
        for step in (1, 2, 3):
            total = total + self.move(vectors, self.z_pairs[step])
        return lax.dynamic_index_in_dim(total, self.wide, 0, keepdims=False)


def rotary_tables(length):
    half = HEAD_DIM // 2
    frequency = jnp.exp(jnp.arange(half, dtype=F32) * (-2.0 * math.log(10000.0) / HEAD_DIM))
    angles = jnp.arange(length, dtype=F32)[:, None] * frequency[None, :]
    sine = jnp.sin(angles)
    cosine = jnp.concatenate([jnp.cos(angles)] * 4, axis=1)
    return cosine, jnp.concatenate([-sine, sine, -sine, sine], axis=1)


def call(kernel, name, tables, grid, ins, outs, scratch=(), flops=0, moved=0):
    def spec(block, index, buffers=None):
        if buffers:
            return pl.BlockSpec(block, index, pipeline_mode=pl.Buffered(buffers))
        return pl.BlockSpec(block, index)

    return pl.pallas_call(
        kernel,
        out_shape=[jax.ShapeDtypeStruct(shape, dtype) for shape, dtype, *_ in outs],
        grid_spec=pltpu.PrefetchScalarGridSpec(
            num_scalar_prefetch=len(tables),
            grid=grid,
            in_specs=[spec(*rest) for _, *rest in ins],
            out_specs=[spec(*rest) for _, _, *rest in outs],
            scratch_shapes=list(scratch),
        ),
        compiler_params=pltpu.CompilerParams(vmem_limit_bytes=VMEM_BYTES),
        cost_estimate=pl.CostEstimate(flops=flops, bytes_accessed=moved, transcendentals=0),
        name=name,
    )(*tables, *[array for array, *_ in ins])


def whole(array, buffers=1):
    rank = array.ndim
    return (array, array.shape, lambda i, *_: (0,) * rank, buffers)


def rows_of(array, tile):
    return (array, (tile, array.shape[1]), lambda i, *_: (i, 0))


def out_rows(shape, dtype, tile):
    return (shape, dtype, (tile, shape[1]), lambda i, *_: (i, 0))


def out_whole(shape, dtype):
    return (shape, dtype, shape, lambda i, *_: (0,) * len(shape))


def put_in_order(places, pieces, held):
    for i in range(BLOCKS):
        held[places[i]] = pieces[i // 4][i % 4]


def matrix(held):
    blocks, rows, columns = held.shape
    return held[...].reshape(blocks * rows, columns)


def normalise(values):
    average = jnp.mean(values, axis=-1, keepdims=True)
    centered = values - average
    scale = lax.rsqrt(jnp.mean(centered * centered, axis=-1, keepdims=True) + EPSILON)
    return centered * scale, scale


def norm_back(grad, hat, scale, gain):
    e = grad * gain
    inner = jnp.mean(e * hat, axis=-1, keepdims=True)
    return scale * (e - jnp.mean(e, axis=-1, keepdims=True) - hat * inner)


def turned(values):
    lane = lax.broadcasted_iota(jnp.int32, values.shape, 1)
    return jnp.where(lane % 64 < 32, pltpu.roll(values, 96, 1), pltpu.roll(values, 32, 1))


def heads(values):
    lane = lax.broadcasted_iota(jnp.int32, values.shape, 1)
    zero = jnp.zeros_like(values)
    return jnp.concatenate([jnp.where(lane < 64, values, zero), jnp.where(lane < 64, zero, values)], axis=0)


def put_turned(out, slots, values):
    rows = out.shape[1]
    flipped = values.T
    for j in range(BLOCKS):
        out[slots[j]] = flipped[j * rows : (j + 1) * rows]


def attention_kernel(length, places, slots, tokens, gain, shift, cosine, sine, *refs):
    pieces, (act_turned, qkv, attended, attended_turned), held = refs[:8], refs[8:12], refs[12]
    rows, width = tokens.shape

    @pl.when(pl.program_id(0) == 0)
    def _():
        put_in_order(places, pieces, held)

    hat, _ = normalise(tokens[...].astype(F32))
    act = (hat * gain[...] + shift[...]).astype(BF16)
    put_turned(act_turned, slots, act)
    cos, sin = cosine[...], sine[...]
    for start in range(0, 3 * width, 512):
        part = dot(act, held[:, :, start : start + 512].reshape(width, 512))
        if start < 2 * width:
            for lanes in range(0, 512, 128):
                piece = part[:, lanes : lanes + 128]
                qkv[:, start + lanes : start + lanes + 128] = (piece * cos + turned(piece) * sin).astype(BF16)
        else:
            qkv[:, start : start + 512] = part.astype(BF16)
    for top in range(0, rows, length):
        for lanes in range(0, width, 128):
            q = qkv[top : top + length, lanes : lanes + 128]
            k = heads(qkv[top : top + length, width + lanes : width + lanes + 128])
            v = heads(qkv[top : top + length, 2 * width + lanes : 2 * width + lanes + 128])
            scores = dot_nt(q, k) * HEAD_DIM ** (-0.5)
            probs = []
            for head in range(2):
                own = scores[:, head * length : (head + 1) * length]
                e = jnp.exp(own - jnp.max(own, axis=-1, keepdims=True))
                probs.append((e / jnp.sum(e, axis=-1, keepdims=True)).astype(BF16))
            out = dot(jnp.concatenate(probs, axis=1), v)
            attended[top : top + length, lanes : lanes + 128] = out.astype(BF16)
    put_turned(attended_turned, slots, attended[...])


def middle_kernel(length, places, slots, tokens, attended, scales, gain, shift, *refs):
    pieces, (middle, act, act_turned), held = refs[:8], refs[8:11], refs[11]
    rows = tokens.shape[0]

    @pl.when(pl.program_id(0) == 0)
    def _():
        put_in_order(places, pieces, held)

    values = tokens[...].astype(F32) + dot(attended[...], matrix(held))
    middle[...] = values
    hat, _ = normalise(values)
    normed = hat * gain[...] + shift[...]
    first = pl.program_id(0) * (rows // length)
    for s in range(rows // length):
        act[s * length : (s + 1) * length, :] = (
            normed[s * length : (s + 1) * length, :] * scales[pl.ds(first + s, 1), :]
        ).astype(BF16)
    put_turned(act_turned, slots, act[...])


def up_kernel(places, act, bias, *refs):
    pieces, (hidden, slope), held = refs[:8], refs[8:10], refs[10]
    put_in_order(places, pieces, held)
    v = dot(act[...], matrix(held)) + bias[...]
    a = jnp.abs(v) * math.sqrt(0.5)
    t = 1.0 / (1.0 + 0.3275911 * a)
    bell = jnp.exp(-0.5 * v * v)
    series = ((((1.061405429 * t - 1.453152027) * t + 1.421413741) * t - 0.284496736) * t + 0.254829592) * t
    tail = 0.5 * series * bell
    area = jnp.where(v < 0, tail, 1.0 - tail)
    hidden[...] = (v * area).astype(BF16)
    slope[...] = (area + v * bell * (1.0 / math.sqrt(2.0 * math.pi))).astype(BF16)


def down_grad_kernel(with_got, places, *refs):
    blocks, cotangent = refs[:4], refs[4]
    part = jnp.concatenate([block[...] for block in blocks], axis=1)
    total = dot(part.T, cotangent[...]).reshape(4, -1, cotangent.shape[1])
    if not with_got:
        refs[5][0] = total.astype(BF16)
        return
    got, send, keep = refs[5:8]
    total = (total + got[0].astype(F32)).astype(BF16)

    @pl.when(pl.program_id(0) < 2)
    def _():
        send[0] = total

    @pl.when(pl.program_id(0) >= 2)
    def _():
        keep[0] = total


def weight_grad_kernel(with_got, turned_act, grad, *refs):
    blocks, rows = turned_act.shape[:2]
    total = dot(turned_act[...].reshape(blocks * rows, -1), grad[...]).reshape(4, 4, rows, -1)
    if not with_got:
        refs[0][...] = total.astype(BF16)
        return
    got, send, keep = refs
    total = (total + got[...].astype(F32)).astype(BF16)
    for second in range(2):
        keep[second] = total[2 * second]
        send[second] = total[2 * second + 1]


def pre_grad_kernel(places, cotangent, slope, *refs):
    pieces, (grad_pre, bias), held = refs[:8], refs[8:10], refs[10]

    @pl.when(pl.program_id(0) == 0)
    def _():
        put_in_order(places, pieces, held)

    count = slope.shape[1] // held.shape[1]
    rows = held[pl.ds(pl.program_id(0) * count, count)].reshape(slope.shape[1], -1)
    grad = (dot_nt(cotangent[...], rows) * slope[...].astype(F32)).astype(BF16)
    grad_pre[...] = grad
    bias[...] = jnp.sum(grad.astype(F32), axis=0, keepdims=True)


def output_kernel(places, hidden, middle, bias, *refs):
    pieces, output, held = refs[:8], refs[8], refs[9]

    @pl.when(pl.program_id(0) == 0)
    def _():
        put_in_order(places, pieces, held)

    output[...] = (middle[...] + dot(hidden[...], matrix(held)) + bias[...]).astype(BF16)


def middle_grad_kernel(length, places, grad_pre, middle, cotangent, scales, gain, shift, *refs):
    pieces, (grad_middle, grad_branch, grad_scale, gain_sum, shift_sum), held = refs[:8], refs[8:13], refs[13]
    rows = middle.shape[0]

    @pl.when(pl.program_id(0) == 0)
    def _():
        put_in_order(places, pieces, held)
        gain_sum[...] = jnp.zeros_like(gain_sum)
        shift_sum[...] = jnp.zeros_like(shift_sum)

    grad_scaled = dot_nt(grad_pre[...], matrix(held))
    hat, scale = normalise(middle[...])
    first = pl.program_id(0) * (rows // length)
    for s in range(rows // length):
        at = slice(s * length, (s + 1) * length)
        own, own_hat = grad_scaled[at], hat[at]
        normed = own_hat * gain[...] + shift[...]
        grad_scale[pl.ds(first + s, 1), :] = jnp.sum(own * normed, axis=0, keepdims=True)
        grad = own * scales[pl.ds(first + s, 1), :]
        gain_sum[...] += jnp.sum(grad * own_hat, axis=0, keepdims=True)
        shift_sum[...] += jnp.sum(grad, axis=0, keepdims=True)
        total = cotangent[at, :].astype(F32) + norm_back(grad, own_hat, scale[at], gain[...])
        grad_middle[at, :] = total
        grad_branch[at, :] = total.astype(BF16)


def attention_grad_kernel(length, places, grad_branch, qkv, cosine, sine, *refs):
    pieces, grad_projected, held, grad_attended = refs[:8], refs[8], refs[9], refs[10]
    rows, width = grad_branch.shape
    factor = HEAD_DIM ** (-0.5)

    @pl.when(pl.program_id(0) == 0)
    def _():
        put_in_order(places, pieces, held)

    grad_attended[...] = dot_nt(grad_branch[...], matrix(held)).astype(BF16)
    cos, sin = cosine[...], sine[...]
    for top in range(0, rows, length):
        at = slice(top, top + length)
        for lanes in range(0, width, 128):
            q = heads(qkv[at, lanes : lanes + 128])
            k = qkv[at, width + lanes : width + lanes + 128]
            v = qkv[at, 2 * width + lanes : 2 * width + lanes + 128]
            g = heads(grad_attended[at, lanes : lanes + 128])
            scores = dot_nt(k, q) * factor
            e = jnp.exp(scores - jnp.max(scores, axis=0, keepdims=True))
            probs = e / jnp.sum(e, axis=0, keepdims=True)
            grad_values = dot(probs.astype(BF16), g)
            grad_probs = dot_nt(v, g)
            inner = jnp.sum(grad_probs * probs, axis=0, keepdims=True)
            grad_scores = (probs * (grad_probs - inner)).astype(BF16)
            grad_keys = dot(grad_scores, q) * factor
            flipped = jnp.concatenate([grad_scores[:, :length].T, grad_scores[:, length:].T], axis=1)
            grad_queries = dot(flipped, heads(k)) * factor
            for start, grad in ((lanes, grad_queries), (width + lanes, grad_keys)):
                grad_projected[at, start : start + 128] = (grad * cos[at] - turned(grad) * sin[at]).astype(BF16)
            grad_projected[at, 2 * width + lanes : 2 * width + lanes + 128] = grad_values.astype(BF16)


def token_grad_kernel(places, grad_projected, tokens, grad_middle, gain, *refs):
    pieces, (grad_tokens, gain_sum, shift_sum), held = refs[:8], refs[8:11], refs[11]

    @pl.when(pl.program_id(0) == 0)
    def _():
        put_in_order(places, pieces, held)
        gain_sum[...] = jnp.zeros_like(gain_sum)
        shift_sum[...] = jnp.zeros_like(shift_sum)

    grad = dot_nt(grad_projected[...], matrix(held))
    hat, scale = normalise(tokens[...].astype(F32))
    gain_sum[...] += jnp.sum(grad * hat, axis=0, keepdims=True)
    shift_sum[...] += jnp.sum(grad, axis=0, keepdims=True)
    grad_tokens[...] = grad_middle[...] + norm_back(grad, hat, scale, gain[...])


def shards(plan, tokens, cotangent, noise_index, time_embed, ln1_gain, ln1_shift, w_qkv, w_out, ln2_gain, ln2_shift,
           w_time, w_up, up_bias, w_down, down_bias):
    rows, width = tokens.shape
    seqs = noise_index.shape[0]
    length = rows // seqs
    levels = time_embed.shape[0]
    ff = w_up.shape[1]
    tile = 2 * length
    steps = rows // tile
    per = ln1_gain.shape[0]

    def chosen(index, table):
        picks = (index[:, None] == jnp.arange(levels, dtype=jnp.int32)[None, :]).astype(BF16)
        return dot(picks, table).astype(BF16)

    if plan is not None:
        places, slots = plan.enter()
        lines = [v.reshape(-1, per) for v in (ln1_gain, ln1_shift, ln2_gain, ln2_shift, down_bias, up_bias)]
        index_line = jnp.pad(noise_index.astype(BF16), (0, per - seqs))[None]
        small = plan.gather_small(jnp.concatenate(lines + [index_line]))
        vectors = plan.in_order(small)
        gain_one, shift_one, gain_two, shift_two, bias_down = [
            vectors[:, i].reshape(1, -1).astype(F32) for i in range(5)
        ]
        bias_up = vectors[:, 5:-1].reshape(1, -1).astype(F32)
        near = small[:, -1, :seqs].reshape(-1).astype(jnp.int32)
        own_levels = lax.dynamic_slice_in_dim(time_embed, plan.wide * per, per, 1)
        partial = dot(chosen(near, own_levels), w_time).reshape(-1, seqs, width)
        scales = 1.0 + plan.spread_rows(partial)
        full = [plan.gather(w) for w in (w_qkv, w_out, w_up, w_down)]
    else:
        places = slots = jnp.arange(BLOCKS, dtype=jnp.int32)

        def gathered(v):
            return lax.all_gather(v, "wide", axis=0, tiled=True)

        gain_one, shift_one, gain_two, shift_two, bias_down, bias_up = [
            gathered(v).astype(F32)[None] for v in (ln1_gain, ln1_shift, ln2_gain, ln2_shift, down_bias, up_bias)
        ]
        embedded = chosen(noise_index, time_embed)
        scales = 1.0 + dot(embedded, gathered(w_time))
        full = []
        for w in (w_qkv, w_out, w_up, w_down):
            w = gathered(w)
            full.append(list(w.reshape(8, 4, w.shape[0] // BLOCKS, w.shape[1])))
    qkv_pieces, out_pieces, up_pieces, down_pieces = full
    cosine, sine = rotary_tables(length)
    cosine, sine = jnp.tile(cosine, (tile // length, 1)), jnp.tile(sine, (tile // length, 1))
    deep = width // BLOCKS

    def held(pieces):
        _, r, c = pieces[0].shape
        return pltpu.VMEM((BLOCKS, r, c), BF16)

    def turned_out():
        return ((BLOCKS, deep, rows), BF16, (BLOCKS, deep, tile), lambda i, *_: (0, 0, i))

    act_one_turned, qkv, attended, attended_turned = call(
        functools.partial(attention_kernel, length), "attention", (places, slots), (steps,),
        [rows_of(tokens, tile), whole(gain_one), whole(shift_one), whole(cosine), whole(sine)]
        + [whole(p) for p in qkv_pieces],
        [turned_out(), out_rows((rows, 3 * width), BF16, tile), out_rows((rows, width), BF16, tile), turned_out()],
        [held(qkv_pieces)], flops=2 * rows * width * 3 * width * 2, moved=20 * rows * width,
    )
    middle, act_two, act_two_turned = call(
        functools.partial(middle_kernel, length), "middle", (places, slots), (steps,),
        [rows_of(tokens, tile), rows_of(attended, tile), whole(scales), whole(gain_two), whole(shift_two)]
        + [whole(p) for p in out_pieces],
        [out_rows((rows, width), F32, tile), out_rows((rows, width), BF16, tile), turned_out()],
        [held(out_pieces)], flops=2 * rows * width * width * 2, moved=14 * rows * width,
    )
    strip = 512
    strips = ff // strip

    def columns_of(array, wide=strip):
        return (array, (array.shape[0], wide), lambda i, *_: (0, i))

    def piece_columns(piece):
        return (piece, piece.shape[:2] + (strip,), lambda i, *_: (0, 0, i))

    def out_columns(shape, dtype):
        return (shape, dtype, shape[:-1] + (strip,), lambda i, *_: (0,) * (len(shape) - 1) + (i,))

    hidden, slope = call(
        up_kernel, "up", (places,), (strips,),
        [whole(act_two), columns_of(bias_up)] + [piece_columns(p) for p in up_pieces],
        [out_columns((rows, ff), BF16), out_columns((rows, ff), BF16)],
        [pltpu.VMEM((BLOCKS, deep, strip), BF16)], flops=2 * rows * width * ff * 2, moved=26 * rows * width,
    )

    def down_grad(order, got):
        order = jnp.asarray(order, jnp.int32)
        table = places.reshape(8, 4)[order].reshape(-1)
        fr = ff // BLOCKS
        ins = [(hidden, (rows, fr), lambda i, t, o, j=j: (0, t[4 * i + j])) for j in range(4)] + [whole(cotangent)]
        block = (1, 4, fr, width)
        if got is None:
            outs = [((4, 4, fr, width), BF16, block, lambda i, t, o: (i, 0, 0, 0))]
        else:
            ins.append((got, block, lambda i, t, o: (o[i], 0, 0, 0)))
            outs = [
                ((2, 4, fr, width), BF16, block, lambda i, t, o: (jnp.minimum(i, 1), 0, 0, 0)),
                ((2, 4, fr, width), BF16, block, lambda i, t, o: (jnp.maximum(i - 2, 0), 0, 0, 0)),
            ]

        def kernel(t, o, *refs):
            down_grad_kernel(got is not None, t, *refs)

        return call(kernel, "down_grad", (table, order), (4,), ins, outs,
                    flops=rows * width * ff, moved=8 * rows * width)

    def weight_grad(turned_act, grad, half, got):
        ins = [
            (turned_act, (BLOCKS // 2, deep, rows), lambda i, *_: (half, 0, 0), 1),
            columns_of(grad),
        ]
        columns = grad.shape[1]
        if got is None:
            outs = [out_columns((4, 4, deep, columns), BF16)]
        else:
            ins.append((got, (4, 4, deep, strip), lambda i, *_: (0, 0, 0, i)))
            outs = [out_columns((2, 4, deep, columns), BF16)] * 2
        return call(functools.partial(weight_grad_kernel, got is not None), "weight_grad", (), (columns // strip,),
                    ins, outs, flops=rows * width * columns, moved=3 * rows * columns)

    def summed(theirs, ours):
        (sent,) = theirs()
        if plan is not None:
            return plan.scatter(*ours(plan.move(sent, plan.core_pairs)))
        send, keep = ours(jnp.zeros_like(sent))
        mine = jnp.stack([keep[0], send[0], keep[1], send[1]])
        grad = jnp.concatenate([mine, sent]).reshape(-1, sent.shape[-1])
        grad = lax.psum_scatter(grad, "wide", scatter_dimension=0, tiled=True)
        return lax.psum(grad, "group").astype(F32)

    grad_w_down = summed(lambda: down_grad((4, 5, 6, 7), None), lambda got: down_grad((1, 3, 0, 2), got))
    grad_down_bias = jnp.sum(cotangent.astype(F32), axis=0)
    grad_pre, grad_up_bias = call(
        pre_grad_kernel, "pre_grad", (places,), (strips,),
        [whole(cotangent), columns_of(slope)] + [whole(p) for p in down_pieces],
        [out_columns((rows, ff), BF16), out_columns((1, ff), F32)],
        [held(down_pieces)], flops=2 * rows * width * ff, moved=26 * rows * width,
    )
    grad_w_up = summed(
        lambda: weight_grad(act_two_turned, grad_pre, 1, None), lambda got: weight_grad(act_two_turned, grad_pre, 0, got)
    )
    (output,) = call(
        output_kernel, "output", (places,), (steps,),
        [rows_of(hidden, tile), rows_of(middle, tile), whole(bias_down)] + [whole(p) for p in down_pieces],
        [out_rows((rows, width), BF16, tile)],
        [held(down_pieces)], flops=2 * rows * width * ff, moved=22 * rows * width,
    )
    grad_middle, grad_branch, grad_scale, grad_gain_two, grad_shift_two = call(
        functools.partial(middle_grad_kernel, length), "middle_grad", (places,), (steps,),
        [rows_of(grad_pre, tile), rows_of(middle, tile), rows_of(cotangent, tile), whole(scales), whole(gain_two)]
        + [whole(shift_two)] + [whole(p) for p in up_pieces],
        [out_rows((rows, width), F32, tile), out_rows((rows, width), BF16, tile), out_whole((seqs, width), F32)]
        + [out_whole((1, width), F32)] * 2,
        [held(up_pieces)], flops=2 * rows * width * ff, moved=28 * rows * width,
    )
    grad_scale = grad_scale.astype(BF16)
    grad_w_out = summed(
        lambda: weight_grad(attended_turned, grad_branch, 1, None),
        lambda got: weight_grad(attended_turned, grad_branch, 0, got),
    )
    (grad_projected,) = call(
        functools.partial(attention_grad_kernel, length), "attention_grad", (places,), (steps,),
        [rows_of(grad_branch, tile), rows_of(qkv, tile), whole(cosine), whole(sine)] + [whole(p) for p in out_pieces],
        [out_rows((rows, 3 * width), BF16, tile)],
        [held(out_pieces), pltpu.VMEM((tile, width), BF16)],
        flops=2 * rows * width * 3 * width * 2, moved=16 * rows * width,
    )
    grad_w_qkv = summed(
        lambda: weight_grad(act_one_turned, grad_projected, 1, None),
        lambda got: weight_grad(act_one_turned, grad_projected, 0, got),
    )
    grad_tokens, grad_gain_one, grad_shift_one = call(
        token_grad_kernel, "token_grad", (places,), (steps,),
        [rows_of(grad_projected, tile), rows_of(tokens, tile), rows_of(grad_middle, tile), whole(gain_one)]
        + [whole(p) for p in qkv_pieces],
        [out_rows((rows, width), F32, tile)] + [out_whole((1, width), F32)] * 2,
        [held(qkv_pieces)], flops=2 * rows * width * 3 * width, moved=22 * rows * width,
    )
    sums = (grad_gain_one, grad_shift_one, grad_gain_two, grad_shift_two, grad_down_bias, grad_up_bias)
    if plan is not None:
        index_lanes = jnp.broadcast_to(noise_index.astype(BF16)[:, None], (seqs, 128))
        everyone = plan.gather_all(jnp.concatenate([grad_scale, index_lanes], axis=1))
        picked = chosen(everyone[:, width].astype(jnp.int32), own_levels)
        grad_w_time = lax.dot_general(
            picked, everyone[:, :width], (((0,), (0,)), ((), ())), preferred_element_type=F32
        )
        small_sum = plan.sum_small(jnp.concatenate([v.reshape(8, -1, per) for v in sums], axis=1))
        vec = [small_sum[i] for i in range(5)] + [small_sum[5:].reshape(-1)]
    else:
        grad_w_time = lax.dot_general(
            embedded, grad_scale, (((0,), (0,)), ((), ())), preferred_element_type=F32
        )
        grad_w_time = lax.psum(lax.psum_scatter(grad_w_time, "wide", scatter_dimension=0, tiled=True), "group")
        vec = [
            lax.psum(lax.psum_scatter(v.reshape(-1), "wide", scatter_dimension=0, tiled=True), "group") for v in sums
        ]
    return (output, grad_tokens, vec[0], vec[1], grad_w_qkv, grad_w_out, vec[2], vec[3], grad_w_time, grad_w_up,
            vec[5], grad_w_down, vec[4])


def solution(mesh):
    plan = Plan() if (mesh.shape["group"], mesh.shape["wide"]) == (4, 8) else None
    split, rows, line = P(BOTH, None), P("wide", None), P("wide")
    in_specs = (split, split, P(BOTH), P(), line, line, rows, rows, line, line, rows, rows, line, rows, line)
    out_specs = (split, split, line, line, rows, rows, line, line, rows, rows, line, rows, line)
    return jax.shard_map(
        functools.partial(shards, plan), mesh=mesh, in_specs=in_specs, out_specs=out_specs, check_vma=False
    )
```

```python
import functools
import math

import jax
import jax.numpy as jnp
from jax import lax
from jax.experimental import pallas as pl
from jax.experimental.pallas import tpu as pltpu
from jax.sharding import PartitionSpec as P

HEAD_DIM = 64
EPSILON = 1e-05
BOTH = ("group", "wide")
F32 = jnp.float32
BF16 = jnp.bfloat16
BLOCKS = 32
VMEM_BYTES = 58 * 2**20


def sum_of(*terms):
    total = terms[0].astype(F32)
    for term in terms[1:]:
        total = total + term.astype(F32)
    return total.astype(BF16)


def tie(*values):
    return lax.optimization_barrier(values)


def dot(a, b):
    return jnp.dot(a, b, preferred_element_type=F32)


def dot_nt(a, b):
    return lax.dot_general(a, b, (((1,), (1,)), ((), ())), preferred_element_type=F32)


def dot_tn(a, b):
    return lax.dot_general(a, b, (((0,), (0,)), ((), ())), preferred_element_type=F32)


class Plan:
    def __init__(self):
        def pairs(target):
            found = []
            for index in range(32):
                group, wide = divmod(index, 8)
                y, core, z, x = target(group // 2, group % 2, wide // 2, wide % 2)
                found.append((index, (y * 2 + core) * 8 + z * 2 + x))
            return found

        self.core_pairs = pairs(lambda y, c, z, x: (y, 1 - c, z, x))
        self.y_pairs = pairs(lambda y, c, z, x: (1 - y, c, z, x))
        self.x_pairs = pairs(lambda y, c, z, x: (y, c, z, 1 - x))
        self.first_pairs = pairs(lambda y, c, z, x: (y, c, z, 1 - x) if c == 0 else (1 - y, c, z, x))
        self.second_pairs = pairs(lambda y, c, z, x: (1 - y, c, z, x) if c == 0 else (y, c, z, 1 - x))
        self.z_groups = [[(y * 2 + c) * 8 + z * 2 + x for z in range(4)] for y in (0, 1) for c in (0, 1) for x in (0, 1)]
        self.z_pairs = [pairs(lambda y, c, z, x, step=step: (y, c, (z - step) % 4, x)) for step in range(4)]

    def enter(self):
        self.group = lax.axis_index("group")
        self.wide = lax.axis_index("wide")
        y, core = self.group // 2, self.group % 2
        z, x = self.wide // 2, self.wide % 2
        self.z, self.x, self.y, self.core = z, x, y, core
        slot = jnp.arange(BLOCKS, dtype=jnp.int32)
        holder = core ^ (slot // 16)
        second, first, step = (slot // 8) % 2, (slot // 4) % 2, slot % 4
        across = jnp.where(holder == 0, first, second)
        along = jnp.where(holder == 0, second, first)
        spot = (x ^ across) * 4 + (y ^ along) * 2 + holder
        places, near_places = step * 8 + spot, ((z + step) % 4) * 8 + spot
        block_z, block_x, block_y, block_core = slot // 8, (slot // 4) % 2, (slot // 2) % 2, slot % 2
        off_x, off_y = block_x ^ x, block_y ^ y
        first = jnp.where(block_core == 0, off_x, off_y)
        second = jnp.where(block_core == 0, off_y, off_x)
        spot = (((block_core ^ core) * 2 + second) * 2 + first) * 4
        tables = places, near_places, spot + block_z, spot + (block_z - z) % 4
        return [table.astype(jnp.int32) for table in tables]

    def move(self, value, pairs):
        return lax.ppermute(value, BOTH, pairs)

    def own_block(self, shard):
        rows = shard.shape[0] // 4
        return lax.dynamic_slice_in_dim(shard, self.group * rows, rows, 0)

    def along_z(self, own):
        return lax.all_gather(own, BOTH, axis_index_groups=self.z_groups, axis=0)

    def near_z(self, own):
        return [own] + [self.move(own, self.z_pairs[step]) for step in (1, 2, 3)]

    def first(self, value):
        return self.move(value, self.first_pairs)

    def second(self, value):
        return self.move(value, self.second_pairs)

    def across(self, value):
        return self.move(value, self.core_pairs)

    def over_z(self, part):
        return lax.psum_scatter(part, BOTH, axis_index_groups=self.z_groups, scatter_dimension=0)

    def over_group(self, own):
        return lax.all_gather(own, "group", axis=0, tiled=True)

    def to_z(self, *weights):
        def part(step):
            return jnp.concatenate([sum_of(*[term[step] for term in terms]) for terms in weights], axis=1)

        return [part(0)] + [self.move(part(step), self.z_pairs[4 - step]) for step in (1, 2, 3)]

    def in_group(self, own):
        along = self.move(own, self.y_pairs)
        parts = [own, self.across(own), along, self.across(along)]
        parts = [jnp.where(self.core == 0, parts[i], parts[i ^ 1]) for i in range(4)]
        return jnp.concatenate([jnp.where(self.y == 0, parts[i], parts[i ^ 2]) for i in range(4)])

    def in_wide_order(self, near):
        near = jnp.where(self.x == 0, near, near[:, ::-1])
        near = lax.dynamic_slice_in_dim(jnp.concatenate([near, near]), (4 - self.z) % 4, 4, 0)
        return near.reshape((8,) + near.shape[2:])

    def sum_x(self, pair):
        return pair[0] + self.move(pair[1], self.x_pairs)

    def sum_z(self, near):
        total = near[0]
        for step in (1, 2, 3):
            total = total + self.move(near[step], self.z_pairs[4 - step])
        return total


def rotary_tables(length):
    half = HEAD_DIM // 2
    frequency = jnp.exp(jnp.arange(half, dtype=F32) * (-2.0 * math.log(10000.0) / HEAD_DIM))
    angles = jnp.arange(length, dtype=F32)[:, None] * frequency[None, :]
    sine = jnp.sin(angles)
    cosine = jnp.concatenate([jnp.cos(angles)] * 4, axis=1)
    return cosine, jnp.concatenate([-sine, sine, -sine, sine], axis=1)


def call(kernel, name, tables, grid, ins, outs, scratch=(), flops=0, moved=0):
    def spec(block, index, buffers=None):
        if buffers:
            return pl.BlockSpec(block, index, pipeline_mode=pl.Buffered(buffers))
        return pl.BlockSpec(block, index)

    return pl.pallas_call(
        kernel,
        out_shape=[jax.ShapeDtypeStruct(shape, dtype) for shape, dtype, *_ in outs],
        grid_spec=pltpu.PrefetchScalarGridSpec(
            num_scalar_prefetch=len(tables),
            grid=grid,
            in_specs=[spec(*rest) for _, *rest in ins],
            out_specs=[spec(*rest) for _, _, *rest in outs],
            scratch_shapes=list(scratch),
        ),
        compiler_params=pltpu.CompilerParams(vmem_limit_bytes=VMEM_BYTES),
        cost_estimate=pl.CostEstimate(flops=0, bytes_accessed=0, transcendentals=0),
        name=name,
    )(*tables, *[array for array, *_ in ins])


def whole(array, buffers=1):
    rank = array.ndim
    return (array, array.shape, lambda i, *_: (0,) * rank, buffers)


def columns_at(array, first, count):
    return (array, array.shape[:-1] + (count,), lambda i, *_: (0,) * (array.ndim - 1) + (first // count,), 1)


def rows_of(array, tile):
    return (array, (tile, array.shape[1]), lambda i, *_: (i, 0))


def out_rows(shape, dtype, tile):
    return (shape, dtype, (tile, shape[1]), lambda i, *_: (i, 0))


def out_whole(shape, dtype):
    return (shape, dtype, shape, lambda i, *_: (0,) * len(shape), 1)


def put_in_order(places, pieces, held):
    for i in range(BLOCKS):
        held[places[i]] = pieces[i // 4][i % 4]


def matrix(held):
    blocks, rows, columns = held.shape
    return held[...].reshape(blocks * rows, columns)


def normalise(values):
    average = jnp.mean(values, axis=-1, keepdims=True)
    centered = values - average
    scale = lax.rsqrt(jnp.mean(centered * centered, axis=-1, keepdims=True) + EPSILON)
    return centered * scale, scale


def norm_back(grad, hat, scale, gain):
    e = grad * gain
    inner = jnp.mean(e * hat, axis=-1, keepdims=True)
    return scale * (e - jnp.mean(e, axis=-1, keepdims=True) - hat * inner)


def turned(values):
    lane = lax.broadcasted_iota(jnp.int32, values.shape, 1)
    return jnp.where(lane % 64 < 32, pltpu.roll(values, 96, 1), pltpu.roll(values, 32, 1))


def heads(values):
    lane = lax.broadcasted_iota(jnp.int32, values.shape, 1)
    zero = jnp.zeros_like(values)
    return jnp.concatenate([jnp.where(lane < 64, values, zero), jnp.where(lane < 64, zero, values)], axis=0)


def put_turned(out, slots, values):
    rows = out.shape[1]
    flipped = values.T
    for j in range(BLOCKS):
        out[slots[j]] = flipped[j * rows : (j + 1) * rows]


def attention_kernel(length, places, slots, tokens, gain, shift, cosine, sine, *refs):
    pieces, (act_turned, qkv, attended, attended_turned), held = refs[:8], refs[8:12], refs[12]
    rows, width = tokens.shape

    @pl.when(pl.program_id(0) == 0)
    def _():
        put_in_order(places, pieces, held)

    hat, _ = normalise(tokens[...].astype(F32))
    act = (hat * gain[...] + shift[...]).astype(BF16)
    put_turned(act_turned, slots, act)
    cos, sin = cosine[...], sine[...]
    for start in range(0, 3 * width, 512):
        part = dot(act, held[:, :, start : start + 512].reshape(width, 512))
        if start < 2 * width:
            for lanes in range(0, 512, 128):
                piece = part[:, lanes : lanes + 128]
                qkv[:, start + lanes : start + lanes + 128] = (piece * cos + turned(piece) * sin).astype(BF16)
        else:
            qkv[:, start : start + 512] = part.astype(BF16)
    for top in range(0, rows, length):
        for lanes in range(0, width, 128):
            q = qkv[top : top + length, lanes : lanes + 128]
            k = heads(qkv[top : top + length, width + lanes : width + lanes + 128])
            v = heads(qkv[top : top + length, 2 * width + lanes : 2 * width + lanes + 128])
            scores = dot_nt(q, k) * HEAD_DIM ** (-0.5)
            probs = []
            for head in range(2):
                own = scores[:, head * length : (head + 1) * length]
                e = jnp.exp(own - jnp.max(own, axis=-1, keepdims=True))
                probs.append((e / jnp.sum(e, axis=-1, keepdims=True)).astype(BF16))
            out = dot(jnp.concatenate(probs, axis=1), v)
            attended[top : top + length, lanes : lanes + 128] = out.astype(BF16)
    put_turned(attended_turned, slots, attended[...])


def middle_kernel(length, places, near_slots, slots, tokens, attended, scales, gain, shift, *refs):
    pieces, (middle, act, act_turned), held = refs[:8], refs[8:11], refs[11]
    rows = tokens.shape[0]

    @pl.when(pl.program_id(0) == 0)
    def _():
        put_in_order(places, pieces, held)

    values = tokens[...].astype(F32) + dot(attended[...], matrix(held))
    middle[...] = values
    hat, _ = normalise(values)
    normed = hat * gain[...] + shift[...]
    first = pl.program_id(0) * (rows // length)
    for s in range(rows // length):
        act[s * length : (s + 1) * length, :] = (
            normed[s * length : (s + 1) * length, :] * scales[pl.ds(first + s, 1), :]
        ).astype(BF16)
    put_turned(act_turned, slots, act[...])


def split_out(slot, block, theirs, send, keep):
    piece, at = slot // 4, slot % 4

    @pl.when(slot >= BLOCKS // 2)
    def _():
        theirs[piece - 4, at] = block

    @pl.when((slot < BLOCKS // 2) & (piece % 2 == 1))
    def _():
        send[piece // 2, at] = block

    @pl.when((slot < BLOCKS // 2) & (piece % 2 == 0))
    def _():
        keep[piece // 2, at] = block


def up_kernel(places, slots, act, bias, cotangent, *refs):
    pieces, (hidden, slope, theirs, send, keep), held = refs[:8], refs[8:13], refs[13]
    put_in_order(places, pieces, held)
    v = dot(act[...], matrix(held)) + bias[...]
    area = 0.5 + 0.5 * lax.erf(v * math.sqrt(0.5))
    low = (v * area).astype(BF16)
    hidden[...] = low
    slope[...] = (area + v * jnp.exp(-0.5 * v * v) * (1.0 / math.sqrt(2.0 * math.pi))).astype(BF16)
    grad = dot_tn(low, cotangent[...]).astype(BF16)
    rows = theirs.shape[2]
    count = hidden.shape[1] // rows
    for k in range(count):
        split_out(slots[pl.program_id(0) * count + k], grad[k * rows : (k + 1) * rows], theirs, send, keep)


def near_grad_kernel(strips, act_one, grad_projected, attended, grad_branch, theirs, send, keep):
    blocks, rows = act_one.shape[:2]

    @pl.when(pl.program_id(0) < strips)
    def _():
        put_apart(dot(act_one[...].reshape(blocks * rows, -1), grad_projected[...]), rows, theirs, send, keep)

    @pl.when(pl.program_id(0) >= strips)
    def _():
        put_apart(dot(attended[...].reshape(blocks * rows, -1), grad_branch[...]), rows, theirs, send, keep)


def put_apart(total, rows, theirs, send, keep):
    total = total.astype(BF16).reshape(8, 4, rows, -1)
    theirs[...] = total[4:]
    for second in range(2):
        keep[second] = total[2 * second]
        send[second] = total[2 * second + 1]


def feed_back_kernel(length, places, cotangent, slope, turned_act, middle, scales, gain, shift, *refs):
    down, up = refs[:8], refs[8:16]
    theirs, send, keep, bias, grad_middle, grad_branch, grad_scale, gain_sum, shift_sum = refs[16:25]
    held_down, held_up, total = refs[25:]
    step = pl.program_id(0)

    @pl.when(step == 0)
    def _():
        put_in_order(places, down, held_down)
        total[...] = jnp.zeros_like(total)

    put_in_order(places, up, held_up)
    strip = slope.shape[1]
    count = strip // held_down.shape[1]
    rows = held_down[pl.ds(step * count, count)].reshape(strip, -1)
    grad = (dot_nt(cotangent[...], rows) * slope[...].astype(F32)).astype(BF16)
    bias[...] = jnp.sum(grad.astype(F32), axis=0, keepdims=True)
    blocks, deep = turned_act.shape[:2]
    put_apart(dot(turned_act[...].reshape(blocks * deep, -1), grad), deep, theirs, send, keep)
    total[...] += dot_nt(grad, matrix(held_up))

    @pl.when(step == pl.num_programs(0) - 1)
    def _():
        gains, shifts = jnp.zeros_like(gain_sum), jnp.zeros_like(shift_sum)
        for s in range(middle.shape[0] // length):
            at = slice(s * length, (s + 1) * length)
            own = total[at, :]
            hat, scale = normalise(middle[at, :])
            normed = hat * gain[...] + shift[...]
            grad_scale[s : s + 1, :] = jnp.sum(own * normed, axis=0, keepdims=True)
            grad = own * scales[s : s + 1, :]
            gains += jnp.sum(grad * hat, axis=0, keepdims=True)
            shifts += jnp.sum(grad, axis=0, keepdims=True)
            out = cotangent[at, :].astype(F32) + norm_back(grad, hat, scale, gain[...])
            grad_middle[at, :] = out
            grad_branch[at, :] = out.astype(BF16)
        gain_sum[...] = gains
        shift_sum[...] = shifts


def sum_kernel(*refs):
    total = refs[0][...].astype(F32)
    for ref in refs[1:-1]:
        total = total + ref[...].astype(F32)
    refs[-1][...] = total.astype(BF16)


def sum_pieces(count, *terms):
    _, _, rows, columns = terms[0][0].shape
    block = (1, 2, rows, columns)
    ins = [
        (array, block, lambda i, first=first, stride=stride: (first + stride * (i // 2), i % 2, 0, 0))
        for array, first, stride in terms
    ]
    out = ((count, 4, rows, columns), BF16, block, lambda i: (i // 2, i % 2, 0, 0))
    size = count * 4 * rows * columns
    return call(sum_kernel, "sum_pieces", (), (2 * count,), ins, [out], flops=size, moved=2 * size * (len(terms) + 1))[0]


def output_kernel(places, hidden, middle, bias, *refs):
    pieces, output, held = refs[:8], refs[8], refs[9]

    @pl.when(pl.program_id(0) == 0)
    def _():
        put_in_order(places, pieces, held)

    output[...] = (middle[...] + dot(hidden[...], matrix(held)) + bias[...]).astype(BF16)


def attention_grad_kernel(length, places, grad_branch, qkv, cosine, sine, *refs):
    pieces, grad_projected, held, grad_attended = refs[:8], refs[8], refs[9], refs[10]
    rows, width = grad_branch.shape
    factor = HEAD_DIM ** (-0.5)

    @pl.when(pl.program_id(0) == 0)
    def _():
        put_in_order(places, pieces, held)

    grad_attended[...] = dot_nt(grad_branch[...], matrix(held)).astype(BF16)
    cos, sin = cosine[...], sine[...]
    for top in range(0, rows, length):
        at = slice(top, top + length)
        for lanes in range(0, width, 128):
            q = heads(qkv[at, lanes : lanes + 128])
            k = qkv[at, width + lanes : width + lanes + 128]
            v = qkv[at, 2 * width + lanes : 2 * width + lanes + 128]
            g = heads(grad_attended[at, lanes : lanes + 128])
            scores = dot_nt(k, q) * factor
            e = jnp.exp(scores - jnp.max(scores, axis=0, keepdims=True))
            probs = e / jnp.sum(e, axis=0, keepdims=True)
            grad_values = dot(probs.astype(BF16), g)
            grad_probs = dot_nt(v, g)
            inner = jnp.sum(grad_probs * probs, axis=0, keepdims=True)
            grad_scores = (probs * (grad_probs - inner)).astype(BF16)
            grad_keys = dot(grad_scores, q) * factor
            flipped = jnp.concatenate([grad_scores[:, :length].T, grad_scores[:, length:].T], axis=1)
            grad_queries = dot(flipped, heads(k)) * factor
            for start, grad in ((lanes, grad_queries), (width + lanes, grad_keys)):
                grad_projected[at, start : start + 128] = (grad * cos[at] - turned(grad) * sin[at]).astype(BF16)
            grad_projected[at, 2 * width + lanes : 2 * width + lanes + 128] = grad_values.astype(BF16)


def token_grad_kernel(places, grad_projected, tokens, grad_middle, gain, *refs):
    pieces, (grad_tokens, gain_sum, shift_sum), held = refs[:8], refs[8:11], refs[11]

    @pl.when(pl.program_id(0) == 0)
    def _():
        put_in_order(places, pieces, held)
        gain_sum[...] = jnp.zeros_like(gain_sum)
        shift_sum[...] = jnp.zeros_like(shift_sum)

    grad = dot_nt(grad_projected[...], matrix(held))
    hat, scale = normalise(tokens[...].astype(F32))
    gain_sum[...] += jnp.sum(grad * hat, axis=0, keepdims=True)
    shift_sum[...] += jnp.sum(grad, axis=0, keepdims=True)
    grad_tokens[...] = grad_middle[...] + norm_back(grad, hat, scale, gain[...])


class Fallback:
    def vector(self, shard):
        return lax.all_gather(shard, "wide", axis=0, tiled=True).astype(F32)[None]

    def pieces(self, shard):
        full = lax.all_gather(shard, "wide", axis=0, tiled=True)
        return list(full.reshape(8, 4, full.shape[0] // BLOCKS, full.shape[1]))

    def sum(self, grad):
        grad = lax.psum_scatter(grad, "wide", scatter_dimension=0, tiled=True)
        return lax.psum(grad, "group").astype(F32)


class Layer:
    def __init__(self, tokens, cotangent, seqs, ff, places, near_places, slots, near_slots):
        self.tokens, self.cotangent = tokens, cotangent
        self.places, self.near_places, self.slots, self.near_slots = places, near_places, slots, near_slots
        self.rows, self.width = tokens.shape
        self.seqs, self.ff = seqs, ff
        self.length = self.rows // seqs
        self.tile = 2 * self.length
        self.steps = self.rows // self.tile
        self.strip = 512
        self.deep = self.width // BLOCKS
        cosine, sine = rotary_tables(self.length)
        self.tables = [jnp.tile(t, (self.tile // self.length, 1)) for t in (cosine, sine)]

    def held(self, pieces):
        return pltpu.VMEM((BLOCKS,) + pieces[0].shape[1:], BF16)

    def qkv_part(self, pieces):
        return [columns_at(p, 0, 3 * self.width) for p in pieces]

    def out_part(self, pieces):
        return [columns_at(p, 3 * self.width, self.width) for p in pieces]

    def held_part(self, columns):
        return pltpu.VMEM((BLOCKS, self.deep, columns), BF16)

    def turned_out(self):
        return ((BLOCKS, self.deep, self.rows), BF16, (BLOCKS, self.deep, self.tile), lambda i, *_: (0, 0, i))

    def by_rows(self, array):
        return rows_of(array, self.tile)

    def rows_out(self, columns, dtype):
        return out_rows((self.rows, columns), dtype, self.tile)

    def by_columns(self, array):
        return (array, array.shape[:-1] + (self.strip,), lambda i, *_: (0,) * (array.ndim - 1) + (i,))

    def columns_out(self, shape, dtype):
        return (shape, dtype, shape[:-1] + (self.strip,), lambda i, *_: (0,) * (len(shape) - 1) + (i,))

    def attention(self, gain, shift, pieces):
        rows, width = self.rows, self.width
        return call(
            functools.partial(attention_kernel, self.length), "attention", (self.near_places, self.near_slots), (self.steps,),
            [self.by_rows(self.tokens), whole(gain), whole(shift)] + [whole(t) for t in self.tables]
            + self.qkv_part(pieces),
            [self.turned_out(), self.rows_out(3 * width, BF16), self.rows_out(width, BF16), self.turned_out()],
            [self.held_part(3 * width)], flops=12 * rows * width * width, moved=20 * rows * width,
        )

    def middle(self, attended, scales, gain, shift, pieces):
        rows, width = self.rows, self.width
        return call(
            functools.partial(middle_kernel, self.length), "middle", (self.near_places, self.near_slots, self.slots), (self.steps,),
            [self.by_rows(self.tokens), self.by_rows(attended), whole(scales), whole(gain), whole(shift)]
            + self.out_part(pieces),
            [self.rows_out(width, F32), self.rows_out(width, BF16), self.turned_out()],
            [self.held_part(width)], flops=4 * rows * width * width, moved=14 * rows * width,
        )

    def up(self, act, bias, pieces):
        rows, width, ff = self.rows, self.width, self.ff
        fr = ff // BLOCKS
        return call(
            up_kernel, "up", (self.places, self.slots), (ff // self.strip,),
            [whole(act), self.by_columns(bias), whole(self.cotangent)] + [self.by_columns(p) for p in pieces],
            [self.columns_out((rows, ff), BF16)] * 2 + [out_whole((n, 4, fr, width), BF16) for n in (4, 2, 2)],
            [pltpu.VMEM((BLOCKS, self.deep, self.strip), BF16)],
            flops=4 * rows * width * ff, moved=8 * rows * ff,
        )

    def near_grad(self, act_one, grad_projected, attended, grad_branch, half):
        columns, strip = 2 * self.width, self.strip
        strips = 3 * self.width // strip
        at = half * columns // strip
        ins = [
            whole(act_one),
            (grad_projected, (self.rows, strip), lambda i: (0, jnp.minimum(i + at, strips - 1))),
            whole(attended),
            (grad_branch, (self.rows, strip), lambda i: (0, jnp.maximum(i + at - strips, 0))),
        ]
        return call(
            functools.partial(near_grad_kernel, strips - at), "near_grad", (), (columns // strip,), ins,
            [self.columns_out((n, 4, self.deep, columns), BF16) for n in (4, 2, 2)],
            flops=2 * self.rows * self.width * columns, moved=4 * self.rows * columns,
        )

    def feed_back(self, slope, act, middle, scales, gain, shift, down, up):
        rows, width, ff = self.rows, self.width, self.ff
        return call(
            functools.partial(feed_back_kernel, self.length), "feed_back", (self.places,), (ff // self.strip,),
            [whole(self.cotangent), self.by_columns(slope)] + [whole(v) for v in (act, middle, scales, gain, shift)]
            + [whole(p) for p in down] + [self.by_columns(p) for p in up],
            [self.columns_out((n, 4, self.deep, ff), BF16) for n in (4, 2, 2)]
            + [self.columns_out((1, ff), F32), out_whole((rows, width), F32), out_whole((rows, width), BF16)]
            + [out_whole((self.seqs, width), F32)] + [out_whole((1, width), F32)] * 2,
            [self.held(down), pltpu.VMEM((BLOCKS, self.deep, self.strip), BF16), pltpu.VMEM((rows, width), F32)],
            flops=6 * rows * width * ff, moved=10 * rows * ff,
        )

    def output(self, hidden, middle, bias, pieces):
        rows, width = self.rows, self.width
        return call(
            output_kernel, "output", (self.places,), (self.steps,),
            [self.by_rows(hidden), self.by_rows(middle), whole(bias)] + [whole(p) for p in pieces],
            [self.rows_out(width, BF16)],
            [self.held(pieces)], flops=2 * rows * width * self.ff, moved=22 * rows * width,
        )[0]

    def attention_grad(self, grad_branch, qkv, pieces):
        rows, width = self.rows, self.width
        return call(
            functools.partial(attention_grad_kernel, self.length), "attention_grad", (self.near_places,), (self.steps,),
            [self.by_rows(grad_branch), self.by_rows(qkv)] + [whole(t) for t in self.tables] + self.out_part(pieces),
            [self.rows_out(3 * width, BF16)],
            [self.held_part(width), pltpu.VMEM((self.tile, width), BF16)],
            flops=12 * rows * width * width, moved=16 * rows * width,
        )[0]

    def token_grad(self, grad_projected, grad_middle, gain, pieces):
        rows, width = self.rows, self.width
        return call(
            token_grad_kernel, "token_grad", (self.near_places,), (self.steps,),
            [self.by_rows(grad_projected), self.by_rows(self.tokens), self.by_rows(grad_middle), whole(gain)]
            + self.qkv_part(pieces),
            [self.rows_out(width, F32)] + [out_whole((1, width), F32)] * 2,
            [self.held_part(3 * width)], flops=6 * rows * width * width, moved=22 * rows * width,
        )


def chosen(index, table):
    levels = jnp.arange(table.shape[0], dtype=jnp.int32)
    return dot((index[:, None] == levels[None, :]).astype(BF16), table).astype(BF16)


def outer(a, b):
    return lax.dot_general(a, b, (((0,), (0,)), ((), ())), preferred_element_type=F32)


def fallback_shards(tokens, cotangent, noise_index, time_embed, ln1_gain, ln1_shift, w_qkv, w_out, ln2_gain, ln2_shift,
                    w_time, w_up, up_bias, w_down, down_bias):
    net = Fallback()
    order = jnp.arange(BLOCKS, dtype=jnp.int32)
    layer = Layer(tokens, cotangent, noise_index.shape[0], w_up.shape[1], order, order, order, order)
    gain_one, shift_one, gain_two, shift_two, bias_down, bias_up = [
        net.vector(v) for v in (ln1_gain, ln1_shift, ln2_gain, ln2_shift, down_bias, up_bias)
    ]
    embedded = chosen(noise_index, time_embed)
    scales = 1.0 + dot(embedded, lax.all_gather(w_time, "wide", axis=0, tiled=True))
    near_pieces, up_pieces, down_pieces = [
        net.pieces(w) for w in (jnp.concatenate([w_qkv, w_out], axis=1), w_up, w_down)
    ]
    act_one, qkv, attended, attended_turned = layer.attention(gain_one, shift_one, near_pieces)
    middle, act_two, act_two_turned = layer.middle(attended, scales, gain_two, shift_two, near_pieces)
    hidden, slope, *down_terms = layer.up(act_two, bias_up, up_pieces)
    output = layer.output(hidden, middle, bias_down, down_pieces)
    *up_terms, grad_up_bias, grad_middle, grad_branch, grad_scale, grad_gain_two, grad_shift_two = layer.feed_back(
        slope, act_two_turned, middle, scales, gain_two, shift_two, down_pieces, up_pieces
    )
    grad_projected = layer.attention_grad(grad_branch, qkv, near_pieces)
    grad_tokens, grad_gain_one, grad_shift_one = layer.token_grad(grad_projected, grad_middle, gain_one, near_pieces)

    def summed(theirs, send, keep):
        mine = jnp.stack([keep[0], send[0], keep[1], send[1]])
        return net.sum(jnp.concatenate([mine, theirs]).reshape(-1, theirs.shape[-1]))

    grads = (act_one, grad_projected, attended_turned, grad_branch)
    near = jnp.concatenate([summed(*layer.near_grad(*grads, half)) for half in range(2)], axis=1)
    width = tokens.shape[1]
    return (
        output,
        grad_tokens,
        net.sum(grad_gain_one[0]),
        net.sum(grad_shift_one[0]),
        near[:, : 3 * width],
        near[:, 3 * width :],
        net.sum(grad_gain_two[0]),
        net.sum(grad_shift_two[0]),
        net.sum(outer(embedded, grad_scale.astype(BF16))),
        summed(*up_terms),
        net.sum(grad_up_bias[0]),
        summed(*down_terms),
        net.sum(jnp.sum(cotangent.astype(F32), axis=0)),
    )


def plan_shards(plan, tokens, cotangent, noise_index, time_embed, ln1_gain, ln1_shift, w_qkv, w_out, ln2_gain,
                ln2_shift, w_time, w_up, up_bias, w_down, down_bias):
    seqs, per, width = noise_index.shape[0], ln1_gain.shape[0], tokens.shape[1]
    layer = Layer(tokens, cotangent, seqs, w_up.shape[1], *plan.enter())
    first, second, across = plan.first, plan.second, plan.across

    lines = [v.reshape(-1, per) for v in (ln1_gain, ln1_shift, ln2_gain, ln2_shift, down_bias, up_bias)]
    index_line = jnp.pad(noise_index.astype(BF16), (0, per - seqs))[None]
    lines = jnp.concatenate(lines + [index_line])
    lines = jnp.concatenate([lines, plan.move(lines, plan.x_pairs)])
    line_count = lines.shape[0]
    lines = jnp.pad(lines, ((0, w_qkv.shape[0] // 4 - line_count), (0, 0)))
    parts = plan.near_z(jnp.concatenate([plan.own_block(w_qkv), plan.own_block(w_out), lines], axis=1))
    own_up, own_down = plan.own_block(w_up), plan.own_block(w_down)

    *parts, own_up = tie(*parts, own_up)
    near_z = jnp.stack(parts)
    near_1, near_2 = first(near_z), second(near_z)
    up_z = plan.along_z(own_up)
    lines = jnp.stack([part[:line_count, -per:] for part in parts]).reshape(4, 2, -1, per)
    own_levels = lax.dynamic_slice_in_dim(time_embed, plan.wide * per, per, 1)
    index = lines[:, :, -1, :seqs].reshape(-1).astype(jnp.int32)
    partial = plan.sum_z(dot(chosen(index, own_levels), w_time).reshape(4, 2, seqs, width))
    vectors = plan.in_wide_order(lines)
    gain_one, shift_one, gain_two, shift_two, bias_down = [vectors[:, i].reshape(1, -1).astype(F32) for i in range(5)]
    bias_up = vectors[:, 5:-1].reshape(1, -1).astype(F32)

    near_1, near_2, own_down, partial, gain_one, shift_one = tie(near_1, near_2, own_down, partial, gain_one, shift_one)
    near_12, near_1c, near_2c, near_c = second(near_1), across(near_1), across(near_2), across(near_z)
    scales = 1.0 + plan.sum_x(partial)
    down_z = plan.along_z(own_down)

    near_12, near_1c, near_2c, near_c, up_z, scales = tie(near_12, near_1c, near_2c, near_c, up_z, scales)
    near_12c, up_1, up_2 = across(near_12), first(up_z), second(up_z)
    near_pieces = [near_z, near_1, near_2, near_12, near_c, near_1c, near_2c, near_12c]
    act_one, qkv, attended, attended_turned = layer.attention(gain_one, shift_one, near_pieces)

    attended, up_1, up_2 = tie(attended, up_1, up_2)
    up_12, up_c, up_1c, up_2c = second(up_1), across(up_z), across(up_1), across(up_2)
    middle, act_two, act_two_turned = layer.middle(attended, scales, gain_two, shift_two, near_pieces)

    act_two, up_12, up_2c, up_c, up_1c, down_z = tie(act_two, up_12, up_2c, up_c, up_1c, down_z)
    up_12c = across(up_12)
    down_1, down_2, down_c = first(down_z), second(down_z), across(down_z)
    up_pieces = [up_z, up_1, up_2, up_12, up_c, up_1c, up_2c, up_12c]
    hidden, slope, down_theirs, down_send, down_keep = layer.up(act_two, bias_up, up_pieces)

    hidden, slope, down_theirs, down_1, down_2, down_c = tie(hidden, slope, down_theirs, down_1, down_2, down_c)
    down_12, down_sent, down_1c, down_2c = second(down_1), across(down_theirs), across(down_1), across(down_2)

    down_sent, down_1c, down_2c = tie(down_sent, down_1c, down_2c)
    down_sum = sum_pieces(2, (down_send, 0, 1), (down_sent, 1, 2))

    down_sum, down_12, slope = tie(down_sum, down_12, slope)
    down_got, down_12c = first(down_sum), across(down_12)
    down_pieces = [down_z, down_1, down_2, down_12, down_c, down_1c, down_2c, down_12c]
    up_theirs, up_send, up_keep, grad_up_bias, grad_middle, grad_branch, grad_scale, grad_gain_two, grad_shift_two = (
        layer.feed_back(slope, act_two_turned, middle, scales, gain_two, shift_two, down_pieces, up_pieces)
    )

    up_theirs, grad_branch, down_got, grad_scale, cotangent = tie(
        up_theirs, grad_branch, down_got, grad_scale, cotangent
    )
    up_sent = across(up_theirs)
    down_fold = sum_pieces(1, (down_keep, 1, 1), (down_sent, 2, 1), (down_got, 1, 1))[0]
    sums = (grad_gain_two, grad_shift_two, jnp.sum(cotangent.astype(F32), axis=0), grad_up_bias)
    rows = [grad_scale, jnp.broadcast_to(noise_index[:, None], (seqs, 128)).astype(F32)]
    everyone = jnp.concatenate(rows + [v.reshape(seqs, -1) for v in sums], axis=1).astype(BF16)[None]

    up_sent, down_fold, everyone, grad_branch = tie(up_sent, down_fold, everyone, grad_branch)
    down_more = second(down_fold)
    up_fold = sum_pieces(2, (up_send, 0, 1), (up_sent, 1, 2))
    everyone = plan.near_z(everyone)

    up_fold, grad_branch = tie(up_fold, grad_branch)
    up_got = first(up_fold)
    grad_projected = layer.attention_grad(grad_branch, qkv, near_pieces)

    grad_projected, down_more, up_got, *everyone = tie(grad_projected, down_more, up_got, *everyone)
    everyone = jnp.concatenate(everyone)
    more = plan.move(everyone, plan.x_pairs)
    up_fold = sum_pieces(1, (up_keep, 1, 1), (up_sent, 2, 1), (up_got, 1, 1))[0]

    up_fold, grad_projected = tie(up_fold, grad_projected)
    up_more = second(up_fold)
    down_join = sum_pieces(1, (down_keep, 0, 1), (down_sent, 0, 1), (down_got, 0, 1), (down_more[None], 0, 1))[0]

    down_join, grad_projected = tie(down_join, grad_projected)
    grad_w_down = plan.over_z(down_join)
    grads = (act_one, grad_projected, attended_turned, grad_branch)
    low_theirs, low_send, low_keep = layer.near_grad(*grads, 0)

    low_theirs, grad_projected, grad_branch, more = tie(low_theirs, grad_projected, grad_branch, more)
    low_sent = across(low_theirs)
    everyone = jnp.concatenate([everyone, more])
    more = plan.move(everyone, plan.y_pairs)
    high_theirs, high_send, high_keep = layer.near_grad(act_one, grad_projected, attended_turned, grad_branch, 1)

    high_theirs, grad_projected, low_sent = tie(high_theirs, grad_projected, low_sent)
    high_sent = across(high_theirs)
    low_fold = sum_pieces(2, (low_send, 0, 1), (low_sent, 1, 2))

    low_fold, high_sent = tie(low_fold, high_sent)
    low_got = first(low_fold)
    high_fold = sum_pieces(2, (high_send, 0, 1), (high_sent, 1, 2))

    high_fold, up_more, grad_projected = tie(high_fold, up_more, grad_projected)
    high_got = first(high_fold)
    up_join = sum_pieces(1, (up_keep, 0, 1), (up_sent, 0, 1), (up_got, 0, 1), (up_more[None], 0, 1))[0]

    up_join, grad_projected = tie(up_join, grad_projected)
    grad_w_up = plan.over_z(up_join)
    grad_tokens, grad_gain_one, grad_shift_one = layer.token_grad(grad_projected, grad_middle, gain_one, near_pieces)

    grad_tokens, grad_gain_one, grad_shift_one, more, low_got, high_got, grad_w_down, hidden = tie(
        grad_tokens, grad_gain_one, grad_shift_one, more, low_got, high_got, grad_w_down, hidden
    )
    low_fold = sum_pieces(1, (low_keep, 1, 1), (low_sent, 2, 1), (low_got, 1, 1))[0]
    high_fold = sum_pieces(1, (high_keep, 1, 1), (high_sent, 2, 1), (high_got, 1, 1))[0]

    low_fold, high_fold, hidden = tie(low_fold, high_fold, hidden)
    low_more, high_more = second(low_fold), second(high_fold)
    grad_w_down = plan.over_group(grad_w_down)
    everyone = jnp.concatenate([everyone, more])
    more = across(everyone)
    ones = jnp.stack([grad_gain_one.reshape(8, per), grad_shift_one.reshape(8, per)], axis=1)
    ones_z = plan.near_z(ones)
    output = layer.output(hidden, middle, bias_down, down_pieces)

    output, low_more, high_more, grad_w_up, more, *ones_z = tie(output, low_more, high_more, grad_w_up, more, *ones_z)
    parts = plan.to_z(
        [low_keep[0], low_sent[0], low_got[0], low_more], [high_keep[0], high_sent[0], high_got[0], high_more]
    )
    grad_w_up = plan.over_group(grad_w_up)
    ones = sum(ones_z)
    ones = ones + across(ones)
    ones = ones + plan.move(ones, plan.x_pairs)
    ones = ones + plan.move(ones, plan.y_pairs)
    ones = lax.dynamic_index_in_dim(ones, plan.wide, 0, keepdims=False)
    everyone = jnp.concatenate([everyone, more])
    rest = everyone[..., width:].astype(F32)
    picked = chosen(rest[..., 0].reshape(-1).astype(jnp.int32), own_levels)
    grad_w_time = outer(picked, everyone[..., :width].reshape(-1, width))
    rest = jnp.sum(lax.dynamic_index_in_dim(rest, plan.wide, 1, keepdims=False)[:, 128:], axis=0)
    gain_sum, shift_sum, down_sum, up_sum = jnp.split(rest, (per, 2 * per, 3 * per))
    grad_w_down = grad_w_down.astype(F32)

    ones, grad_w_time, grad_w_down, grad_w_up, *parts = tie(ones, grad_w_time, grad_w_down, grad_w_up, *parts)
    near = plan.in_group(sum_of(*parts))
    grad_w_up = grad_w_up.astype(F32)

    near, grad_w_up = tie(near, grad_w_up)
    near = near.astype(F32)
    return (output, grad_tokens, ones[0], ones[1], near[:, : 3 * width], near[:, 3 * width :], gain_sum, shift_sum,
            grad_w_time, grad_w_up, up_sum, grad_w_down, down_sum)


def solution(mesh):
    fits = (mesh.shape["group"], mesh.shape["wide"]) == (4, 8)
    shards = functools.partial(plan_shards, Plan()) if fits else fallback_shards
    split, rows, line = P(BOTH, None), P("wide", None), P("wide")
    in_specs = (split, split, P(BOTH), P(), line, line, rows, rows, line, line, rows, rows, line, rows, line)
    out_specs = (split, split, line, line, rows, rows, line, line, rows, rows, line, rows, line)
    return jax.shard_map(shards, mesh=mesh, in_specs=in_specs, out_specs=out_specs, check_vma=False)
```

```python
import functools
import math

import jax
import jax.numpy as jnp
from jax import lax
from jax.experimental import pallas as pl
from jax.experimental.pallas import tpu as pltpu
from jax.sharding import PartitionSpec as P

HEAD_DIM = 64
EPSILON = 1e-05
BOTH = ("group", "wide")
F32 = jnp.float32
BF16 = jnp.bfloat16
BLOCKS = 32
VMEM_BYTES = 58 * 2**20


def sum_of(*terms):
    total = terms[0].astype(F32)
    for term in terms[1:]:
        total = total + term.astype(F32)
    return total.astype(BF16)


def tie(*values):
    return lax.optimization_barrier(values)


def dot(a, b):
    return jnp.dot(a, b, preferred_element_type=F32)


def dot_nt(a, b):
    return lax.dot_general(a, b, (((1,), (1,)), ((), ())), preferred_element_type=F32)


def dot_tn(a, b):
    return lax.dot_general(a, b, (((0,), (0,)), ((), ())), preferred_element_type=F32)


class Plan:
    def __init__(self):
        def pairs(target):
            found = []
            for index in range(32):
                group, wide = divmod(index, 8)
                y, core, z, x = target(group // 2, group % 2, wide // 2, wide % 2)
                found.append((index, (y * 2 + core) * 8 + z * 2 + x))
            return found

        self.core_pairs = pairs(lambda y, c, z, x: (y, 1 - c, z, x))
        self.y_pairs = pairs(lambda y, c, z, x: (1 - y, c, z, x))
        self.x_pairs = pairs(lambda y, c, z, x: (y, c, z, 1 - x))
        self.first_pairs = pairs(lambda y, c, z, x: (y, c, z, 1 - x) if c == 0 else (1 - y, c, z, x))
        self.second_pairs = pairs(lambda y, c, z, x: (1 - y, c, z, x) if c == 0 else (y, c, z, 1 - x))
        self.z_groups = [[(y * 2 + c) * 8 + z * 2 + x for z in range(4)] for y in (0, 1) for c in (0, 1) for x in (0, 1)]
        self.z_pairs = [pairs(lambda y, c, z, x, step=step: (y, c, (z - step) % 4, x)) for step in range(4)]

    def enter(self):
        self.group = lax.axis_index("group")
        self.wide = lax.axis_index("wide")
        y, core = self.group // 2, self.group % 2
        z, x = self.wide // 2, self.wide % 2
        self.z, self.x, self.y, self.core = z, x, y, core
        slot = jnp.arange(BLOCKS, dtype=jnp.int32)
        holder = core ^ (slot // 16)
        second, first, step = (slot // 8) % 2, (slot // 4) % 2, slot % 4
        across = jnp.where(holder == 0, first, second)
        along = jnp.where(holder == 0, second, first)
        spot = (x ^ across) * 4 + (y ^ along) * 2 + holder
        places, near_places = step * 8 + spot, ((z + step) % 4) * 8 + spot
        block_z, block_x, block_y, block_core = slot // 8, (slot // 4) % 2, (slot // 2) % 2, slot % 2
        off_x, off_y = block_x ^ x, block_y ^ y
        first = jnp.where(block_core == 0, off_x, off_y)
        second = jnp.where(block_core == 0, off_y, off_x)
        spot = (((block_core ^ core) * 2 + second) * 2 + first) * 4
        tables = places, near_places, spot + block_z, spot + (block_z - z) % 4
        return [table.astype(jnp.int32) for table in tables]

    def move(self, value, pairs):
        return lax.ppermute(value, BOTH, pairs)

    def own_block(self, shard):
        rows = shard.shape[0] // 4
        return lax.dynamic_slice_in_dim(shard, self.group * rows, rows, 0)

    def along_z(self, own):
        return lax.all_gather(own, BOTH, axis_index_groups=self.z_groups, axis=0)

    def near_z(self, own):
        return [own] + [self.move(own, self.z_pairs[step]) for step in (1, 2, 3)]

    def first(self, value):
        return self.move(value, self.first_pairs)

    def second(self, value):
        return self.move(value, self.second_pairs)

    def across(self, value):
        return self.move(value, self.core_pairs)

    def over_z(self, part):
        return lax.psum_scatter(part, BOTH, axis_index_groups=self.z_groups, scatter_dimension=0)

    def over_group(self, own):
        return lax.all_gather(own, "group", axis=0, tiled=True)

    def to_z(self, *weights):
        def part(step):
            return jnp.concatenate([sum_of(*[term[step] for term in terms]) for terms in weights], axis=1)

        return [part(0)] + [self.move(part(step), self.z_pairs[4 - step]) for step in (1, 2, 3)]

    def in_group(self, own):
        along = self.move(own, self.y_pairs)
        parts = [own, self.across(own), along, self.across(along)]
        parts = [jnp.where(self.core == 0, parts[i], parts[i ^ 1]) for i in range(4)]
        return jnp.concatenate([jnp.where(self.y == 0, parts[i], parts[i ^ 2]) for i in range(4)])

    def in_wide_order(self, near):
        near = jnp.where(self.x == 0, near, near[:, ::-1])
        near = lax.dynamic_slice_in_dim(jnp.concatenate([near, near]), (4 - self.z) % 4, 4, 0)
        return near.reshape((8,) + near.shape[2:])

    def sum_x(self, pair):
        return pair[0] + self.move(pair[1], self.x_pairs)

    def sum_z(self, near):
        total = near[0]
        for step in (1, 2, 3):
            total = total + self.move(near[step], self.z_pairs[4 - step])
        return total


def rotary_tables(length):
    half = HEAD_DIM // 2
    frequency = jnp.exp(jnp.arange(half, dtype=F32) * (-2.0 * math.log(10000.0) / HEAD_DIM))
    angles = jnp.arange(length, dtype=F32)[:, None] * frequency[None, :]
    sine = jnp.sin(angles)
    cosine = jnp.concatenate([jnp.cos(angles)] * 4, axis=1)
    return cosine, jnp.concatenate([-sine, sine, -sine, sine], axis=1)


def call(kernel, name, tables, grid, ins, outs, scratch=(), flops=0, moved=0):
    def spec(block, index, buffers=None):
        if buffers:
            return pl.BlockSpec(block, index, pipeline_mode=pl.Buffered(buffers))
        return pl.BlockSpec(block, index)

    return pl.pallas_call(
        kernel,
        out_shape=[jax.ShapeDtypeStruct(shape, dtype) for shape, dtype, *_ in outs],
        grid_spec=pltpu.PrefetchScalarGridSpec(
            num_scalar_prefetch=len(tables),
            grid=grid,
            in_specs=[spec(*rest) for _, *rest in ins],
            out_specs=[spec(*rest) for _, _, *rest in outs],
            scratch_shapes=list(scratch),
        ),
        compiler_params=pltpu.CompilerParams(vmem_limit_bytes=VMEM_BYTES),
        cost_estimate=pl.CostEstimate(flops=0, bytes_accessed=0, transcendentals=0),
        name=name,
    )(*tables, *[array for array, *_ in ins])


def whole(array, buffers=1):
    rank = array.ndim
    return (array, array.shape, lambda i, *_: (0,) * rank, buffers)


def columns_at(array, first, count):
    return (array, array.shape[:-1] + (count,), lambda i, *_: (0,) * (array.ndim - 1) + (first // count,), 1)


def rows_of(array, tile):
    return (array, (tile, array.shape[1]), lambda i, *_: (i, 0))


def out_rows(shape, dtype, tile):
    return (shape, dtype, (tile, shape[1]), lambda i, *_: (i, 0))


def out_whole(shape, dtype):
    return (shape, dtype, shape, lambda i, *_: (0,) * len(shape), 1)


def put_in_order(places, pieces, held):
    for i in range(BLOCKS):
        held[places[i]] = pieces[i // 4][i % 4]


def matrix(held):
    blocks, rows, columns = held.shape
    return held[...].reshape(blocks * rows, columns)


def normalise(values):
    average = jnp.mean(values, axis=-1, keepdims=True)
    centered = values - average
    scale = lax.rsqrt(jnp.mean(centered * centered, axis=-1, keepdims=True) + EPSILON)
    return centered * scale, scale


def norm_back(grad, hat, scale, gain):
    e = grad * gain
    inner = jnp.mean(e * hat, axis=-1, keepdims=True)
    return scale * (e - jnp.mean(e, axis=-1, keepdims=True) - hat * inner)


def turned(values):
    lane = lax.broadcasted_iota(jnp.int32, values.shape, 1)
    return jnp.where(lane % 64 < 32, pltpu.roll(values, 96, 1), pltpu.roll(values, 32, 1))


def heads(values):
    lane = lax.broadcasted_iota(jnp.int32, values.shape, 1)
    zero = jnp.zeros_like(values)
    return jnp.concatenate([jnp.where(lane < 64, values, zero), jnp.where(lane < 64, zero, values)], axis=0)


def put_turned(out, slots, values):
    rows = out.shape[1]
    flipped = values.T
    for j in range(BLOCKS):
        out[slots[j]] = flipped[j * rows : (j + 1) * rows]


def attention_kernel(length, places, slots, tokens, gain, shift, cosine, sine, *refs):
    pieces, (act_turned, qkv, attended, attended_turned), held = refs[:8], refs[8:12], refs[12]
    rows, width = tokens.shape

    @pl.when(pl.program_id(0) == 0)
    def _():
        put_in_order(places, pieces, held)

    hat, _ = normalise(tokens[...].astype(F32))
    act = (hat * gain[...] + shift[...]).astype(BF16)
    put_turned(act_turned, slots, act)
    cos, sin = cosine[...], sine[...]
    for start in range(0, 3 * width, 512):
        part = dot(act, held[:, :, start : start + 512].reshape(width, 512))
        if start < 2 * width:
            for lanes in range(0, 512, 128):
                piece = part[:, lanes : lanes + 128]
                qkv[:, start + lanes : start + lanes + 128] = (piece * cos + turned(piece) * sin).astype(BF16)
        else:
            qkv[:, start : start + 512] = part.astype(BF16)
    group = 1024
    factor = HEAD_DIM ** (-0.5)
    for top in range(0, rows, length):
        at = slice(top, top + length)
        for first in range(0, width, group):
            starts = range(first, first + group, 128)
            queries = [heads(qkv[at, lanes : lanes + 128]) for lanes in starts]
            scores = [
                dot_nt(qkv[at, width + lanes : width + lanes + 128], q) for lanes, q in zip(starts, queries, strict=True)
            ]
            probs = []
            for score in scores:
                e = jnp.exp(factor * (score - jnp.max(score, axis=0, keepdims=True)))
                probs.append((e * (1.0 / jnp.sum(e, axis=0, keepdims=True))).astype(BF16))
            probs = [jnp.concatenate([p[:, :length].T, p[:, length:].T], axis=1) for p in probs]
            for lanes, p in zip(starts, probs, strict=True):
                v = heads(qkv[at, 2 * width + lanes : 2 * width + lanes + 128])
                attended[at, lanes : lanes + 128] = dot(p, v).astype(BF16)
    put_turned(attended_turned, slots, attended[...])


def middle_kernel(length, places, near_slots, slots, tokens, attended, scales, gain, shift, *refs):
    pieces, (middle, act, act_turned), held = refs[:8], refs[8:11], refs[11]
    rows = tokens.shape[0]

    @pl.when(pl.program_id(0) == 0)
    def _():
        put_in_order(places, pieces, held)

    values = tokens[...].astype(F32) + dot(attended[...], matrix(held))
    middle[...] = values
    hat, _ = normalise(values)
    normed = hat * gain[...] + shift[...]
    first = pl.program_id(0) * (rows // length)
    for s in range(rows // length):
        act[s * length : (s + 1) * length, :] = (
            normed[s * length : (s + 1) * length, :] * scales[pl.ds(first + s, 1), :]
        ).astype(BF16)
    put_turned(act_turned, slots, act[...])


def split_out(slot, block, theirs, send, keep):
    piece, at = slot // 4, slot % 4

    @pl.when(slot >= BLOCKS // 2)
    def _():
        theirs[piece - 4, at] = block

    @pl.when((slot < BLOCKS // 2) & (piece % 2 == 1))
    def _():
        send[piece // 2, at] = block

    @pl.when((slot < BLOCKS // 2) & (piece % 2 == 0))
    def _():
        keep[piece // 2, at] = block


def up_kernel(places, slots, act, bias, cotangent, *refs):
    pieces, (hidden, slope, theirs, send, keep), held = refs[:8], refs[8:13], refs[13]
    put_in_order(places, pieces, held)
    v = dot(act[...], matrix(held)) + bias[...]
    area = 0.5 + 0.5 * lax.erf(v * math.sqrt(0.5))
    low = (v * area).astype(BF16)
    hidden[...] = low
    slope[...] = (area + v * jnp.exp(-0.5 * v * v) * (1.0 / math.sqrt(2.0 * math.pi))).astype(BF16)
    grad = dot_tn(low, cotangent[...]).astype(BF16)
    rows = theirs.shape[2]
    count = hidden.shape[1] // rows
    for k in range(count):
        split_out(slots[pl.program_id(0) * count + k], grad[k * rows : (k + 1) * rows], theirs, send, keep)


def near_grad_kernel(strips, act_one, grad_projected, attended, grad_branch, theirs, send, keep):
    blocks, rows = act_one.shape[:2]

    @pl.when(pl.program_id(0) < strips)
    def _():
        put_apart(dot(act_one[...].reshape(blocks * rows, -1), grad_projected[...]), rows, theirs, send, keep)

    @pl.when(pl.program_id(0) >= strips)
    def _():
        put_apart(dot(attended[...].reshape(blocks * rows, -1), grad_branch[...]), rows, theirs, send, keep)


def put_apart(total, rows, theirs, send, keep):
    total = total.astype(BF16).reshape(8, 4, rows, -1)
    theirs[...] = total[4:]
    for second in range(2):
        keep[second] = total[2 * second]
        send[second] = total[2 * second + 1]


def feed_back_kernel(length, places, cotangent, slope, turned_act, middle, scales, gain, shift, *refs):
    down, up = refs[:8], refs[8:16]
    theirs, send, keep, bias, grad_middle, grad_branch, grad_scale, gain_sum, shift_sum = refs[16:25]
    held_down, held_up, total = refs[25:]
    step = pl.program_id(0)

    @pl.when(step == 0)
    def _():
        put_in_order(places, down, held_down)
        total[...] = jnp.zeros_like(total)

    put_in_order(places, up, held_up)
    strip = slope.shape[1]
    count = strip // held_down.shape[1]
    rows = held_down[pl.ds(step * count, count)].reshape(strip, -1)
    grad = (dot_nt(cotangent[...], rows) * slope[...].astype(F32)).astype(BF16)
    bias[...] = jnp.sum(grad.astype(F32), axis=0, keepdims=True)
    blocks, deep = turned_act.shape[:2]
    put_apart(dot(turned_act[...].reshape(blocks * deep, -1), grad), deep, theirs, send, keep)
    total[...] += dot_nt(grad, matrix(held_up))

    @pl.when(step == pl.num_programs(0) - 1)
    def _():
        gains, shifts = jnp.zeros_like(gain_sum), jnp.zeros_like(shift_sum)
        for s in range(middle.shape[0] // length):
            at = slice(s * length, (s + 1) * length)
            own = total[at, :]
            hat, scale = normalise(middle[at, :])
            normed = hat * gain[...] + shift[...]
            grad_scale[s : s + 1, :] = jnp.sum(own * normed, axis=0, keepdims=True)
            grad = own * scales[s : s + 1, :]
            gains += jnp.sum(grad * hat, axis=0, keepdims=True)
            shifts += jnp.sum(grad, axis=0, keepdims=True)
            out = cotangent[at, :].astype(F32) + norm_back(grad, hat, scale, gain[...])
            grad_middle[at, :] = out
            grad_branch[at, :] = out.astype(BF16)
        gain_sum[...] = gains
        shift_sum[...] = shifts


def sum_kernel(*refs):
    total = refs[0][...].astype(F32)
    for ref in refs[1:-1]:
        total = total + ref[...].astype(F32)
    refs[-1][...] = total.astype(BF16)


def sum_pieces(count, *terms):
    _, _, rows, columns = terms[0][0].shape
    block = (1, 2, rows, columns)
    ins = [
        (array, block, lambda i, first=first, stride=stride: (first + stride * (i // 2), i % 2, 0, 0))
        for array, first, stride in terms
    ]
    out = ((count, 4, rows, columns), BF16, block, lambda i: (i // 2, i % 2, 0, 0))
    size = count * 4 * rows * columns
    return call(sum_kernel, "sum_pieces", (), (2 * count,), ins, [out], flops=size, moved=2 * size * (len(terms) + 1))[0]


def output_kernel(places, hidden, middle, bias, *refs):
    pieces, output, held = refs[:8], refs[8], refs[9]

    @pl.when(pl.program_id(0) == 0)
    def _():
        put_in_order(places, pieces, held)

    output[...] = (middle[...] + dot(hidden[...], matrix(held)) + bias[...]).astype(BF16)


def attention_grad_kernel(length, places, grad_branch, qkv, cosine, sine, *refs):
    pieces, grad_projected, held, grad_attended = refs[:8], refs[8], refs[9], refs[10]
    rows, width = grad_branch.shape
    factor = HEAD_DIM ** (-0.5)

    @pl.when(pl.program_id(0) == 0)
    def _():
        put_in_order(places, pieces, held)

    grad_attended[...] = dot_nt(grad_branch[...], matrix(held)).astype(BF16)
    cos, sin = cosine[...], sine[...]
    group = 512
    for top in range(0, rows, length):
        at = slice(top, top + length)
        for first in range(0, width, group):
            starts = range(first, first + group, 128)
            q = [heads(qkv[at, lanes : lanes + 128]) for lanes in starts]
            k = [qkv[at, width + lanes : width + lanes + 128] for lanes in starts]
            g = [heads(grad_attended[at, lanes : lanes + 128]) for lanes in starts]
            scores = [dot_nt(a, b) for a, b in zip(k, q, strict=True)]
            grad_probs = [
                dot_nt(qkv[at, 2 * width + lanes : 2 * width + lanes + 128], b) for lanes, b in zip(starts, g, strict=True)
            ]
            probs = []
            for score in scores:
                e = jnp.exp(factor * (score - jnp.max(score, axis=0, keepdims=True)))
                probs.append(e * (1.0 / jnp.sum(e, axis=0, keepdims=True)))
            grad_values = [dot(p.astype(BF16), b) for p, b in zip(probs, g, strict=True)]
            grad_scores = []
            for p, gp in zip(probs, grad_probs, strict=True):
                inner = jnp.sum(gp * p, axis=0, keepdims=True)
                grad_scores.append((p * (gp - inner)).astype(BF16))
            grad_keys = [dot(gs, b) * factor for gs, b in zip(grad_scores, q, strict=True)]
            flipped = [jnp.concatenate([gs[:, :length].T, gs[:, length:].T], axis=1) for gs in grad_scores]
            grad_queries = [dot(f, heads(b)) * factor for f, b in zip(flipped, k, strict=True)]
            for n, lanes in enumerate(starts):
                for start, grad in ((lanes, grad_queries[n]), (width + lanes, grad_keys[n])):
                    grad_projected[at, start : start + 128] = (grad * cos[at] - turned(grad) * sin[at]).astype(BF16)
                grad_projected[at, 2 * width + lanes : 2 * width + lanes + 128] = grad_values[n].astype(BF16)


def token_grad_kernel(places, grad_projected, tokens, grad_middle, gain, *refs):
    pieces, (grad_tokens, gain_sum, shift_sum), held = refs[:8], refs[8:11], refs[11]

    @pl.when(pl.program_id(0) == 0)
    def _():
        put_in_order(places, pieces, held)
        gain_sum[...] = jnp.zeros_like(gain_sum)
        shift_sum[...] = jnp.zeros_like(shift_sum)

    grad = dot_nt(grad_projected[...], matrix(held))
    hat, scale = normalise(tokens[...].astype(F32))
    gain_sum[...] += jnp.sum(grad * hat, axis=0, keepdims=True)
    shift_sum[...] += jnp.sum(grad, axis=0, keepdims=True)
    grad_tokens[...] = grad_middle[...] + norm_back(grad, hat, scale, gain[...])


class Fallback:
    def vector(self, shard):
        return lax.all_gather(shard, "wide", axis=0, tiled=True).astype(F32)[None]

    def pieces(self, shard):
        full = lax.all_gather(shard, "wide", axis=0, tiled=True)
        return list(full.reshape(8, 4, full.shape[0] // BLOCKS, full.shape[1]))

    def sum(self, grad):
        grad = lax.psum_scatter(grad, "wide", scatter_dimension=0, tiled=True)
        return lax.psum(grad, "group").astype(F32)


class Layer:
    def __init__(self, tokens, cotangent, seqs, ff, places, near_places, slots, near_slots):
        self.tokens, self.cotangent = tokens, cotangent
        self.places, self.near_places, self.slots, self.near_slots = places, near_places, slots, near_slots
        self.rows, self.width = tokens.shape
        self.seqs, self.ff = seqs, ff
        self.length = self.rows // seqs
        self.tile = 2 * self.length
        self.steps = self.rows // self.tile
        self.strip = 512
        self.deep = self.width // BLOCKS
        cosine, sine = rotary_tables(self.length)
        self.tables = [jnp.tile(t, (self.tile // self.length, 1)) for t in (cosine, sine)]

    def held(self, pieces):
        return pltpu.VMEM((BLOCKS,) + pieces[0].shape[1:], BF16)

    def qkv_part(self, pieces):
        return [columns_at(p, 0, 3 * self.width) for p in pieces]

    def out_part(self, pieces):
        return [columns_at(p, 3 * self.width, self.width) for p in pieces]

    def held_part(self, columns):
        return pltpu.VMEM((BLOCKS, self.deep, columns), BF16)

    def turned_out(self):
        return ((BLOCKS, self.deep, self.rows), BF16, (BLOCKS, self.deep, self.tile), lambda i, *_: (0, 0, i))

    def by_rows(self, array):
        return rows_of(array, self.tile)

    def rows_out(self, columns, dtype):
        return out_rows((self.rows, columns), dtype, self.tile)

    def by_columns(self, array):
        return (array, array.shape[:-1] + (self.strip,), lambda i, *_: (0,) * (array.ndim - 1) + (i,))

    def columns_out(self, shape, dtype):
        return (shape, dtype, shape[:-1] + (self.strip,), lambda i, *_: (0,) * (len(shape) - 1) + (i,))

    def attention(self, gain, shift, pieces):
        rows, width = self.rows, self.width
        return call(
            functools.partial(attention_kernel, self.length), "attention", (self.near_places, self.near_slots), (self.steps,),
            [self.by_rows(self.tokens), whole(gain), whole(shift)] + [whole(t) for t in self.tables]
            + self.qkv_part(pieces),
            [self.turned_out(), self.rows_out(3 * width, BF16), self.rows_out(width, BF16), self.turned_out()],
            [self.held_part(3 * width)], flops=12 * rows * width * width, moved=20 * rows * width,
        )

    def middle(self, attended, scales, gain, shift, pieces):
        rows, width = self.rows, self.width
        return call(
            functools.partial(middle_kernel, self.length), "middle", (self.near_places, self.near_slots, self.slots), (self.steps,),
            [self.by_rows(self.tokens), self.by_rows(attended), whole(scales), whole(gain), whole(shift)]
            + self.out_part(pieces),
            [self.rows_out(width, F32), self.rows_out(width, BF16), self.turned_out()],
            [self.held_part(width)], flops=4 * rows * width * width, moved=14 * rows * width,
        )

    def up(self, act, bias, pieces):
        rows, width, ff = self.rows, self.width, self.ff
        fr = ff // BLOCKS
        return call(
            up_kernel, "up", (self.places, self.slots), (ff // self.strip,),
            [whole(act), self.by_columns(bias), whole(self.cotangent)] + [self.by_columns(p) for p in pieces],
            [self.columns_out((rows, ff), BF16)] * 2 + [out_whole((n, 4, fr, width), BF16) for n in (4, 2, 2)],
            [pltpu.VMEM((BLOCKS, self.deep, self.strip), BF16)],
            flops=4 * rows * width * ff, moved=8 * rows * ff,
        )

    def near_grad(self, act_one, grad_projected, attended, grad_branch, half):
        columns, strip = 2 * self.width, self.strip
        strips = 3 * self.width // strip
        at = half * columns // strip
        ins = [
            whole(act_one),
            (grad_projected, (self.rows, strip), lambda i: (0, jnp.minimum(i + at, strips - 1))),
            whole(attended),
            (grad_branch, (self.rows, strip), lambda i: (0, jnp.maximum(i + at - strips, 0))),
        ]
        return call(
            functools.partial(near_grad_kernel, strips - at), "near_grad", (), (columns // strip,), ins,
            [self.columns_out((n, 4, self.deep, columns), BF16) for n in (4, 2, 2)],
            flops=2 * self.rows * self.width * columns, moved=4 * self.rows * columns,
        )

    def feed_back(self, slope, act, middle, scales, gain, shift, down, up):
        rows, width, ff = self.rows, self.width, self.ff
        return call(
            functools.partial(feed_back_kernel, self.length), "feed_back", (self.places,), (ff // self.strip,),
            [whole(self.cotangent), self.by_columns(slope)] + [whole(v) for v in (act, middle, scales, gain, shift)]
            + [whole(p) for p in down] + [self.by_columns(p) for p in up],
            [self.columns_out((n, 4, self.deep, ff), BF16) for n in (4, 2, 2)]
            + [self.columns_out((1, ff), F32), out_whole((rows, width), F32), out_whole((rows, width), BF16)]
            + [out_whole((self.seqs, width), F32)] + [out_whole((1, width), F32)] * 2,
            [self.held(down), pltpu.VMEM((BLOCKS, self.deep, self.strip), BF16), pltpu.VMEM((rows, width), F32)],
            flops=6 * rows * width * ff, moved=10 * rows * ff,
        )

    def output(self, hidden, middle, bias, pieces):
        rows, width = self.rows, self.width
        return call(
            output_kernel, "output", (self.places,), (self.steps,),
            [self.by_rows(hidden), self.by_rows(middle), whole(bias)] + [whole(p) for p in pieces],
            [self.rows_out(width, BF16)],
            [self.held(pieces)], flops=2 * rows * width * self.ff, moved=22 * rows * width,
        )[0]

    def attention_grad(self, grad_branch, qkv, pieces):
        rows, width = self.rows, self.width
        return call(
            functools.partial(attention_grad_kernel, self.length), "attention_grad", (self.near_places,), (self.steps,),
            [self.by_rows(grad_branch), self.by_rows(qkv)] + [whole(t) for t in self.tables] + self.out_part(pieces),
            [self.rows_out(3 * width, BF16)],
            [self.held_part(width), pltpu.VMEM((self.tile, width), BF16)],
            flops=12 * rows * width * width, moved=16 * rows * width,
        )[0]

    def token_grad(self, grad_projected, grad_middle, gain, pieces):
        rows, width = self.rows, self.width
        return call(
            token_grad_kernel, "token_grad", (self.near_places,), (self.steps,),
            [self.by_rows(grad_projected), self.by_rows(self.tokens), self.by_rows(grad_middle), whole(gain)]
            + self.qkv_part(pieces),
            [self.rows_out(width, F32)] + [out_whole((1, width), F32)] * 2,
            [self.held_part(3 * width)], flops=6 * rows * width * width, moved=22 * rows * width,
        )


def chosen(index, table):
    levels = jnp.arange(table.shape[0], dtype=jnp.int32)
    return dot((index[:, None] == levels[None, :]).astype(BF16), table).astype(BF16)


def outer(a, b):
    return lax.dot_general(a, b, (((0,), (0,)), ((), ())), preferred_element_type=F32)


def fallback_shards(tokens, cotangent, noise_index, time_embed, ln1_gain, ln1_shift, w_qkv, w_out, ln2_gain, ln2_shift,
                    w_time, w_up, up_bias, w_down, down_bias):
    net = Fallback()
    order = jnp.arange(BLOCKS, dtype=jnp.int32)
    layer = Layer(tokens, cotangent, noise_index.shape[0], w_up.shape[1], order, order, order, order)
    gain_one, shift_one, gain_two, shift_two, bias_down, bias_up = [
        net.vector(v) for v in (ln1_gain, ln1_shift, ln2_gain, ln2_shift, down_bias, up_bias)
    ]
    embedded = chosen(noise_index, time_embed)
    scales = 1.0 + dot(embedded, lax.all_gather(w_time, "wide", axis=0, tiled=True))
    near_pieces, up_pieces, down_pieces = [
        net.pieces(w) for w in (jnp.concatenate([w_qkv, w_out], axis=1), w_up, w_down)
    ]
    act_one, qkv, attended, attended_turned = layer.attention(gain_one, shift_one, near_pieces)
    middle, act_two, act_two_turned = layer.middle(attended, scales, gain_two, shift_two, near_pieces)
    hidden, slope, *down_terms = layer.up(act_two, bias_up, up_pieces)
    output = layer.output(hidden, middle, bias_down, down_pieces)
    *up_terms, grad_up_bias, grad_middle, grad_branch, grad_scale, grad_gain_two, grad_shift_two = layer.feed_back(
        slope, act_two_turned, middle, scales, gain_two, shift_two, down_pieces, up_pieces
    )
    grad_projected = layer.attention_grad(grad_branch, qkv, near_pieces)
    grad_tokens, grad_gain_one, grad_shift_one = layer.token_grad(grad_projected, grad_middle, gain_one, near_pieces)

    def summed(theirs, send, keep):
        mine = jnp.stack([keep[0], send[0], keep[1], send[1]])
        return net.sum(jnp.concatenate([mine, theirs]).reshape(-1, theirs.shape[-1]))

    grads = (act_one, grad_projected, attended_turned, grad_branch)
    near = jnp.concatenate([summed(*layer.near_grad(*grads, half)) for half in range(2)], axis=1)
    width = tokens.shape[1]
    return (
        output,
        grad_tokens,
        net.sum(grad_gain_one[0]),
        net.sum(grad_shift_one[0]),
        near[:, : 3 * width],
        near[:, 3 * width :],
        net.sum(grad_gain_two[0]),
        net.sum(grad_shift_two[0]),
        net.sum(outer(embedded, grad_scale.astype(BF16))),
        summed(*up_terms),
        net.sum(grad_up_bias[0]),
        summed(*down_terms),
        net.sum(jnp.sum(cotangent.astype(F32), axis=0)),
    )


def plan_shards(plan, tokens, cotangent, noise_index, time_embed, ln1_gain, ln1_shift, w_qkv, w_out, ln2_gain,
                ln2_shift, w_time, w_up, up_bias, w_down, down_bias):
    seqs, per, width = noise_index.shape[0], ln1_gain.shape[0], tokens.shape[1]
    layer = Layer(tokens, cotangent, seqs, w_up.shape[1], *plan.enter())
    first, second, across = plan.first, plan.second, plan.across

    lines = [v.reshape(-1, per) for v in (ln1_gain, ln1_shift, ln2_gain, ln2_shift, down_bias, up_bias)]
    index_line = jnp.pad(noise_index.astype(BF16), (0, per - seqs))[None]
    lines = jnp.concatenate(lines + [index_line])
    lines = jnp.concatenate([lines, plan.move(lines, plan.x_pairs)])
    line_count = lines.shape[0]
    lines = jnp.pad(lines, ((0, w_qkv.shape[0] // 4 - line_count), (0, 0)))
    parts = plan.near_z(jnp.concatenate([plan.own_block(w_qkv), plan.own_block(w_out), lines], axis=1))
    own_up, own_down = plan.own_block(w_up), plan.own_block(w_down)

    *parts, own_up = tie(*parts, own_up)
    near_z = jnp.stack(parts)
    near_1, near_2 = first(near_z), second(near_z)
    up_z = plan.along_z(own_up)
    lines = jnp.stack([part[:line_count, -per:] for part in parts]).reshape(4, 2, -1, per)
    own_levels = lax.dynamic_slice_in_dim(time_embed, plan.wide * per, per, 1)
    index = lines[:, :, -1, :seqs].reshape(-1).astype(jnp.int32)
    partial = plan.sum_z(dot(chosen(index, own_levels), w_time).reshape(4, 2, seqs, width))
    vectors = plan.in_wide_order(lines)
    gain_one, shift_one, gain_two, shift_two, bias_down = [vectors[:, i].reshape(1, -1).astype(F32) for i in range(5)]
    bias_up = vectors[:, 5:-1].reshape(1, -1).astype(F32)

    near_1, near_2, own_down, partial, gain_one, shift_one = tie(near_1, near_2, own_down, partial, gain_one, shift_one)
    near_12, near_1c, near_2c, near_c = second(near_1), across(near_1), across(near_2), across(near_z)
    scales = 1.0 + plan.sum_x(partial)
    down_z = plan.along_z(own_down)

    near_12, near_1c, near_2c, near_c, up_z, scales = tie(near_12, near_1c, near_2c, near_c, up_z, scales)
    near_12c, up_1, up_2 = across(near_12), first(up_z), second(up_z)
    near_pieces = [near_z, near_1, near_2, near_12, near_c, near_1c, near_2c, near_12c]
    act_one, qkv, attended, attended_turned = layer.attention(gain_one, shift_one, near_pieces)

    attended, up_1, up_2 = tie(attended, up_1, up_2)
    up_12, up_c, up_1c, up_2c = second(up_1), across(up_z), across(up_1), across(up_2)
    middle, act_two, act_two_turned = layer.middle(attended, scales, gain_two, shift_two, near_pieces)

    act_two, up_12, up_2c, up_c, up_1c, down_z = tie(act_two, up_12, up_2c, up_c, up_1c, down_z)
    up_12c = across(up_12)
    down_1, down_2, down_c = first(down_z), second(down_z), across(down_z)
    up_pieces = [up_z, up_1, up_2, up_12, up_c, up_1c, up_2c, up_12c]
    hidden, slope, down_theirs, down_send, down_keep = layer.up(act_two, bias_up, up_pieces)

    hidden, slope, down_theirs, down_1, down_2, down_c = tie(hidden, slope, down_theirs, down_1, down_2, down_c)
    down_12, down_sent, down_1c, down_2c = second(down_1), across(down_theirs), across(down_1), across(down_2)

    down_sent, down_1c, down_2c = tie(down_sent, down_1c, down_2c)
    down_sum = sum_pieces(2, (down_send, 0, 1), (down_sent, 1, 2))

    down_sum, down_12, slope = tie(down_sum, down_12, slope)
    down_got, down_12c = first(down_sum), across(down_12)
    down_pieces = [down_z, down_1, down_2, down_12, down_c, down_1c, down_2c, down_12c]
    up_theirs, up_send, up_keep, grad_up_bias, grad_middle, grad_branch, grad_scale, grad_gain_two, grad_shift_two = (
        layer.feed_back(slope, act_two_turned, middle, scales, gain_two, shift_two, down_pieces, up_pieces)
    )

    up_theirs, grad_branch, down_got = tie(up_theirs, grad_branch, down_got)
    up_sent = across(up_theirs)
    down_fold = sum_pieces(1, (down_keep, 1, 1), (down_sent, 2, 1), (down_got, 1, 1))[0]

    up_sent, down_fold, grad_branch = tie(up_sent, down_fold, grad_branch)
    up_fold = sum_pieces(2, (up_send, 0, 1), (up_sent, 1, 2))

    up_fold, grad_branch = tie(up_fold, grad_branch)
    up_got = first(up_fold)
    grad_projected = layer.attention_grad(grad_branch, qkv, near_pieces)

    grad_projected, grad_scale, cotangent, down_fold = tie(grad_projected, grad_scale, cotangent, down_fold)
    down_more = second(down_fold)
    low_theirs, low_send, low_keep = layer.near_grad(act_one, grad_projected, attended_turned, grad_branch, 0)

    low_theirs, grad_projected, grad_branch, up_got, grad_scale = tie(
        low_theirs, grad_projected, grad_branch, up_got, grad_scale
    )
    low_sent = across(low_theirs)
    sums = (grad_gain_two, grad_shift_two, jnp.sum(cotangent.astype(F32), axis=0), grad_up_bias)
    rows = [grad_scale, jnp.broadcast_to(noise_index[:, None], (seqs, 128)).astype(F32)]
    everyone = jnp.concatenate(rows + [v.reshape(seqs, -1) for v in sums], axis=1).astype(BF16)[None]
    up_fold = sum_pieces(1, (up_keep, 1, 1), (up_sent, 2, 1), (up_got, 1, 1))[0]

    up_fold, everyone, grad_projected, grad_branch, down_more = tie(
        up_fold, everyone, grad_projected, grad_branch, down_more
    )
    up_more = second(up_fold)
    everyone = plan.near_z(everyone)
    down_join = sum_pieces(1, (down_keep, 0, 1), (down_sent, 0, 1), (down_got, 0, 1), (down_more[None], 0, 1))[0]

    down_join, grad_projected, grad_branch = tie(down_join, grad_projected, grad_branch)
    grad_w_down = plan.over_z(down_join)
    high_theirs, high_send, high_keep = layer.near_grad(act_one, grad_projected, attended_turned, grad_branch, 1)

    high_theirs, grad_projected, low_sent, up_more, *everyone = tie(
        high_theirs, grad_projected, low_sent, up_more, *everyone
    )
    high_sent = across(high_theirs)
    everyone = jnp.concatenate(everyone)
    more = plan.move(everyone, plan.x_pairs)
    low_fold = sum_pieces(2, (low_send, 0, 1), (low_sent, 1, 2))

    low_fold, high_sent, more = tie(low_fold, high_sent, more)
    low_got = first(low_fold)
    everyone = jnp.concatenate([everyone, more])
    high_fold = sum_pieces(2, (high_send, 0, 1), (high_sent, 1, 2))

    high_fold, everyone, grad_projected = tie(high_fold, everyone, grad_projected)
    more = plan.move(everyone, plan.y_pairs)
    high_got = first(high_fold)
    grad_tokens, grad_gain_one, grad_shift_one = layer.token_grad(grad_projected, grad_middle, gain_one, near_pieces)

    grad_tokens, grad_gain_one, grad_shift_one = tie(grad_tokens, grad_gain_one, grad_shift_one)
    ones = jnp.stack([grad_gain_one.reshape(8, per), grad_shift_one.reshape(8, per)], axis=1)
    ones_sent = across(ones)

    ones_sent, grad_w_down, ones = tie(ones_sent, grad_w_down, ones)
    ones = ones + ones_sent
    ones_sent = plan.move(ones, plan.x_pairs)
    grad_w_down = plan.over_group(grad_w_down)
    up_join = sum_pieces(1, (up_keep, 0, 1), (up_sent, 0, 1), (up_got, 0, 1), (up_more[None], 0, 1))[0]

    ones_sent, low_got, high_got, up_join = tie(ones_sent, low_got, high_got, up_join)
    ones = ones + ones_sent
    ones_sent = plan.move(ones, plan.y_pairs)
    low_fold = sum_pieces(1, (low_keep, 1, 1), (low_sent, 2, 1), (low_got, 1, 1))[0]
    high_fold = sum_pieces(1, (high_keep, 1, 1), (high_sent, 2, 1), (high_got, 1, 1))[0]

    low_fold, high_fold, middle, more, up_join = tie(low_fold, high_fold, middle, more, up_join)
    low_more, high_more = second(low_fold), second(high_fold)
    grad_w_up = plan.over_z(up_join)
    everyone = jnp.concatenate([everyone, more])
    more = across(everyone)
    output = layer.output(hidden, middle, bias_down, down_pieces)

    output, low_more, high_more, more, ones_sent, grad_w_down = tie(
        output, low_more, high_more, more, ones_sent, grad_w_down
    )
    ones = ones + ones_sent
    ones = lax.dynamic_index_in_dim(ones.reshape(4, 2, 2, per), plan.x, 1, keepdims=False)
    ones = lax.dynamic_slice_in_dim(jnp.concatenate([ones, ones]), plan.z, 4, 0)
    ones = jnp.pad(ones, ((0, 0), (0, layer.deep - 2), (0, 0)))
    parts = plan.to_z(
        [low_keep[0], low_sent[0], low_got[0], low_more], [high_keep[0], high_sent[0], high_got[0], high_more], [ones]
    )

    grad_w_up, grad_w_down = tie(grad_w_up, grad_w_down)
    grad_w_up, grad_w_down = plan.over_group(grad_w_up), grad_w_down.astype(F32)

    grad_w_up, everyone, more, grad_w_down, *parts = tie(grad_w_up, everyone, more, grad_w_down, *parts)
    near = plan.in_group(sum_of(*parts))
    grad_w_up = grad_w_up.astype(F32)
    everyone = jnp.concatenate([everyone, more])
    rest = everyone[..., width:].astype(F32)
    picked = chosen(rest[..., 0].reshape(-1).astype(jnp.int32), own_levels)
    grad_w_time = outer(picked, everyone[..., :width].reshape(-1, width))
    rest = jnp.sum(lax.dynamic_index_in_dim(rest, plan.wide, 1, keepdims=False)[:, 128:], axis=0)
    gain_sum, shift_sum, down_sum, up_sum = jnp.split(rest, (per, 2 * per, 3 * per))

    near, grad_w_up, grad_w_time = tie(near, grad_w_up, grad_w_time)
    grad_w_qkv, grad_w_out, ones = jnp.split(near.astype(F32), (3 * width, 4 * width), axis=1)
    return (output, grad_tokens, ones[0], ones[1], grad_w_qkv, grad_w_out, gain_sum, shift_sum,
            grad_w_time, grad_w_up, up_sum, grad_w_down, down_sum)


def solution(mesh):
    fits = (mesh.shape["group"], mesh.shape["wide"]) == (4, 8)
    shards = functools.partial(plan_shards, Plan()) if fits else fallback_shards
    split, rows, line = P(BOTH, None), P("wide", None), P("wide")
    in_specs = (split, split, P(BOTH), P(), line, line, rows, rows, line, line, rows, rows, line, rows, line)
    out_specs = (split, split, line, line, rows, rows, line, line, rows, rows, line, rows, line)
    return jax.shard_map(shards, mesh=mesh, in_specs=in_specs, out_specs=out_specs, check_vma=False)
```

```python
import functools
import math

import jax
import jax.numpy as jnp
from jax import lax
from jax.experimental import pallas as pl
from jax.experimental.pallas import tpu as pltpu
from jax.sharding import PartitionSpec as P

HEAD_DIM = 64
EPSILON = 1e-05
BOTH = ("group", "wide")
F32 = jnp.float32
BF16 = jnp.bfloat16
BLOCKS = 32
VMEM_BYTES = 58 * 2**20


def sum_of(*terms):
    total = terms[0].astype(F32)
    for term in terms[1:]:
        total = total + term.astype(F32)
    return total.astype(BF16)


def tie(*values):
    return lax.optimization_barrier(values)


def dot(a, b):
    return jnp.dot(a, b, preferred_element_type=F32)


def dot_nt(a, b):
    return lax.dot_general(a, b, (((1,), (1,)), ((), ())), preferred_element_type=F32)


def dot_tn(a, b):
    return lax.dot_general(a, b, (((0,), (0,)), ((), ())), preferred_element_type=F32)


class Plan:
    def __init__(self):
        def pairs(target):
            found = []
            for index in range(32):
                group, wide = divmod(index, 8)
                y, core, z, x = target(group // 2, group % 2, wide // 2, wide % 2)
                found.append((index, (y * 2 + core) * 8 + z * 2 + x))
            return found

        self.core_pairs = pairs(lambda y, c, z, x: (y, 1 - c, z, x))
        self.y_pairs = pairs(lambda y, c, z, x: (1 - y, c, z, x))
        self.x_pairs = pairs(lambda y, c, z, x: (y, c, z, 1 - x))
        self.first_pairs = pairs(lambda y, c, z, x: (y, c, z, 1 - x) if c == 0 else (1 - y, c, z, x))
        self.second_pairs = pairs(lambda y, c, z, x: (1 - y, c, z, x) if c == 0 else (y, c, z, 1 - x))
        self.z_groups = [[(y * 2 + c) * 8 + z * 2 + x for z in range(4)] for y in (0, 1) for c in (0, 1) for x in (0, 1)]
        self.z_pairs = [pairs(lambda y, c, z, x, step=step: (y, c, (z - step) % 4, x)) for step in range(4)]

    def enter(self):
        self.group = lax.axis_index("group")
        self.wide = lax.axis_index("wide")
        y, core = self.group // 2, self.group % 2
        z, x = self.wide // 2, self.wide % 2
        self.z, self.x, self.y, self.core = z, x, y, core
        slot = jnp.arange(BLOCKS, dtype=jnp.int32)
        holder = core ^ (slot // 16)
        second, first, step = (slot // 8) % 2, (slot // 4) % 2, slot % 4
        across = jnp.where(holder == 0, first, second)
        along = jnp.where(holder == 0, second, first)
        spot = (x ^ across) * 4 + (y ^ along) * 2 + holder
        places, near_places = step * 8 + spot, ((z + step) % 4) * 8 + spot
        block_z, block_x, block_y, block_core = slot // 8, (slot // 4) % 2, (slot // 2) % 2, slot % 2
        off_x, off_y = block_x ^ x, block_y ^ y
        first = jnp.where(block_core == 0, off_x, off_y)
        second = jnp.where(block_core == 0, off_y, off_x)
        spot = (((block_core ^ core) * 2 + second) * 2 + first) * 4
        tables = places, near_places, spot + block_z, spot + (block_z - z) % 4
        return [table.astype(jnp.int32) for table in tables]

    def move(self, value, pairs):
        return lax.ppermute(value, BOTH, pairs)

    def own_block(self, shard):
        rows = shard.shape[0] // 4
        return lax.dynamic_slice_in_dim(shard, self.group * rows, rows, 0)

    def along_z(self, own):
        return lax.all_gather(own, BOTH, axis_index_groups=self.z_groups, axis=0)

    def near_z(self, own):
        return [own] + [self.move(own, self.z_pairs[step]) for step in (1, 2, 3)]

    def first(self, value):
        return self.move(value, self.first_pairs)

    def second(self, value):
        return self.move(value, self.second_pairs)

    def across(self, value):
        return self.move(value, self.core_pairs)

    def over_z(self, part):
        return lax.psum_scatter(part, BOTH, axis_index_groups=self.z_groups, scatter_dimension=0)

    def over_group(self, own):
        return lax.all_gather(own, "group", axis=0, tiled=True)

    def to_z(self, *weights):
        def part(step):
            return jnp.concatenate([sum_of(*[term[step] for term in terms]) for terms in weights], axis=1)

        return [part(0)] + [self.move(part(step), self.z_pairs[4 - step]) for step in (1, 2, 3)]

    def in_group(self, own):
        along = self.move(own, self.y_pairs)
        parts = [own, self.across(own), along, self.across(along)]
        parts = [jnp.where(self.core == 0, parts[i], parts[i ^ 1]) for i in range(4)]
        return jnp.concatenate([jnp.where(self.y == 0, parts[i], parts[i ^ 2]) for i in range(4)])

    def in_wide_order(self, near):
        near = jnp.where(self.x == 0, near, near[:, ::-1])
        near = lax.dynamic_slice_in_dim(jnp.concatenate([near, near]), (4 - self.z) % 4, 4, 0)
        return near.reshape((8,) + near.shape[2:])

    def sum_x(self, pair):
        return pair[0] + self.move(pair[1], self.x_pairs)

    def sum_z(self, near):
        total = near[0]
        for step in (1, 2, 3):
            total = total + self.move(near[step], self.z_pairs[4 - step])
        return total


def rotary_tables(length):
    half = HEAD_DIM // 2
    frequency = jnp.exp(jnp.arange(half, dtype=F32) * (-2.0 * math.log(10000.0) / HEAD_DIM))
    angles = jnp.arange(length, dtype=F32)[:, None] * frequency[None, :]
    sine = jnp.sin(angles)
    cosine = jnp.concatenate([jnp.cos(angles)] * 4, axis=1)
    return cosine, jnp.concatenate([-sine, sine, -sine, sine], axis=1)


def call(kernel, name, tables, grid, ins, outs, scratch=(), flops=0, moved=0):
    def spec(block, index, buffers=None):
        if buffers:
            return pl.BlockSpec(block, index, pipeline_mode=pl.Buffered(buffers))
        return pl.BlockSpec(block, index)

    return pl.pallas_call(
        kernel,
        out_shape=[jax.ShapeDtypeStruct(shape, dtype) for shape, dtype, *_ in outs],
        grid_spec=pltpu.PrefetchScalarGridSpec(
            num_scalar_prefetch=len(tables),
            grid=grid,
            in_specs=[spec(*rest) for _, *rest in ins],
            out_specs=[spec(*rest) for _, _, *rest in outs],
            scratch_shapes=list(scratch),
        ),
        compiler_params=pltpu.CompilerParams(vmem_limit_bytes=VMEM_BYTES),
        cost_estimate=pl.CostEstimate(flops=0, bytes_accessed=0, transcendentals=0),
        name=name,
    )(*tables, *[array for array, *_ in ins])


def whole(array, buffers=1):
    rank = array.ndim
    return (array, array.shape, lambda i, *_: (0,) * rank, buffers)


def columns_at(array, first, count):
    return (array, array.shape[:-1] + (count,), lambda i, *_: (0,) * (array.ndim - 1) + (first // count,), 1)


def rows_of(array, tile):
    return (array, (tile, array.shape[1]), lambda i, *_: (i, 0))


def out_rows(shape, dtype, tile):
    return (shape, dtype, (tile, shape[1]), lambda i, *_: (i, 0))


def out_whole(shape, dtype):
    return (shape, dtype, shape, lambda i, *_: (0,) * len(shape), 1)


def put_in_order(places, pieces, held):
    for i in range(BLOCKS):
        held[places[i]] = pieces[i // 4][i % 4]


def matrix(held):
    blocks, rows, columns = held.shape
    return held[...].reshape(blocks * rows, columns)


def normalise(values):
    average = jnp.mean(values, axis=-1, keepdims=True)
    centered = values - average
    scale = lax.rsqrt(jnp.mean(centered * centered, axis=-1, keepdims=True) + EPSILON)
    return centered * scale, scale


def norm_back(grad, hat, scale, gain):
    e = grad * gain
    inner = jnp.mean(e * hat, axis=-1, keepdims=True)
    return scale * (e - jnp.mean(e, axis=-1, keepdims=True) - hat * inner)


def turned(values):
    lane = lax.broadcasted_iota(jnp.int32, values.shape, 1)
    return jnp.where(lane % 64 < 32, pltpu.roll(values, 96, 1), pltpu.roll(values, 32, 1))


def heads(values):
    lane = lax.broadcasted_iota(jnp.int32, values.shape, 1)
    zero = jnp.zeros_like(values)
    return jnp.concatenate([jnp.where(lane < 64, values, zero), jnp.where(lane < 64, zero, values)], axis=0)


def put_turned(out, slots, values):
    rows = out.shape[1]
    flipped = values.T
    for j in range(BLOCKS):
        out[slots[j]] = flipped[j * rows : (j + 1) * rows]


def attention_kernel(length, places, slots, tokens, gain, shift, cosine, sine, *refs):
    pieces, (act_turned, qkv, attended, attended_turned), held = refs[:8], refs[8:12], refs[12]
    rows, width = tokens.shape

    @pl.when(pl.program_id(0) == 0)
    def _():
        put_in_order(places, pieces, held)

    hat, _ = normalise(tokens[...].astype(F32))
    act = (hat * gain[...] + shift[...]).astype(BF16)
    put_turned(act_turned, slots, act)
    cos, sin = cosine[...], sine[...]
    for start in range(0, 3 * width, 512):
        part = dot(act, held[:, :, start : start + 512].reshape(width, 512))
        if start < 2 * width:
            for lanes in range(0, 512, 128):
                piece = part[:, lanes : lanes + 128]
                qkv[:, start + lanes : start + lanes + 128] = (piece * cos + turned(piece) * sin).astype(BF16)
        else:
            qkv[:, start : start + 512] = part.astype(BF16)
    group = 1024
    factor = HEAD_DIM ** (-0.5)
    for top in range(0, rows, length):
        at = slice(top, top + length)
        for first in range(0, width, group):
            starts = range(first, first + group, 128)
            queries = [heads(qkv[at, lanes : lanes + 128]) for lanes in starts]
            scores = [
                dot_nt(qkv[at, width + lanes : width + lanes + 128], q) for lanes, q in zip(starts, queries, strict=True)
            ]
            probs = []
            for score in scores:
                e = jnp.exp(factor * (score - jnp.max(score, axis=0, keepdims=True)))
                probs.append((e * (1.0 / jnp.sum(e, axis=0, keepdims=True))).astype(BF16))
            probs = [jnp.concatenate([p[:, :length].T, p[:, length:].T], axis=1) for p in probs]
            for lanes, p in zip(starts, probs, strict=True):
                v = heads(qkv[at, 2 * width + lanes : 2 * width + lanes + 128])
                attended[at, lanes : lanes + 128] = dot(p, v).astype(BF16)
    put_turned(attended_turned, slots, attended[...])


def middle_kernel(length, places, near_slots, slots, tokens, attended, scales, gain, shift, *refs):
    pieces, (middle, act, act_turned), held = refs[:8], refs[8:11], refs[11]
    rows = tokens.shape[0]

    @pl.when(pl.program_id(0) == 0)
    def _():
        put_in_order(places, pieces, held)

    values = tokens[...].astype(F32) + dot(attended[...], matrix(held))
    middle[...] = values
    hat, _ = normalise(values)
    normed = hat * gain[...] + shift[...]
    first = pl.program_id(0) * (rows // length)
    for s in range(rows // length):
        act[s * length : (s + 1) * length, :] = (
            normed[s * length : (s + 1) * length, :] * scales[pl.ds(first + s, 1), :]
        ).astype(BF16)
    put_turned(act_turned, slots, act[...])


def split_out(slot, block, theirs, send, keep):
    piece, at = slot // 4, slot % 4

    @pl.when(slot >= BLOCKS // 2)
    def _():
        theirs[piece - 4, at] = block

    @pl.when((slot < BLOCKS // 2) & (piece % 2 == 1))
    def _():
        send[piece // 2, at] = block

    @pl.when((slot < BLOCKS // 2) & (piece % 2 == 0))
    def _():
        keep[piece // 2, at] = block


def up_kernel(places, slots, act, bias, cotangent, *refs):
    pieces, (hidden, slope, theirs, send, keep), held = refs[:8], refs[8:13], refs[13]
    put_in_order(places, pieces, held)
    v = dot(act[...], matrix(held)) + bias[...]
    area = 0.5 + 0.5 * lax.erf(v * math.sqrt(0.5))
    low = (v * area).astype(BF16)
    hidden[...] = low
    slope[...] = (area + v * jnp.exp(-0.5 * v * v) * (1.0 / math.sqrt(2.0 * math.pi))).astype(BF16)
    grad = dot_tn(low, cotangent[...]).astype(BF16)
    rows = theirs.shape[2]
    count = hidden.shape[1] // rows
    for k in range(count):
        split_out(slots[pl.program_id(0) * count + k], grad[k * rows : (k + 1) * rows], theirs, send, keep)


def near_grad_kernel(strips, act_one, grad_projected, attended, grad_branch, theirs, send, keep):
    blocks, rows = act_one.shape[:2]

    @pl.when(pl.program_id(0) < strips)
    def _():
        put_apart(dot(act_one[...].reshape(blocks * rows, -1), grad_projected[...]), rows, theirs, send, keep)

    @pl.when(pl.program_id(0) >= strips)
    def _():
        put_apart(dot(attended[...].reshape(blocks * rows, -1), grad_branch[...]), rows, theirs, send, keep)


def put_apart(total, rows, theirs, send, keep):
    total = total.astype(BF16).reshape(8, 4, rows, -1)
    theirs[...] = total[4:]
    for second in range(2):
        keep[second] = total[2 * second]
        send[second] = total[2 * second + 1]


def feed_back_kernel(length, places, cotangent, slope, turned_act, middle, scales, gain, shift, *refs):
    down, up = refs[:8], refs[8:16]
    theirs, send, keep, bias, grad_middle, grad_branch, grad_scale, gain_sum, shift_sum = refs[16:25]
    held_down, held_up, total = refs[25:]
    step = pl.program_id(0)

    @pl.when(step == 0)
    def _():
        put_in_order(places, down, held_down)
        total[...] = jnp.zeros_like(total)

    put_in_order(places, up, held_up)
    strip = slope.shape[1]
    count = strip // held_down.shape[1]
    rows = held_down[pl.ds(step * count, count)].reshape(strip, -1)
    grad = (dot_nt(cotangent[...], rows) * slope[...].astype(F32)).astype(BF16)
    bias[...] = jnp.sum(grad.astype(F32), axis=0, keepdims=True)
    blocks, deep = turned_act.shape[:2]
    put_apart(dot(turned_act[...].reshape(blocks * deep, -1), grad), deep, theirs, send, keep)
    total[...] += dot_nt(grad, matrix(held_up))

    @pl.when(step == pl.num_programs(0) - 1)
    def _():
        gains, shifts = jnp.zeros_like(gain_sum), jnp.zeros_like(shift_sum)
        for s in range(middle.shape[0] // length):
            at = slice(s * length, (s + 1) * length)
            own = total[at, :]
            hat, scale = normalise(middle[at, :])
            normed = hat * gain[...] + shift[...]
            grad_scale[s : s + 1, :] = jnp.sum(own * normed, axis=0, keepdims=True)
            grad = own * scales[s : s + 1, :]
            gains += jnp.sum(grad * hat, axis=0, keepdims=True)
            shifts += jnp.sum(grad, axis=0, keepdims=True)
            out = cotangent[at, :].astype(F32) + norm_back(grad, hat, scale, gain[...])
            grad_middle[at, :] = out
            grad_branch[at, :] = out.astype(BF16)
        gain_sum[...] = gains
        shift_sum[...] = shifts


def sum_kernel(*refs):
    total = refs[0][...].astype(F32)
    for ref in refs[1:-1]:
        total = total + ref[...].astype(F32)
    refs[-1][...] = total.astype(BF16)


def sum_pieces(count, *terms):
    _, _, rows, columns = terms[0][0].shape
    halves = 1 if count > 1 else 2
    block = (1, 4 // halves, rows, columns)
    ins = [
        (array, block, lambda i, first=first, stride=stride: (first + stride * (i // halves), i % halves, 0, 0))
        for array, first, stride in terms
    ]
    out = ((count, 4, rows, columns), BF16, block, lambda i: (i // halves, i % halves, 0, 0))
    size = count * 4 * rows * columns
    return call(sum_kernel, "sum_pieces", (), (halves * count,), ins, [out], flops=size, moved=2 * size * (len(terms) + 1))[0]


def output_kernel(places, hidden, middle, bias, *refs):
    pieces, output, held = refs[:8], refs[8], refs[9]

    @pl.when(pl.program_id(0) == 0)
    def _():
        put_in_order(places, pieces, held)

    output[...] = (middle[...] + dot(hidden[...], matrix(held)) + bias[...]).astype(BF16)


def attention_grad_kernel(length, places, grad_branch, qkv, cosine, sine, *refs):
    pieces, grad_projected, held, grad_attended = refs[:8], refs[8], refs[9], refs[10]
    rows, width = grad_branch.shape
    factor = HEAD_DIM ** (-0.5)

    @pl.when(pl.program_id(0) == 0)
    def _():
        put_in_order(places, pieces, held)

    grad_attended[...] = dot_nt(grad_branch[...], matrix(held)).astype(BF16)
    cos, sin = cosine[...], sine[...]
    group = 512
    for top in range(0, rows, length):
        at = slice(top, top + length)
        for first in range(0, width, group):
            starts = range(first, first + group, 128)
            q = [heads(qkv[at, lanes : lanes + 128]) for lanes in starts]
            k = [qkv[at, width + lanes : width + lanes + 128] for lanes in starts]
            g = [heads(grad_attended[at, lanes : lanes + 128]) for lanes in starts]
            scores = [dot_nt(a, b) for a, b in zip(k, q, strict=True)]
            grad_probs = [
                dot_nt(qkv[at, 2 * width + lanes : 2 * width + lanes + 128], b) for lanes, b in zip(starts, g, strict=True)
            ]
            probs = []
            for score in scores:
                e = jnp.exp(factor * (score - jnp.max(score, axis=0, keepdims=True)))
                probs.append(e * (1.0 / jnp.sum(e, axis=0, keepdims=True)))
            grad_values = [dot(p.astype(BF16), b) for p, b in zip(probs, g, strict=True)]
            grad_scores = []
            for p, gp in zip(probs, grad_probs, strict=True):
                inner = jnp.sum(gp * p, axis=0, keepdims=True)
                grad_scores.append((p * (gp - inner)).astype(BF16))
            grad_keys = [dot(gs, b) * factor for gs, b in zip(grad_scores, q, strict=True)]
            flipped = [jnp.concatenate([gs[:, :length].T, gs[:, length:].T], axis=1) for gs in grad_scores]
            grad_queries = [dot(f, heads(b)) * factor for f, b in zip(flipped, k, strict=True)]
            for n, lanes in enumerate(starts):
                for start, grad in ((lanes, grad_queries[n]), (width + lanes, grad_keys[n])):
                    grad_projected[at, start : start + 128] = (grad * cos[at] - turned(grad) * sin[at]).astype(BF16)
                grad_projected[at, 2 * width + lanes : 2 * width + lanes + 128] = grad_values[n].astype(BF16)


def token_grad_kernel(places, grad_projected, tokens, grad_middle, gain, *refs):
    pieces, (grad_tokens, gain_sum, shift_sum), held = refs[:8], refs[8:11], refs[11]

    @pl.when(pl.program_id(0) == 0)
    def _():
        put_in_order(places, pieces, held)
        gain_sum[...] = jnp.zeros_like(gain_sum)
        shift_sum[...] = jnp.zeros_like(shift_sum)

    grad = dot_nt(grad_projected[...], matrix(held))
    hat, scale = normalise(tokens[...].astype(F32))
    gain_sum[...] += jnp.sum(grad * hat, axis=0, keepdims=True)
    shift_sum[...] += jnp.sum(grad, axis=0, keepdims=True)
    grad_tokens[...] = grad_middle[...] + norm_back(grad, hat, scale, gain[...])


class Fallback:
    def vector(self, shard):
        return lax.all_gather(shard, "wide", axis=0, tiled=True).astype(F32)[None]

    def pieces(self, shard):
        full = lax.all_gather(shard, "wide", axis=0, tiled=True)
        return list(full.reshape(8, 4, full.shape[0] // BLOCKS, full.shape[1]))

    def sum(self, grad):
        grad = lax.psum_scatter(grad, "wide", scatter_dimension=0, tiled=True)
        return lax.psum(grad, "group").astype(F32)


class Layer:
    def __init__(self, tokens, cotangent, seqs, ff, places, near_places, slots, near_slots):
        self.tokens, self.cotangent = tokens, cotangent
        self.places, self.near_places, self.slots, self.near_slots = places, near_places, slots, near_slots
        self.rows, self.width = tokens.shape
        self.seqs, self.ff = seqs, ff
        self.length = self.rows // seqs
        self.tile = 2 * self.length
        self.steps = self.rows // self.tile
        self.strip = 512
        self.deep = self.width // BLOCKS
        cosine, sine = rotary_tables(self.length)
        self.tables = [jnp.tile(t, (self.tile // self.length, 1)) for t in (cosine, sine)]

    def held(self, pieces):
        return pltpu.VMEM((BLOCKS,) + pieces[0].shape[1:], BF16)

    def qkv_part(self, pieces):
        return [columns_at(p, 0, 3 * self.width) for p in pieces]

    def out_part(self, pieces):
        return [columns_at(p, 3 * self.width, self.width) for p in pieces]

    def held_part(self, columns):
        return pltpu.VMEM((BLOCKS, self.deep, columns), BF16)

    def turned_out(self):
        return ((BLOCKS, self.deep, self.rows), BF16, (BLOCKS, self.deep, self.tile), lambda i, *_: (0, 0, i))

    def by_rows(self, array):
        return rows_of(array, self.tile)

    def rows_out(self, columns, dtype):
        return out_rows((self.rows, columns), dtype, self.tile)

    def by_columns(self, array, strip):
        return (array, array.shape[:-1] + (strip,), lambda i, *_: (0,) * (array.ndim - 1) + (i,))

    def columns_out(self, shape, dtype, strip):
        return (shape, dtype, shape[:-1] + (strip,), lambda i, *_: (0,) * (len(shape) - 1) + (i,))

    def attention(self, gain, shift, pieces):
        rows, width = self.rows, self.width
        return call(
            functools.partial(attention_kernel, self.length), "attention", (self.near_places, self.near_slots), (self.steps,),
            [self.by_rows(self.tokens), whole(gain), whole(shift)] + [whole(t) for t in self.tables]
            + self.qkv_part(pieces),
            [self.turned_out(), self.rows_out(3 * width, BF16), self.rows_out(width, BF16), self.turned_out()],
            [self.held_part(3 * width)], flops=12 * rows * width * width, moved=20 * rows * width,
        )

    def middle(self, attended, scales, gain, shift, pieces):
        rows, width = self.rows, self.width
        return call(
            functools.partial(middle_kernel, self.length), "middle", (self.near_places, self.near_slots, self.slots), (self.steps,),
            [self.by_rows(self.tokens), self.by_rows(attended), whole(scales), whole(gain), whole(shift)]
            + self.out_part(pieces),
            [self.rows_out(width, F32), self.rows_out(width, BF16), self.turned_out()],
            [self.held_part(width)], flops=4 * rows * width * width, moved=14 * rows * width,
        )

    def up(self, act, bias, pieces):
        rows, width, ff = self.rows, self.width, self.ff
        fr, strip = ff // BLOCKS, 2 * self.strip
        return call(
            up_kernel, "up", (self.places, self.slots), (ff // strip,),
            [whole(act), self.by_columns(bias, strip), whole(self.cotangent)] + [self.by_columns(p, strip) for p in pieces],
            [self.columns_out((rows, ff), BF16, strip)] * 2 + [out_whole((n, 4, fr, width), BF16) for n in (4, 2, 2)],
            [pltpu.VMEM((BLOCKS, self.deep, strip), BF16)],
            flops=4 * rows * width * ff, moved=8 * rows * ff,
        )

    def near_grad(self, act_one, grad_projected, attended, grad_branch, half):
        columns, strip = 2 * self.width, 2 * self.strip
        strips = 3 * self.width // strip
        at = half * columns // strip
        ins = [
            whole(act_one),
            (grad_projected, (self.rows, strip), lambda i: (0, jnp.minimum(i + at, strips - 1))),
            whole(attended),
            (grad_branch, (self.rows, strip), lambda i: (0, jnp.maximum(i + at - strips, 0))),
        ]
        return call(
            functools.partial(near_grad_kernel, strips - at), "near_grad", (), (columns // strip,), ins,
            [self.columns_out((n, 4, self.deep, columns), BF16, strip) for n in (4, 2, 2)],
            flops=2 * self.rows * self.width * columns, moved=4 * self.rows * columns,
        )

    def feed_back(self, slope, act, middle, scales, gain, shift, down, up):
        rows, width, ff = self.rows, self.width, self.ff
        return call(
            functools.partial(feed_back_kernel, self.length), "feed_back", (self.places,), (ff // self.strip,),
            [whole(self.cotangent), self.by_columns(slope, self.strip)] + [whole(v) for v in (act, middle, scales, gain, shift)]
            + [whole(p) for p in down] + [self.by_columns(p, self.strip) for p in up],
            [self.columns_out((n, 4, self.deep, ff), BF16, self.strip) for n in (4, 2, 2)]
            + [self.columns_out((1, ff), F32, self.strip), out_whole((rows, width), F32), out_whole((rows, width), BF16)]
            + [out_whole((self.seqs, width), F32)] + [out_whole((1, width), F32)] * 2,
            [self.held(down), pltpu.VMEM((BLOCKS, self.deep, self.strip), BF16), pltpu.VMEM((rows, width), F32)],
            flops=6 * rows * width * ff, moved=10 * rows * ff,
        )

    def output(self, hidden, middle, bias, pieces):
        rows, width = self.rows, self.width
        return call(
            output_kernel, "output", (self.places,), (self.steps,),
            [self.by_rows(hidden), self.by_rows(middle), whole(bias)] + [whole(p) for p in pieces],
            [self.rows_out(width, BF16)],
            [self.held(pieces)], flops=2 * rows * width * self.ff, moved=22 * rows * width,
        )[0]

    def attention_grad(self, grad_branch, qkv, pieces):
        rows, width = self.rows, self.width
        return call(
            functools.partial(attention_grad_kernel, self.length), "attention_grad", (self.near_places,), (self.steps,),
            [self.by_rows(grad_branch), self.by_rows(qkv)] + [whole(t) for t in self.tables] + self.out_part(pieces),
            [self.rows_out(3 * width, BF16)],
            [self.held_part(width), pltpu.VMEM((self.tile, width), BF16)],
            flops=12 * rows * width * width, moved=16 * rows * width,
        )[0]

    def token_grad(self, grad_projected, grad_middle, gain, pieces):
        rows, width = self.rows, self.width
        return call(
            token_grad_kernel, "token_grad", (self.near_places,), (self.steps,),
            [self.by_rows(grad_projected), self.by_rows(self.tokens), self.by_rows(grad_middle), whole(gain)]
            + self.qkv_part(pieces),
            [self.rows_out(width, F32)] + [out_whole((1, width), F32)] * 2,
            [self.held_part(3 * width)], flops=6 * rows * width * width, moved=22 * rows * width,
        )


def chosen(index, table):
    levels = jnp.arange(table.shape[0], dtype=jnp.int32)
    return dot((index[:, None] == levels[None, :]).astype(BF16), table).astype(BF16)


def outer(a, b):
    return lax.dot_general(a, b, (((0,), (0,)), ((), ())), preferred_element_type=F32)


def fallback_shards(tokens, cotangent, noise_index, time_embed, ln1_gain, ln1_shift, w_qkv, w_out, ln2_gain, ln2_shift,
                    w_time, w_up, up_bias, w_down, down_bias):
    net = Fallback()
    order = jnp.arange(BLOCKS, dtype=jnp.int32)
    layer = Layer(tokens, cotangent, noise_index.shape[0], w_up.shape[1], order, order, order, order)
    gain_one, shift_one, gain_two, shift_two, bias_down, bias_up = [
        net.vector(v) for v in (ln1_gain, ln1_shift, ln2_gain, ln2_shift, down_bias, up_bias)
    ]
    embedded = chosen(noise_index, time_embed)
    scales = 1.0 + dot(embedded, lax.all_gather(w_time, "wide", axis=0, tiled=True))
    near_pieces, up_pieces, down_pieces = [
        net.pieces(w) for w in (jnp.concatenate([w_qkv, w_out], axis=1), w_up, w_down)
    ]
    act_one, qkv, attended, attended_turned = layer.attention(gain_one, shift_one, near_pieces)
    middle, act_two, act_two_turned = layer.middle(attended, scales, gain_two, shift_two, near_pieces)
    hidden, slope, *down_terms = layer.up(act_two, bias_up, up_pieces)
    output = layer.output(hidden, middle, bias_down, down_pieces)
    *up_terms, grad_up_bias, grad_middle, grad_branch, grad_scale, grad_gain_two, grad_shift_two = layer.feed_back(
        slope, act_two_turned, middle, scales, gain_two, shift_two, down_pieces, up_pieces
    )
    grad_projected = layer.attention_grad(grad_branch, qkv, near_pieces)
    grad_tokens, grad_gain_one, grad_shift_one = layer.token_grad(grad_projected, grad_middle, gain_one, near_pieces)

    def summed(theirs, send, keep):
        mine = jnp.stack([keep[0], send[0], keep[1], send[1]])
        return net.sum(jnp.concatenate([mine, theirs]).reshape(-1, theirs.shape[-1]))

    grads = (act_one, grad_projected, attended_turned, grad_branch)
    near = jnp.concatenate([summed(*layer.near_grad(*grads, half)) for half in range(2)], axis=1)
    width = tokens.shape[1]
    return (
        output,
        grad_tokens,
        net.sum(grad_gain_one[0]),
        net.sum(grad_shift_one[0]),
        near[:, : 3 * width],
        near[:, 3 * width :],
        net.sum(grad_gain_two[0]),
        net.sum(grad_shift_two[0]),
        net.sum(outer(embedded, grad_scale.astype(BF16))),
        summed(*up_terms),
        net.sum(grad_up_bias[0]),
        summed(*down_terms),
        net.sum(jnp.sum(cotangent.astype(F32), axis=0)),
    )


def plan_shards(plan, tokens, cotangent, noise_index, time_embed, ln1_gain, ln1_shift, w_qkv, w_out, ln2_gain,
                ln2_shift, w_time, w_up, up_bias, w_down, down_bias):
    seqs, per, width = noise_index.shape[0], ln1_gain.shape[0], tokens.shape[1]
    layer = Layer(tokens, cotangent, seqs, w_up.shape[1], *plan.enter())
    first, second, across = plan.first, plan.second, plan.across

    lines = [v.reshape(-1, per) for v in (ln1_gain, ln1_shift, ln2_gain, ln2_shift, down_bias, up_bias)]
    index_line = jnp.pad(noise_index.astype(BF16), (0, per - seqs))[None]
    lines = jnp.concatenate(lines + [index_line])
    lines = jnp.concatenate([lines, plan.move(lines, plan.x_pairs)])
    line_count = lines.shape[0]
    lines = jnp.pad(lines, ((0, w_qkv.shape[0] // 4 - line_count), (0, 0)))
    parts = plan.near_z(jnp.concatenate([plan.own_block(w_qkv), plan.own_block(w_out), lines], axis=1))
    own_up, own_down = plan.own_block(w_up), plan.own_block(w_down)

    *parts, own_up = tie(*parts, own_up)
    near_z = jnp.stack(parts)
    near_1, near_2 = first(near_z), second(near_z)
    up_z = plan.along_z(own_up)
    lines = jnp.stack([part[:line_count, -per:] for part in parts]).reshape(4, 2, -1, per)
    own_levels = lax.dynamic_slice_in_dim(time_embed, plan.wide * per, per, 1)
    index = lines[:, :, -1, :seqs].reshape(-1).astype(jnp.int32)
    partial = plan.sum_z(dot(chosen(index, own_levels), w_time).reshape(4, 2, seqs, width))
    vectors = plan.in_wide_order(lines)
    gain_one, shift_one, gain_two, shift_two, bias_down = [vectors[:, i].reshape(1, -1).astype(F32) for i in range(5)]
    bias_up = vectors[:, 5:-1].reshape(1, -1).astype(F32)

    near_1, near_2, own_down, partial, gain_one, shift_one = tie(near_1, near_2, own_down, partial, gain_one, shift_one)
    near_12, near_1c, near_2c, near_c = second(near_1), across(near_1), across(near_2), across(near_z)
    scales = 1.0 + plan.sum_x(partial)
    down_z = plan.along_z(own_down)

    near_12, near_1c, near_2c, near_c, up_z, scales = tie(near_12, near_1c, near_2c, near_c, up_z, scales)
    near_12c, up_1, up_2 = across(near_12), first(up_z), second(up_z)
    near_pieces = [near_z, near_1, near_2, near_12, near_c, near_1c, near_2c, near_12c]
    act_one, qkv, attended, attended_turned = layer.attention(gain_one, shift_one, near_pieces)

    attended, up_1, up_2 = tie(attended, up_1, up_2)
    up_12, up_c, up_1c, up_2c = second(up_1), across(up_z), across(up_1), across(up_2)
    middle, act_two, act_two_turned = layer.middle(attended, scales, gain_two, shift_two, near_pieces)

    act_two, up_12, up_2c, up_c, up_1c, down_z = tie(act_two, up_12, up_2c, up_c, up_1c, down_z)
    up_12c = across(up_12)
    down_1, down_2, down_c = first(down_z), second(down_z), across(down_z)
    up_pieces = [up_z, up_1, up_2, up_12, up_c, up_1c, up_2c, up_12c]
    hidden, slope, down_theirs, down_send, down_keep = layer.up(act_two, bias_up, up_pieces)

    hidden, slope, down_theirs, down_1, down_2, down_c = tie(hidden, slope, down_theirs, down_1, down_2, down_c)
    down_12, down_sent, down_1c, down_2c = second(down_1), across(down_theirs), across(down_1), across(down_2)

    down_sent, down_1c, down_2c = tie(down_sent, down_1c, down_2c)
    down_sum = sum_pieces(2, (down_send, 0, 1), (down_sent, 1, 2))

    down_sum, down_12, slope = tie(down_sum, down_12, slope)
    down_got, down_12c = first(down_sum), across(down_12)
    down_pieces = [down_z, down_1, down_2, down_12, down_c, down_1c, down_2c, down_12c]
    up_theirs, up_send, up_keep, grad_up_bias, grad_middle, grad_branch, grad_scale, grad_gain_two, grad_shift_two = (
        layer.feed_back(slope, act_two_turned, middle, scales, gain_two, shift_two, down_pieces, up_pieces)
    )

    up_theirs, grad_branch, down_got = tie(up_theirs, grad_branch, down_got)
    up_sent = across(up_theirs)
    down_fold = sum_pieces(1, (down_keep, 1, 1), (down_sent, 2, 1), (down_got, 1, 1))[0]

    up_sent, down_fold, grad_branch = tie(up_sent, down_fold, grad_branch)
    up_fold = sum_pieces(2, (up_send, 0, 1), (up_sent, 1, 2))

    up_fold, grad_branch = tie(up_fold, grad_branch)
    up_got = first(up_fold)
    grad_projected = layer.attention_grad(grad_branch, qkv, near_pieces)

    grad_projected, grad_scale, cotangent, down_fold = tie(grad_projected, grad_scale, cotangent, down_fold)
    down_more = second(down_fold)
    low_theirs, low_send, low_keep = layer.near_grad(act_one, grad_projected, attended_turned, grad_branch, 0)

    low_theirs, grad_projected, grad_branch, up_got, grad_scale = tie(
        low_theirs, grad_projected, grad_branch, up_got, grad_scale
    )
    low_sent = across(low_theirs)
    sums = (grad_gain_two, grad_shift_two, jnp.sum(cotangent.astype(F32), axis=0), grad_up_bias)
    rows = [grad_scale, jnp.broadcast_to(noise_index[:, None], (seqs, 128)).astype(F32)]
    everyone = jnp.concatenate(rows + [v.reshape(seqs, -1) for v in sums], axis=1).astype(BF16)[None]
    up_fold = sum_pieces(1, (up_keep, 1, 1), (up_sent, 2, 1), (up_got, 1, 1))[0]

    up_fold, everyone, grad_projected, grad_branch, down_more = tie(
        up_fold, everyone, grad_projected, grad_branch, down_more
    )
    up_more = second(up_fold)
    everyone = plan.near_z(everyone)
    down_join = sum_pieces(1, (down_keep, 0, 1), (down_sent, 0, 1), (down_got, 0, 1), (down_more[None], 0, 1))[0]

    down_join, grad_projected, grad_branch = tie(down_join, grad_projected, grad_branch)
    grad_w_down = plan.over_z(down_join)
    high_theirs, high_send, high_keep = layer.near_grad(act_one, grad_projected, attended_turned, grad_branch, 1)

    high_theirs, grad_projected, low_sent, up_more, *everyone = tie(
        high_theirs, grad_projected, low_sent, up_more, *everyone
    )
    high_sent = across(high_theirs)
    everyone = jnp.concatenate(everyone)
    more = plan.move(everyone, plan.x_pairs)
    low_fold = sum_pieces(2, (low_send, 0, 1), (low_sent, 1, 2))

    low_fold, high_sent, more = tie(low_fold, high_sent, more)
    low_got = first(low_fold)
    everyone = jnp.concatenate([everyone, more])
    high_fold = sum_pieces(2, (high_send, 0, 1), (high_sent, 1, 2))

    high_fold, everyone, grad_projected = tie(high_fold, everyone, grad_projected)
    more = plan.move(everyone, plan.y_pairs)
    high_got = first(high_fold)
    grad_tokens, grad_gain_one, grad_shift_one = layer.token_grad(grad_projected, grad_middle, gain_one, near_pieces)

    grad_tokens, grad_gain_one, grad_shift_one = tie(grad_tokens, grad_gain_one, grad_shift_one)
    ones = jnp.stack([grad_gain_one.reshape(8, per), grad_shift_one.reshape(8, per)], axis=1)
    ones_sent = across(ones)

    ones_sent, grad_w_down, ones = tie(ones_sent, grad_w_down, ones)
    ones = ones + ones_sent
    ones_sent = plan.move(ones, plan.x_pairs)
    grad_w_down = plan.over_group(grad_w_down)
    up_join = sum_pieces(1, (up_keep, 0, 1), (up_sent, 0, 1), (up_got, 0, 1), (up_more[None], 0, 1))[0]

    ones_sent, low_got, high_got, up_join = tie(ones_sent, low_got, high_got, up_join)
    ones = ones + ones_sent
    ones_sent = plan.move(ones, plan.y_pairs)
    low_fold = sum_pieces(1, (low_keep, 1, 1), (low_sent, 2, 1), (low_got, 1, 1))[0]
    high_fold = sum_pieces(1, (high_keep, 1, 1), (high_sent, 2, 1), (high_got, 1, 1))[0]

    low_fold, high_fold, middle, more, up_join = tie(low_fold, high_fold, middle, more, up_join)
    low_more, high_more = second(low_fold), second(high_fold)
    grad_w_up = plan.over_z(up_join)
    everyone = jnp.concatenate([everyone, more])
    more = across(everyone)
    output = layer.output(hidden, middle, bias_down, down_pieces)

    output, low_more, high_more, more, ones_sent, grad_w_down = tie(
        output, low_more, high_more, more, ones_sent, grad_w_down
    )
    ones = ones + ones_sent
    ones = lax.dynamic_index_in_dim(ones.reshape(4, 2, 2, per), plan.x, 1, keepdims=False)
    ones = lax.dynamic_slice_in_dim(jnp.concatenate([ones, ones]), plan.z, 4, 0)
    ones = jnp.pad(ones, ((0, 0), (0, layer.deep - 2), (0, 0)))
    parts = plan.to_z(
        [low_keep[0], low_sent[0], low_got[0], low_more], [high_keep[0], high_sent[0], high_got[0], high_more], [ones]
    )

    grad_w_up, grad_w_down = tie(grad_w_up, grad_w_down)
    grad_w_up, grad_w_down = plan.over_group(grad_w_up), grad_w_down.astype(F32)

    grad_w_up, everyone, more, grad_w_down, *parts = tie(grad_w_up, everyone, more, grad_w_down, *parts)
    near = plan.in_group(sum_of(*parts))
    grad_w_up = grad_w_up.astype(F32)
    everyone = jnp.concatenate([everyone, more])
    rest = everyone[..., width:].astype(F32)
    picked = chosen(rest[..., 0].reshape(-1).astype(jnp.int32), own_levels)
    grad_w_time = outer(picked, everyone[..., :width].reshape(-1, width))
    rest = jnp.sum(lax.dynamic_index_in_dim(rest, plan.wide, 1, keepdims=False)[:, 128:], axis=0)
    gain_sum, shift_sum, down_sum, up_sum = jnp.split(rest, (per, 2 * per, 3 * per))

    near, grad_w_up, grad_w_time = tie(near, grad_w_up, grad_w_time)
    grad_w_qkv, grad_w_out, ones = jnp.split(near.astype(F32), (3 * width, 4 * width), axis=1)
    return (output, grad_tokens, ones[0], ones[1], grad_w_qkv, grad_w_out, gain_sum, shift_sum,
            grad_w_time, grad_w_up, up_sum, grad_w_down, down_sum)


def solution(mesh):
    fits = (mesh.shape["group"], mesh.shape["wide"]) == (4, 8)
    shards = functools.partial(plan_shards, Plan()) if fits else fallback_shards
    split, rows, line = P(BOTH, None), P("wide", None), P("wide")
    in_specs = (split, split, P(BOTH), P(), line, line, rows, rows, line, line, rows, rows, line, rows, line)
    out_specs = (split, split, line, line, rows, rows, line, line, rows, rows, line, rows, line)
    return jax.shard_map(shards, mesh=mesh, in_specs=in_specs, out_specs=out_specs, check_vma=False)
```

```python
import functools
import math

import jax
import jax.numpy as jnp
from jax import lax
from jax.experimental import pallas as pl
from jax.experimental.pallas import tpu as pltpu
from jax.sharding import PartitionSpec as P

HEAD_DIM = 64
EPSILON = 1e-05
BOTH = ("group", "wide")
F32 = jnp.float32
BF16 = jnp.bfloat16
BLOCKS = 32
VMEM_BYTES = 58 * 2**20


def sum_of(*terms):
    total = terms[0].astype(F32)
    for term in terms[1:]:
        total = total + term.astype(F32)
    return total.astype(BF16)


def tie(*values):
    return lax.optimization_barrier(values)


def dot(a, b):
    return jnp.dot(a, b, preferred_element_type=F32)


def dot_nt(a, b):
    return lax.dot_general(a, b, (((1,), (1,)), ((), ())), preferred_element_type=F32)


def dot_tn(a, b):
    return lax.dot_general(a, b, (((0,), (0,)), ((), ())), preferred_element_type=F32)


class Plan:
    def __init__(self):
        def pairs(target):
            found = []
            for index in range(32):
                group, wide = divmod(index, 8)
                y, core, z, x = target(group // 2, group % 2, wide // 2, wide % 2)
                found.append((index, (y * 2 + core) * 8 + z * 2 + x))
            return found

        self.core_pairs = pairs(lambda y, c, z, x: (y, 1 - c, z, x))
        self.y_pairs = pairs(lambda y, c, z, x: (1 - y, c, z, x))
        self.x_pairs = pairs(lambda y, c, z, x: (y, c, z, 1 - x))
        self.first_pairs = pairs(lambda y, c, z, x: (y, c, z, 1 - x) if c == 0 else (1 - y, c, z, x))
        self.second_pairs = pairs(lambda y, c, z, x: (1 - y, c, z, x) if c == 0 else (y, c, z, 1 - x))
        self.z_groups = [[(y * 2 + c) * 8 + z * 2 + x for z in range(4)] for y in (0, 1) for c in (0, 1) for x in (0, 1)]
        self.z_pairs = [pairs(lambda y, c, z, x, step=step: (y, c, (z - step) % 4, x)) for step in range(4)]

    def enter(self):
        self.group = lax.axis_index("group")
        self.wide = lax.axis_index("wide")
        y, core = self.group // 2, self.group % 2
        z, x = self.wide // 2, self.wide % 2
        self.z, self.x, self.y, self.core = z, x, y, core
        slot = jnp.arange(BLOCKS, dtype=jnp.int32)
        holder = core ^ (slot // 16)
        second, first, step = (slot // 8) % 2, (slot // 4) % 2, slot % 4
        across = jnp.where(holder == 0, first, second)
        along = jnp.where(holder == 0, second, first)
        spot = (x ^ across) * 4 + (y ^ along) * 2 + holder
        places, near_places = step * 8 + spot, ((z + step) % 4) * 8 + spot
        block_z, block_x, block_y, block_core = slot // 8, (slot // 4) % 2, (slot // 2) % 2, slot % 2
        off_x, off_y = block_x ^ x, block_y ^ y
        first = jnp.where(block_core == 0, off_x, off_y)
        second = jnp.where(block_core == 0, off_y, off_x)
        spot = (((block_core ^ core) * 2 + second) * 2 + first) * 4
        tables = places, near_places, spot + block_z, spot + (block_z - z) % 4
        return [table.astype(jnp.int32) for table in tables]

    def move(self, value, pairs):
        return lax.ppermute(value, BOTH, pairs)

    def own_block(self, shard):
        rows = shard.shape[0] // 4
        return lax.dynamic_slice_in_dim(shard, self.group * rows, rows, 0)

    def along_z(self, own):
        return lax.all_gather(own, BOTH, axis_index_groups=self.z_groups, axis=0)

    def near_z(self, own):
        return [own] + [self.move(own, self.z_pairs[step]) for step in (1, 2, 3)]

    def first(self, value):
        return self.move(value, self.first_pairs)

    def second(self, value):
        return self.move(value, self.second_pairs)

    def across(self, value):
        return self.move(value, self.core_pairs)

    def over_z(self, part):
        return lax.psum_scatter(part, BOTH, axis_index_groups=self.z_groups, scatter_dimension=0)

    def over_group(self, own):
        return lax.all_gather(own, "group", axis=0, tiled=True)

    def to_z(self, *weights):
        def part(step):
            return jnp.concatenate([sum_of(*[term[step] for term in terms]) for terms in weights], axis=1)

        return [part(0)] + [self.move(part(step), self.z_pairs[4 - step]) for step in (1, 2, 3)]

    def in_group(self, own):
        along = self.move(own, self.y_pairs)
        parts = [own, self.across(own), along, self.across(along)]
        parts = [jnp.where(self.core == 0, parts[i], parts[i ^ 1]) for i in range(4)]
        return jnp.concatenate([jnp.where(self.y == 0, parts[i], parts[i ^ 2]) for i in range(4)])

    def in_wide_order(self, near):
        near = jnp.where(self.x == 0, near, near[:, ::-1])
        near = lax.dynamic_slice_in_dim(jnp.concatenate([near, near]), (4 - self.z) % 4, 4, 0)
        return near.reshape((8,) + near.shape[2:])

    def sum_x(self, pair):
        return pair[0] + self.move(pair[1], self.x_pairs)

    def sum_z(self, near):
        total = near[0]
        for step in (1, 2, 3):
            total = total + self.move(near[step], self.z_pairs[4 - step])
        return total


def rotary_tables(length):
    half = HEAD_DIM // 2
    frequency = jnp.exp(jnp.arange(half, dtype=F32) * (-2.0 * math.log(10000.0) / HEAD_DIM))
    angles = jnp.arange(length, dtype=F32)[:, None] * frequency[None, :]
    sine = jnp.sin(angles)
    cosine = jnp.concatenate([jnp.cos(angles)] * 4, axis=1)
    return cosine, jnp.concatenate([-sine, sine, -sine, sine], axis=1)


def call(kernel, name, tables, grid, ins, outs, scratch=(), flops=0, moved=0):
    def spec(block, index, buffers=None):
        if buffers:
            return pl.BlockSpec(block, index, pipeline_mode=pl.Buffered(buffers))
        return pl.BlockSpec(block, index)

    return pl.pallas_call(
        kernel,
        out_shape=[jax.ShapeDtypeStruct(shape, dtype) for shape, dtype, *_ in outs],
        grid_spec=pltpu.PrefetchScalarGridSpec(
            num_scalar_prefetch=len(tables),
            grid=grid,
            in_specs=[spec(*rest) for _, *rest in ins],
            out_specs=[spec(*rest) for _, _, *rest in outs],
            scratch_shapes=list(scratch),
        ),
        compiler_params=pltpu.CompilerParams(vmem_limit_bytes=VMEM_BYTES),
        cost_estimate=pl.CostEstimate(flops=0, bytes_accessed=0, transcendentals=0),
        name=name,
    )(*tables, *[array for array, *_ in ins])


def whole(array, buffers=1):
    rank = array.ndim
    return (array, array.shape, lambda i, *_: (0,) * rank, buffers)


def columns_at(array, first, count):
    return (array, array.shape[:-1] + (count,), lambda i, *_: (0,) * (array.ndim - 1) + (first // count,), 1)


def rows_of(array, tile):
    return (array, (tile, array.shape[1]), lambda i, *_: (i, 0))


def out_rows(shape, dtype, tile):
    return (shape, dtype, (tile, shape[1]), lambda i, *_: (i, 0))


def out_whole(shape, dtype):
    return (shape, dtype, shape, lambda i, *_: (0,) * len(shape), 1)


def put_in_order(places, pieces, held):
    for i in range(BLOCKS):
        held[places[i]] = pieces[i // 4][i % 4]


def matrix(held):
    blocks, rows, columns = held.shape
    return held[...].reshape(blocks * rows, columns)


def normalise(values):
    average = jnp.mean(values, axis=-1, keepdims=True)
    centered = values - average
    scale = lax.rsqrt(jnp.mean(centered * centered, axis=-1, keepdims=True) + EPSILON)
    return centered * scale, scale


def norm_back(grad, hat, scale, gain):
    e = grad * gain
    inner = jnp.mean(e * hat, axis=-1, keepdims=True)
    return scale * (e - jnp.mean(e, axis=-1, keepdims=True) - hat * inner)


def turned(values):
    lane = lax.broadcasted_iota(jnp.int32, values.shape, 1)
    return jnp.where(lane % 64 < 32, pltpu.roll(values, 96, 1), pltpu.roll(values, 32, 1))


def heads(values):
    lane = lax.broadcasted_iota(jnp.int32, values.shape, 1)
    zero = jnp.zeros_like(values)
    return jnp.concatenate([jnp.where(lane < 64, values, zero), jnp.where(lane < 64, zero, values)], axis=0)


def put_turned(out, slots, values):
    rows = out.shape[1]
    flipped = values.T
    for j in range(BLOCKS):
        out[slots[j]] = flipped[j * rows : (j + 1) * rows]


def attention_kernel(length, places, slots, tokens, gain, shift, cosine, sine, *refs):
    pieces, (act_turned, qkv, attended, attended_turned), held = refs[:8], refs[8:12], refs[12]
    rows, width = tokens.shape

    @pl.when(pl.program_id(0) == 0)
    def _():
        put_in_order(places, pieces, held)

    hat, _ = normalise(tokens[...].astype(F32))
    act = (hat * gain[...] + shift[...]).astype(BF16)
    put_turned(act_turned, slots, act)
    cos, sin = cosine[...], sine[...]
    for start in range(0, 3 * width, 512):
        part = dot(act, held[:, :, start : start + 512].reshape(width, 512))
        if start < 2 * width:
            for lanes in range(0, 512, 128):
                piece = part[:, lanes : lanes + 128]
                qkv[:, start + lanes : start + lanes + 128] = (piece * cos + turned(piece) * sin).astype(BF16)
        else:
            qkv[:, start : start + 512] = part.astype(BF16)
    group = 1024
    factor = HEAD_DIM ** (-0.5)
    for top in range(0, rows, length):
        at = slice(top, top + length)
        for first in range(0, width, group):
            starts = range(first, first + group, 128)
            queries = [heads(qkv[at, lanes : lanes + 128]) for lanes in starts]
            scores = [
                dot_nt(qkv[at, width + lanes : width + lanes + 128], q) for lanes, q in zip(starts, queries, strict=True)
            ]
            probs = []
            for score in scores:
                e = jnp.exp(factor * (score - jnp.max(score, axis=0, keepdims=True)))
                probs.append((e * (1.0 / jnp.sum(e, axis=0, keepdims=True))).astype(BF16))
            probs = [jnp.concatenate([p[:, :length].T, p[:, length:].T], axis=1) for p in probs]
            for lanes, p in zip(starts, probs, strict=True):
                v = heads(qkv[at, 2 * width + lanes : 2 * width + lanes + 128])
                attended[at, lanes : lanes + 128] = dot(p, v).astype(BF16)
    put_turned(attended_turned, slots, attended[...])


def middle_kernel(length, places, near_slots, slots, tokens, attended, scales, gain, shift, *refs):
    pieces, (middle, act, act_turned), held = refs[:8], refs[8:11], refs[11]
    rows = tokens.shape[0]

    @pl.when(pl.program_id(0) == 0)
    def _():
        put_in_order(places, pieces, held)

    values = tokens[...].astype(F32) + dot(attended[...], matrix(held))
    middle[...] = values
    hat, _ = normalise(values)
    normed = hat * gain[...] + shift[...]
    first = pl.program_id(0) * (rows // length)
    for s in range(rows // length):
        act[s * length : (s + 1) * length, :] = (
            normed[s * length : (s + 1) * length, :] * scales[pl.ds(first + s, 1), :]
        ).astype(BF16)
    put_turned(act_turned, slots, act[...])


def split_out(slot, block, theirs, send, keep):
    piece, at = slot // 4, slot % 4

    @pl.when(slot >= BLOCKS // 2)
    def _():
        theirs[piece - 4, at] = block

    @pl.when((slot < BLOCKS // 2) & (piece % 2 == 1))
    def _():
        send[piece // 2, at] = block

    @pl.when((slot < BLOCKS // 2) & (piece % 2 == 0))
    def _():
        keep[piece // 2, at] = block


def up_kernel(places, slots, act, bias, cotangent, *refs):
    pieces, (hidden, slope, theirs, send, keep), held = refs[:8], refs[8:13], refs[13]
    put_in_order(places, pieces, held)
    v = dot(act[...], matrix(held)) + bias[...]
    area = 0.5 + 0.5 * lax.erf(v * math.sqrt(0.5))
    low = (v * area).astype(BF16)
    hidden[...] = low
    slope[...] = (area + v * jnp.exp(-0.5 * v * v) * (1.0 / math.sqrt(2.0 * math.pi))).astype(BF16)
    grad = dot_tn(low, cotangent[...]).astype(BF16)
    rows = theirs.shape[2]
    count = hidden.shape[1] // rows
    for k in range(count):
        split_out(slots[pl.program_id(0) * count + k], grad[k * rows : (k + 1) * rows], theirs, send, keep)


def near_grad_kernel(strips, act_one, grad_projected, attended, grad_branch, theirs, send, keep):
    blocks, rows = act_one.shape[:2]

    @pl.when(pl.program_id(0) < strips)
    def _():
        put_apart(dot(act_one[...].reshape(blocks * rows, -1), grad_projected[...]), rows, theirs, send, keep)

    @pl.when(pl.program_id(0) >= strips)
    def _():
        put_apart(dot(attended[...].reshape(blocks * rows, -1), grad_branch[...]), rows, theirs, send, keep)


def put_apart(total, rows, theirs, send, keep):
    total = total.astype(BF16).reshape(8, 4, rows, -1)
    theirs[...] = total[4:]
    for second in range(2):
        keep[second] = total[2 * second]
        send[second] = total[2 * second + 1]


def feed_back_kernel(length, places, cotangent, slope, turned_act, middle, scales, gain, shift, *refs):
    down, up = refs[:8], refs[8:16]
    theirs, send, keep, bias, grad_middle, grad_branch, grad_scale, gain_sum, shift_sum = refs[16:25]
    held_down, held_up, total = refs[25:]
    step = pl.program_id(0)

    @pl.when(step == 0)
    def _():
        put_in_order(places, down, held_down)
        total[...] = jnp.zeros_like(total)

    put_in_order(places, up, held_up)
    strip = slope.shape[1]
    count = strip // held_down.shape[1]
    rows = held_down[pl.ds(step * count, count)].reshape(strip, -1)
    grad = (dot_nt(cotangent[...], rows) * slope[...].astype(F32)).astype(BF16)
    bias[...] = jnp.sum(grad.astype(F32), axis=0, keepdims=True)
    blocks, deep = turned_act.shape[:2]
    put_apart(dot(turned_act[...].reshape(blocks * deep, -1), grad), deep, theirs, send, keep)
    total[...] += dot_nt(grad, matrix(held_up))

    @pl.when(step == pl.num_programs(0) - 1)
    def _():
        gains, shifts = jnp.zeros_like(gain_sum), jnp.zeros_like(shift_sum)
        for s in range(middle.shape[0] // length):
            at = slice(s * length, (s + 1) * length)
            own = total[at, :]
            hat, scale = normalise(middle[at, :])
            normed = hat * gain[...] + shift[...]
            grad_scale[s : s + 1, :] = jnp.sum(own * normed, axis=0, keepdims=True)
            grad = own * scales[s : s + 1, :]
            gains += jnp.sum(grad * hat, axis=0, keepdims=True)
            shifts += jnp.sum(grad, axis=0, keepdims=True)
            out = cotangent[at, :].astype(F32) + norm_back(grad, hat, scale, gain[...])
            grad_middle[at, :] = out
            grad_branch[at, :] = out.astype(BF16)
        gain_sum[...] = gains
        shift_sum[...] = shifts


def sum_kernel(*refs):
    total = refs[0][...].astype(F32)
    for ref in refs[1:-1]:
        total = total + ref[...].astype(F32)
    refs[-1][...] = total.astype(BF16)


def sum_pieces(count, *terms):
    _, _, rows, columns = terms[0][0].shape
    halves = 1 if count > 1 else 2
    block = (1, 4 // halves, rows, columns)
    ins = [
        (array, block, lambda i, first=first, stride=stride: (first + stride * (i // halves), i % halves, 0, 0))
        for array, first, stride in terms
    ]
    out = ((count, 4, rows, columns), BF16, block, lambda i: (i // halves, i % halves, 0, 0))
    size = count * 4 * rows * columns
    return call(sum_kernel, "sum_pieces", (), (halves * count,), ins, [out], flops=size, moved=2 * size * (len(terms) + 1))[0]


def output_kernel(places, hidden, middle, bias, *refs):
    pieces, output, held = refs[:8], refs[8], refs[9]

    @pl.when(pl.program_id(0) == 0)
    def _():
        put_in_order(places, pieces, held)

    output[...] = (middle[...] + dot(hidden[...], matrix(held)) + bias[...]).astype(BF16)


def attention_grad_kernel(length, places, grad_branch, qkv, cosine, sine, *refs):
    pieces, grad_projected, held, grad_attended = refs[:8], refs[8], refs[9], refs[10]
    rows, width = grad_branch.shape
    factor = HEAD_DIM ** (-0.5)

    @pl.when(pl.program_id(0) == 0)
    def _():
        put_in_order(places, pieces, held)

    grad_attended[...] = dot_nt(grad_branch[...], matrix(held)).astype(BF16)
    cos, sin = cosine[...], sine[...]
    group = 512
    for top in range(0, rows, length):
        at = slice(top, top + length)
        for first in range(0, width, group):
            starts = range(first, first + group, 128)
            q = [heads(qkv[at, lanes : lanes + 128]) for lanes in starts]
            k = [qkv[at, width + lanes : width + lanes + 128] for lanes in starts]
            g = [heads(grad_attended[at, lanes : lanes + 128]) for lanes in starts]
            scores = [dot_nt(a, b) for a, b in zip(k, q, strict=True)]
            grad_probs = [
                dot_nt(qkv[at, 2 * width + lanes : 2 * width + lanes + 128], b) for lanes, b in zip(starts, g, strict=True)
            ]
            probs = []
            for score in scores:
                e = jnp.exp(factor * (score - jnp.max(score, axis=0, keepdims=True)))
                probs.append(e * (1.0 / jnp.sum(e, axis=0, keepdims=True)))
            grad_values = [dot(p.astype(BF16), b) for p, b in zip(probs, g, strict=True)]
            grad_scores = []
            for p, gp in zip(probs, grad_probs, strict=True):
                inner = jnp.sum(gp * p, axis=0, keepdims=True)
                grad_scores.append((p * (gp - inner)).astype(BF16))
            grad_keys = [dot(gs, b) * factor for gs, b in zip(grad_scores, q, strict=True)]
            flipped = [jnp.concatenate([gs[:, :length].T, gs[:, length:].T], axis=1) for gs in grad_scores]
            grad_queries = [dot(f, heads(b)) * factor for f, b in zip(flipped, k, strict=True)]
            for n, lanes in enumerate(starts):
                for start, grad in ((lanes, grad_queries[n]), (width + lanes, grad_keys[n])):
                    grad_projected[at, start : start + 128] = (grad * cos[at] - turned(grad) * sin[at]).astype(BF16)
                grad_projected[at, 2 * width + lanes : 2 * width + lanes + 128] = grad_values[n].astype(BF16)


def token_grad_kernel(places, grad_projected, tokens, grad_middle, gain, *refs):
    pieces, (grad_tokens, gain_sum, shift_sum), held = refs[:8], refs[8:11], refs[11]

    @pl.when(pl.program_id(0) == 0)
    def _():
        put_in_order(places, pieces, held)
        gain_sum[...] = jnp.zeros_like(gain_sum)
        shift_sum[...] = jnp.zeros_like(shift_sum)

    grad = dot_nt(grad_projected[...], matrix(held))
    hat, scale = normalise(tokens[...].astype(F32))
    gain_sum[...] += jnp.sum(grad * hat, axis=0, keepdims=True)
    shift_sum[...] += jnp.sum(grad, axis=0, keepdims=True)
    grad_tokens[...] = grad_middle[...] + norm_back(grad, hat, scale, gain[...])


class Fallback:
    def vector(self, shard):
        return lax.all_gather(shard, "wide", axis=0, tiled=True).astype(F32)[None]

    def pieces(self, shard):
        full = lax.all_gather(shard, "wide", axis=0, tiled=True)
        return list(full.reshape(8, 4, full.shape[0] // BLOCKS, full.shape[1]))

    def sum(self, grad):
        grad = lax.psum_scatter(grad, "wide", scatter_dimension=0, tiled=True)
        return lax.psum(grad, "group").astype(F32)


class Layer:
    def __init__(self, tokens, cotangent, seqs, ff, places, near_places, slots, near_slots):
        self.tokens, self.cotangent = tokens, cotangent
        self.places, self.near_places, self.slots, self.near_slots = places, near_places, slots, near_slots
        self.rows, self.width = tokens.shape
        self.seqs, self.ff = seqs, ff
        self.length = self.rows // seqs
        self.tile = 2 * self.length
        self.steps = self.rows // self.tile
        self.strip = 512
        self.deep = self.width // BLOCKS
        cosine, sine = rotary_tables(self.length)
        self.tables = [jnp.tile(t, (self.tile // self.length, 1)) for t in (cosine, sine)]

    def held(self, pieces):
        return pltpu.VMEM((BLOCKS,) + pieces[0].shape[1:], BF16)

    def qkv_part(self, pieces):
        return [columns_at(p, 0, 3 * self.width) for p in pieces]

    def out_part(self, pieces):
        return [columns_at(p, 3 * self.width, self.width) for p in pieces]

    def held_part(self, columns):
        return pltpu.VMEM((BLOCKS, self.deep, columns), BF16)

    def turned_out(self):
        return ((BLOCKS, self.deep, self.rows), BF16, (BLOCKS, self.deep, self.tile), lambda i, *_: (0, 0, i))

    def by_rows(self, array):
        return rows_of(array, self.tile)

    def rows_out(self, columns, dtype):
        return out_rows((self.rows, columns), dtype, self.tile)

    def by_columns(self, array, strip):
        return (array, array.shape[:-1] + (strip,), lambda i, *_: (0,) * (array.ndim - 1) + (i,))

    def columns_out(self, shape, dtype, strip):
        return (shape, dtype, shape[:-1] + (strip,), lambda i, *_: (0,) * (len(shape) - 1) + (i,))

    def attention(self, gain, shift, pieces):
        rows, width = self.rows, self.width
        return call(
            functools.partial(attention_kernel, self.length), "attention", (self.near_places, self.near_slots), (self.steps,),
            [self.by_rows(self.tokens), whole(gain), whole(shift)] + [whole(t) for t in self.tables]
            + self.qkv_part(pieces),
            [self.turned_out(), self.rows_out(3 * width, BF16), self.rows_out(width, BF16), self.turned_out()],
            [self.held_part(3 * width)], flops=12 * rows * width * width, moved=20 * rows * width,
        )

    def middle(self, attended, scales, gain, shift, pieces):
        rows, width = self.rows, self.width
        return call(
            functools.partial(middle_kernel, self.length), "middle", (self.near_places, self.near_slots, self.slots), (self.steps,),
            [self.by_rows(self.tokens), self.by_rows(attended), whole(scales), whole(gain), whole(shift)]
            + self.out_part(pieces),
            [self.rows_out(width, F32), self.rows_out(width, BF16), self.turned_out()],
            [self.held_part(width)], flops=4 * rows * width * width, moved=14 * rows * width,
        )

    def up(self, act, bias, pieces):
        rows, width, ff = self.rows, self.width, self.ff
        fr, strip = ff // BLOCKS, 2 * self.strip
        return call(
            up_kernel, "up", (self.places, self.slots), (ff // strip,),
            [whole(act), self.by_columns(bias, strip), whole(self.cotangent)] + [self.by_columns(p, strip) for p in pieces],
            [self.columns_out((rows, ff), BF16, strip)] * 2 + [out_whole((n, 4, fr, width), BF16) for n in (4, 2, 2)],
            [pltpu.VMEM((BLOCKS, self.deep, strip), BF16)],
            flops=4 * rows * width * ff, moved=8 * rows * ff,
        )

    def near_grad(self, act_one, grad_projected, attended, grad_branch, half):
        columns, strip = 2 * self.width, 2 * self.strip
        strips = 3 * self.width // strip
        at = half * columns // strip
        ins = [
            whole(act_one),
            (grad_projected, (self.rows, strip), lambda i: (0, jnp.minimum(i + at, strips - 1))),
            whole(attended),
            (grad_branch, (self.rows, strip), lambda i: (0, jnp.maximum(i + at - strips, 0))),
        ]
        return call(
            functools.partial(near_grad_kernel, strips - at), "near_grad", (), (columns // strip,), ins,
            [self.columns_out((n, 4, self.deep, columns), BF16, strip) for n in (4, 2, 2)],
            flops=2 * self.rows * self.width * columns, moved=4 * self.rows * columns,
        )

    def feed_back(self, slope, act, middle, scales, gain, shift, down, up):
        rows, width, ff = self.rows, self.width, self.ff
        return call(
            functools.partial(feed_back_kernel, self.length), "feed_back", (self.places,), (ff // self.strip,),
            [whole(self.cotangent), self.by_columns(slope, self.strip)] + [whole(v) for v in (act, middle, scales, gain, shift)]
            + [whole(p) for p in down] + [self.by_columns(p, self.strip) for p in up],
            [self.columns_out((n, 4, self.deep, ff), BF16, self.strip) for n in (4, 2, 2)]
            + [self.columns_out((1, ff), F32, self.strip), out_whole((rows, width), F32), out_whole((rows, width), BF16)]
            + [out_whole((self.seqs, width), F32)] + [out_whole((1, width), F32)] * 2,
            [self.held(down), pltpu.VMEM((BLOCKS, self.deep, self.strip), BF16), pltpu.VMEM((rows, width), F32)],
            flops=6 * rows * width * ff, moved=10 * rows * ff,
        )

    def output(self, hidden, middle, bias, pieces):
        rows, width = self.rows, self.width
        return call(
            output_kernel, "output", (self.places,), (self.steps,),
            [self.by_rows(hidden), self.by_rows(middle), whole(bias)] + [whole(p) for p in pieces],
            [self.rows_out(width, BF16)],
            [self.held(pieces)], flops=2 * rows * width * self.ff, moved=22 * rows * width,
        )[0]

    def attention_grad(self, grad_branch, qkv, pieces):
        rows, width = self.rows, self.width
        return call(
            functools.partial(attention_grad_kernel, self.length), "attention_grad", (self.near_places,), (self.steps,),
            [self.by_rows(grad_branch), self.by_rows(qkv)] + [whole(t) for t in self.tables] + self.out_part(pieces),
            [self.rows_out(3 * width, BF16)],
            [self.held_part(width), pltpu.VMEM((self.tile, width), BF16)],
            flops=12 * rows * width * width, moved=16 * rows * width,
        )[0]

    def token_grad(self, grad_projected, grad_middle, gain, pieces):
        rows, width = self.rows, self.width
        return call(
            token_grad_kernel, "token_grad", (self.near_places,), (self.steps,),
            [self.by_rows(grad_projected), self.by_rows(self.tokens), self.by_rows(grad_middle), whole(gain)]
            + self.qkv_part(pieces),
            [self.rows_out(width, F32)] + [out_whole((1, width), F32)] * 2,
            [self.held_part(3 * width)], flops=6 * rows * width * width, moved=22 * rows * width,
        )


def chosen(index, table):
    levels = jnp.arange(table.shape[0], dtype=jnp.int32)
    return dot((index[:, None] == levels[None, :]).astype(BF16), table).astype(BF16)


def outer(a, b):
    return lax.dot_general(a, b, (((0,), (0,)), ((), ())), preferred_element_type=F32)


def fallback_shards(tokens, cotangent, noise_index, time_embed, ln1_gain, ln1_shift, w_qkv, w_out, ln2_gain, ln2_shift,
                    w_time, w_up, up_bias, w_down, down_bias):
    net = Fallback()
    order = jnp.arange(BLOCKS, dtype=jnp.int32)
    layer = Layer(tokens, cotangent, noise_index.shape[0], w_up.shape[1], order, order, order, order)
    gain_one, shift_one, gain_two, shift_two, bias_down, bias_up = [
        net.vector(v) for v in (ln1_gain, ln1_shift, ln2_gain, ln2_shift, down_bias, up_bias)
    ]
    embedded = chosen(noise_index, time_embed)
    scales = 1.0 + dot(embedded, lax.all_gather(w_time, "wide", axis=0, tiled=True))
    near_pieces, up_pieces, down_pieces = [
        net.pieces(w) for w in (jnp.concatenate([w_qkv, w_out], axis=1), w_up, w_down)
    ]
    act_one, qkv, attended, attended_turned = layer.attention(gain_one, shift_one, near_pieces)
    middle, act_two, act_two_turned = layer.middle(attended, scales, gain_two, shift_two, near_pieces)
    hidden, slope, *down_terms = layer.up(act_two, bias_up, up_pieces)
    output = layer.output(hidden, middle, bias_down, down_pieces)
    *up_terms, grad_up_bias, grad_middle, grad_branch, grad_scale, grad_gain_two, grad_shift_two = layer.feed_back(
        slope, act_two_turned, middle, scales, gain_two, shift_two, down_pieces, up_pieces
    )
    grad_projected = layer.attention_grad(grad_branch, qkv, near_pieces)
    grad_tokens, grad_gain_one, grad_shift_one = layer.token_grad(grad_projected, grad_middle, gain_one, near_pieces)

    def summed(theirs, send, keep):
        mine = jnp.stack([keep[0], send[0], keep[1], send[1]])
        return net.sum(jnp.concatenate([mine, theirs]).reshape(-1, theirs.shape[-1]))

    grads = (act_one, grad_projected, attended_turned, grad_branch)
    near = jnp.concatenate([summed(*layer.near_grad(*grads, half)) for half in range(2)], axis=1)
    width = tokens.shape[1]
    return (
        output,
        grad_tokens,
        net.sum(grad_gain_one[0]),
        net.sum(grad_shift_one[0]),
        near[:, : 3 * width],
        near[:, 3 * width :],
        net.sum(grad_gain_two[0]),
        net.sum(grad_shift_two[0]),
        net.sum(outer(embedded, grad_scale.astype(BF16))),
        summed(*up_terms),
        net.sum(grad_up_bias[0]),
        summed(*down_terms),
        net.sum(jnp.sum(cotangent.astype(F32), axis=0)),
    )


def plan_shards(plan, tokens, cotangent, noise_index, time_embed, ln1_gain, ln1_shift, w_qkv, w_out, ln2_gain,
                ln2_shift, w_time, w_up, up_bias, w_down, down_bias):
    seqs, per, width = noise_index.shape[0], ln1_gain.shape[0], tokens.shape[1]
    layer = Layer(tokens, cotangent, seqs, w_up.shape[1], *plan.enter())
    first, second, across = plan.first, plan.second, plan.across

    lines = [v.reshape(-1, per) for v in (ln1_gain, ln1_shift, ln2_gain, ln2_shift, down_bias, up_bias)]
    index_line = jnp.pad(noise_index.astype(BF16), (0, per - seqs))[None]
    lines = jnp.concatenate(lines + [index_line])
    lines = jnp.concatenate([lines, plan.move(lines, plan.x_pairs)])
    line_count = lines.shape[0]
    lines = jnp.pad(lines, ((0, w_qkv.shape[0] // 4 - line_count), (0, 0)))
    parts = plan.near_z(jnp.concatenate([plan.own_block(w_qkv), plan.own_block(w_out), lines], axis=1))
    own_up, own_down = plan.own_block(w_up), plan.own_block(w_down)

    *parts, own_up = tie(*parts, own_up)
    near_z = jnp.stack(parts)
    near_1, near_2 = first(near_z), second(near_z)
    up_z = plan.along_z(own_up)
    lines = jnp.stack([part[:line_count, -per:] for part in parts]).reshape(4, 2, -1, per)
    own_levels = lax.dynamic_slice_in_dim(time_embed, plan.wide * per, per, 1)
    index = lines[:, :, -1, :seqs].reshape(-1).astype(jnp.int32)
    partial = plan.sum_z(dot(chosen(index, own_levels), w_time).reshape(4, 2, seqs, width))
    vectors = plan.in_wide_order(lines)
    gain_one, shift_one, gain_two, shift_two, bias_down = [vectors[:, i].reshape(1, -1).astype(F32) for i in range(5)]
    bias_up = vectors[:, 5:-1].reshape(1, -1).astype(F32)

    down_total = jnp.sum(cotangent.astype(F32), axis=0)

    near_1, near_2, own_down, partial, gain_one, shift_one, down_total = tie(
        near_1, near_2, own_down, partial, gain_one, shift_one, down_total
    )
    near_12, near_1c, near_2c, near_c = second(near_1), across(near_1), across(near_2), across(near_z)
    scales = 1.0 + plan.sum_x(partial)
    down_z = plan.along_z(own_down)

    near_12, near_1c, near_2c, near_c, up_z, scales = tie(near_12, near_1c, near_2c, near_c, up_z, scales)
    near_12c, up_1, up_2 = across(near_12), first(up_z), second(up_z)
    near_pieces = [near_z, near_1, near_2, near_12, near_c, near_1c, near_2c, near_12c]
    act_one, qkv, attended, attended_turned = layer.attention(gain_one, shift_one, near_pieces)

    attended, up_1, up_2 = tie(attended, up_1, up_2)
    up_12, up_c, up_1c, up_2c = second(up_1), across(up_z), across(up_1), across(up_2)
    middle, act_two, act_two_turned = layer.middle(attended, scales, gain_two, shift_two, near_pieces)

    act_two, up_12, up_2c, up_c, up_1c, down_z = tie(act_two, up_12, up_2c, up_c, up_1c, down_z)
    up_12c = across(up_12)
    down_1, down_2, down_c = first(down_z), second(down_z), across(down_z)
    up_pieces = [up_z, up_1, up_2, up_12, up_c, up_1c, up_2c, up_12c]
    hidden, slope, down_theirs, down_send, down_keep = layer.up(act_two, bias_up, up_pieces)

    hidden, slope, down_theirs, down_1, down_2, down_c = tie(hidden, slope, down_theirs, down_1, down_2, down_c)
    down_12, down_sent, down_1c, down_2c = second(down_1), across(down_theirs), across(down_1), across(down_2)

    down_sent, down_1c, down_2c = tie(down_sent, down_1c, down_2c)
    down_sum = sum_pieces(2, (down_send, 0, 1), (down_sent, 1, 2))

    down_sum, down_12, slope = tie(down_sum, down_12, slope)
    down_got, down_12c = first(down_sum), across(down_12)
    down_pieces = [down_z, down_1, down_2, down_12, down_c, down_1c, down_2c, down_12c]
    up_theirs, up_send, up_keep, grad_up_bias, grad_middle, grad_branch, grad_scale, grad_gain_two, grad_shift_two = (
        layer.feed_back(slope, act_two_turned, middle, scales, gain_two, shift_two, down_pieces, up_pieces)
    )

    up_theirs, grad_branch, down_got = tie(up_theirs, grad_branch, down_got)
    up_sent = across(up_theirs)
    down_fold = sum_pieces(1, (down_keep, 1, 1), (down_sent, 2, 1), (down_got, 1, 1))[0]

    up_sent, down_fold, grad_branch = tie(up_sent, down_fold, grad_branch)
    up_fold = sum_pieces(2, (up_send, 0, 1), (up_sent, 1, 2))

    up_fold, grad_branch = tie(up_fold, grad_branch)
    up_got = first(up_fold)
    grad_projected = layer.attention_grad(grad_branch, qkv, near_pieces)

    grad_projected, grad_scale, cotangent, down_fold = tie(grad_projected, grad_scale, cotangent, down_fold)
    down_more = second(down_fold)
    low_theirs, low_send, low_keep = layer.near_grad(act_one, grad_projected, attended_turned, grad_branch, 0)

    low_theirs, grad_projected, grad_branch, up_got, grad_scale = tie(
        low_theirs, grad_projected, grad_branch, up_got, grad_scale
    )
    low_sent = across(low_theirs)
    sums = (grad_gain_two, grad_shift_two, down_total, grad_up_bias)
    rows = [grad_scale, jnp.broadcast_to(noise_index[:, None], (seqs, 128)).astype(F32)]
    everyone = jnp.concatenate(rows + [v.reshape(seqs, -1) for v in sums], axis=1).astype(BF16)[None]
    up_fold = sum_pieces(1, (up_keep, 1, 1), (up_sent, 2, 1), (up_got, 1, 1))[0]

    up_fold, everyone, grad_projected, grad_branch, down_more = tie(
        up_fold, everyone, grad_projected, grad_branch, down_more
    )
    up_more = second(up_fold)
    everyone = plan.near_z(everyone)
    down_join = sum_pieces(1, (down_keep, 0, 1), (down_sent, 0, 1), (down_got, 0, 1), (down_more[None], 0, 1))[0]

    down_join, grad_projected, grad_branch = tie(down_join, grad_projected, grad_branch)
    grad_w_down = plan.over_z(down_join)
    high_theirs, high_send, high_keep = layer.near_grad(act_one, grad_projected, attended_turned, grad_branch, 1)

    high_theirs, grad_projected, low_sent, up_more, *everyone = tie(
        high_theirs, grad_projected, low_sent, up_more, *everyone
    )
    high_sent = across(high_theirs)
    everyone = jnp.concatenate(everyone)
    more = plan.move(everyone, plan.x_pairs)
    low_fold = sum_pieces(2, (low_send, 0, 1), (low_sent, 1, 2))

    low_fold, high_sent, more = tie(low_fold, high_sent, more)
    low_got = first(low_fold)
    everyone = jnp.concatenate([everyone, more])
    high_fold = sum_pieces(2, (high_send, 0, 1), (high_sent, 1, 2))

    high_fold, everyone, grad_projected = tie(high_fold, everyone, grad_projected)
    more = plan.move(everyone, plan.y_pairs)
    high_got = first(high_fold)
    grad_tokens, grad_gain_one, grad_shift_one = layer.token_grad(grad_projected, grad_middle, gain_one, near_pieces)

    grad_tokens, grad_gain_one, grad_shift_one = tie(grad_tokens, grad_gain_one, grad_shift_one)
    ones = jnp.stack([grad_gain_one.reshape(8, per), grad_shift_one.reshape(8, per)], axis=1)
    ones_sent = across(ones)

    ones_sent, grad_w_down, ones = tie(ones_sent, grad_w_down, ones)
    ones = ones + ones_sent
    ones_sent = plan.move(ones, plan.x_pairs)
    grad_w_down = plan.over_group(grad_w_down)
    up_join = sum_pieces(1, (up_keep, 0, 1), (up_sent, 0, 1), (up_got, 0, 1), (up_more[None], 0, 1))[0]

    ones_sent, low_got, high_got, up_join = tie(ones_sent, low_got, high_got, up_join)
    ones = ones + ones_sent
    ones_sent = plan.move(ones, plan.y_pairs)
    low_fold = sum_pieces(1, (low_keep, 1, 1), (low_sent, 2, 1), (low_got, 1, 1))[0]
    high_fold = sum_pieces(1, (high_keep, 1, 1), (high_sent, 2, 1), (high_got, 1, 1))[0]

    low_fold, high_fold, middle, more, up_join = tie(low_fold, high_fold, middle, more, up_join)
    low_more, high_more = second(low_fold), second(high_fold)
    grad_w_up = plan.over_z(up_join)
    everyone = jnp.concatenate([everyone, more])
    more = across(everyone)
    output = layer.output(hidden, middle, bias_down, down_pieces)

    output, low_more, high_more, more, ones_sent, grad_w_down = tie(
        output, low_more, high_more, more, ones_sent, grad_w_down
    )
    ones = ones + ones_sent
    ones = lax.dynamic_index_in_dim(ones.reshape(4, 2, 2, per), plan.x, 1, keepdims=False)
    ones = lax.dynamic_slice_in_dim(jnp.concatenate([ones, ones]), plan.z, 4, 0)
    ones = jnp.pad(ones, ((0, 0), (0, layer.deep - 2), (0, 0)))
    parts = plan.to_z(
        [low_keep[0], low_sent[0], low_got[0], low_more], [high_keep[0], high_sent[0], high_got[0], high_more], [ones]
    )

    grad_w_up, grad_w_down = tie(grad_w_up, grad_w_down)
    grad_w_up, grad_w_down = plan.over_group(grad_w_up), grad_w_down.astype(F32)

    grad_w_up, everyone, more, grad_w_down, *parts = tie(grad_w_up, everyone, more, grad_w_down, *parts)
    near = plan.in_group(sum_of(*parts))
    grad_w_up = grad_w_up.astype(F32)
    everyone = jnp.concatenate([everyone, more])
    rest = everyone[..., width:].astype(F32)
    picked = chosen(rest[..., 0].reshape(-1).astype(jnp.int32), own_levels)
    grad_w_time = outer(picked, everyone[..., :width].reshape(-1, width))
    rest = jnp.sum(lax.dynamic_index_in_dim(rest, plan.wide, 1, keepdims=False)[:, 128:], axis=0)
    gain_sum, shift_sum, down_sum, up_sum = jnp.split(rest, (per, 2 * per, 3 * per))

    near, grad_w_up, grad_w_time = tie(near, grad_w_up, grad_w_time)
    grad_w_qkv, grad_w_out, ones = jnp.split(near.astype(F32), (3 * width, 4 * width), axis=1)
    return (output, grad_tokens, ones[0], ones[1], grad_w_qkv, grad_w_out, gain_sum, shift_sum,
            grad_w_time, grad_w_up, up_sum, grad_w_down, down_sum)


def solution(mesh):
    fits = (mesh.shape["group"], mesh.shape["wide"]) == (4, 8)
    shards = functools.partial(plan_shards, Plan()) if fits else fallback_shards
    split, rows, line = P(BOTH, None), P("wide", None), P("wide")
    in_specs = (split, split, P(BOTH), P(), line, line, rows, rows, line, line, rows, rows, line, rows, line)
    out_specs = (split, split, line, line, rows, rows, line, line, rows, rows, line, rows, line)
    return jax.shard_map(shards, mesh=mesh, in_specs=in_specs, out_specs=out_specs, check_vma=False)
```
